32 devices in a mesh: dp: 8 (over y, x, core), sp: 4 (over z).
Axes of the slice: x: 2, y: 2, z: 4, core: 2. Of those that a mesh axis runs over, the one named last changes fastest.
Arguments:
- inputs: bfloat16 [8, 2048, 512], P('dp', 'sp'), may hold values from -6 to 6
- encoder: bfloat16 [8, 2048, 512], P('dp', 'sp'), may hold values from -6 to 6
- cotangent: bfloat16 [8, 2048, 512], P('dp', 'sp'), may hold values from -6 to 6
- w_self: bfloat16 [512, 1536], P('dp'), may hold values from -0.375 to 0.375
- w_self_out: bfloat16 [512, 512], P('dp'), may hold values from -0.75 to 0.75
- w_cross_q: bfloat16 [512, 512], P('dp'), may hold values from -0.375 to 0.375
- w_cross_kv: bfloat16 [512, 1024], P('dp'), may hold values from -0.375 to 0.375
- w_cross_out: bfloat16 [512, 512], P('dp'), may hold values from -0.75 to 0.75
- w_up: bfloat16 [512, 2048], P('dp'), may hold values from -0.25 to 0.25
- w_down: bfloat16 [2048, 512], P('dp'), may hold values from -0.1875 to 0.1875
- biases: bfloat16 [10, 512], P(None, 'dp'), may hold values from -1.5 to 1.5
- norm_gains: bfloat16 [3, 512], P(None, 'dp'), may hold values from 0.25 to 1.75
- up_bias: bfloat16 [2048], P('dp'), may hold values from -1.5 to 1.5
- source_lengths: int32 [8], P('dp'), may hold values from 512 to 2048, as said below
Outputs:
- output: bfloat16 [8, 2048, 512], P('dp', 'sp')
- grad_inputs: float32 [8, 2048, 512], P('dp', 'sp')
- grad_encoder: float32 [8, 2048, 512], P('dp', 'sp')
- grad_w_self: float32 [512, 1536], P('dp', 'sp')
- grad_w_self_out: float32 [512, 512], P('dp', 'sp')
- grad_w_cross_q: float32 [512, 512], P('dp', 'sp')
- grad_w_cross_kv: float32 [512, 1024], P('dp', 'sp')
- grad_w_cross_out: float32 [512, 512], P('dp', 'sp')
- grad_w_up: float32 [512, 2048], P('dp', 'sp')
- grad_w_down: float32 [2048, 512], P('dp', 'sp')
- grad_biases: float32 [10, 512], P(None, ('dp', 'sp'))
- grad_gains: float32 [3, 512], P(None, ('dp', 'sp'))
- grad_up_bias: float32 [2048], P(('dp', 'sp'))
The draws below stay inside these ranges and needn't reach their ends.
Inputs may be any that keep to these rules, and one draw needn't show every extreme that they name: Sequence s attends to encoder states 0 to source_lengths[s] - 1; in every draw some sequence has all 2048.
All inputs are finite; a program needn't handle non-finite values.
Results may differ from the reference program's by a relative error of at most 0.025.
The reference program's roundings to bfloat16 on the way count: a program that leaves them out, or rounds other values in their place, can miss the bound.
Values may be sent and summed in bfloat16 or wider, within the bound.
No kernel may reach another device: no remote copies, remote signals or barrier semaphores. Data moves between devices by JAX's collectives and lax.ppermute only.
A program may use at most 128 MiB of HBM per device.

```python
import jax
import jax.numpy as jnp
from jax import lax

D = 512
H = 8
FF = 2048
DH = 64
LEN = 2048
SRC = 2048
SEQS = 8


def draw_source_lengths(key, part):
    first_key = jax.random.fold_in(key, 11)
    second_key = jax.random.fold_in(key, 12)
    drawn = jax.random.randint(first_key, (SEQS,), SRC // 4, SRC + 1)
    chosen = jax.random.randint(second_key, (), 0, SEQS)
    return jnp.where(jnp.arange(SEQS) == chosen, SRC, drawn).astype(jnp.int32)


def raised(values, stream_key, source, target, parts, factor):
    def block_of(dim):
        return (jnp.arange(values.shape[dim]) // (values.shape[dim] // parts)).reshape((-1,) + (1,) * (values.ndim - 1 - dim))

    near = jax.random.permutation(stream_key, parts)[block_of(target)]
    far = (block_of(target) + parts // 2) % parts
    return jnp.where((block_of(source) == near) | (block_of(source) == far), factor * values, values)


def level_of(rng, shape, shards, smallest, top_value):
    level = 1.0
    for position, shards_of in shards:
        draws = jax.random.uniform(jax.random.fold_in(jax.random.fold_in(rng, 6), position), (shards_of,), jnp.float32, smallest / len(shards), top_value / len(shards))
        level = level * jnp.repeat(jnp.exp(draws), shape[position] // shards_of).reshape((-1,) + (1,) * (len(shape) - 1 - position))
    return level


def gaussian(stream_key, shape, deviation, limit, split=(), held_as=jnp.bfloat16):
    level = level_of(stream_key, shape, split, -0.22, 0.18) if split else 1.0
    values = jax.random.normal(stream_key, shape, jnp.float32) * deviation * level
    return jnp.minimum(jnp.maximum(values, -limit), limit).astype(held_as)


def gaussian_with(stream_key, extent, scale, reach, cuts, heavy, kind=jnp.bfloat16):
    values = scale * jax.random.normal(stream_key, extent, jnp.float32)
    if cuts:
        values = values * level_of(stream_key, extent, cuts, -0.22, 0.18)
    return jnp.clip(raised(values, jax.random.fold_in(stream_key, 3), *heavy), -reach, reach).astype(kind)


def setup_inputs(seed: int = 0) -> dict:
    streams_of = jax.random.split(jax.random.key(seed), 15)
    inputs = gaussian_with(streams_of[0], (SEQS, LEN, D), 1.0, 6.0, ((0, 8), (1, 4)), (0, 2, 8, 2.0))
    encoder = gaussian(streams_of[1], (SEQS, SRC, D), 1.0, 6.0, ((0, 8), (1, 4)))
    cotangent = gaussian_with(streams_of[2], (SEQS, LEN, D), 1.0, 6.0, ((0, 8), (1, 4)), (0, 2, 8, 2.0))
    w_self = gaussian(streams_of[3], (D, 3 * D), (D // 2) ** -0.5, 0.375, ((0, 8),))
    w_self_out = gaussian(streams_of[4], (D, D), (D // 8) ** -0.5, 0.75, ((0, 8),))
    w_cross_q = gaussian(streams_of[5], (D, D), (D // 2) ** -0.5, 0.375, ((0, 8),))
    w_cross_kv = gaussian(streams_of[6], (D, 2 * D), (D // 2) ** -0.5, 0.375, ((0, 8),))
    w_cross_out = gaussian(streams_of[7], (D, D), (D // 8) ** -0.5, 0.75, ((0, 8),))
    w_up = gaussian(streams_of[8], (D, FF), D ** -0.5, 0.25, ((0, 8),))
    w_down = gaussian(streams_of[9], (FF, D), (FF // 2) ** -0.5, 0.1875, ((0, 8),))
    biases = gaussian(streams_of[10], (10, D), 0.3, 1.5, ((1, 8),))
    norm_gains = jnp.clip(1.0 + 0.15 * jax.random.normal(streams_of[11], (3, D), jnp.float32), 0.25, 1.75).astype(jnp.bfloat16)
    up_bias = gaussian(streams_of[12], (FF,), 0.3, 1.5, ((0, 8),))
    source_lengths = draw_source_lengths(jax.random.fold_in(streams_of[14], 71), 0)
    return dict(inputs=inputs, encoder=encoder, cotangent=cotangent, w_self=w_self, w_self_out=w_self_out, w_cross_q=w_cross_q, w_cross_kv=w_cross_kv, w_cross_out=w_cross_out, w_up=w_up, w_down=w_down, biases=biases, norm_gains=norm_gains, up_bias=up_bias, source_lengths=source_lengths)


@jax.custom_vjp
def low(v):
    return lax.optimization_barrier(v.astype(jnp.bfloat16)).astype(jnp.float32)

@jax.custom_vjp
def low_back(v):
    return v

def low_keep(v):
    return (low(v), None)

def low_pass(kept, grad):
    return (grad,)

def back_keep(v):
    return (v, None)

def back_low(kept, grad):
    return (low(grad),)
low.defvjp(low_keep, low_pass)
low_back.defvjp(back_keep, back_low)
eps_norm = 1e-05
masked_out = -1e+30

def rounded_both(value):
    return low(low_back(value))

def product(left, right):
    return jnp.dot(left, right, precision=lax.Precision.HIGHEST)

def layer_norm(resid, gain, shift):
    centred = resid - lax.optimization_barrier(jnp.mean(resid, axis=-1, keepdims=True))
    variance = lax.optimization_barrier(jnp.mean(centred * centred, axis=-1, keepdims=True))
    return centred * lax.rsqrt(variance + eps_norm) * gain + shift

def attend(queries, key_rows, value_rows, allowed):
    length = queries.shape[0]
    step_rows = min(512, length)

    def one_block(first_row):
        query_block = lax.dynamic_slice_in_dim(queries, first_row, step_rows, 0)
        scores = low_back(jnp.einsum('qhe,khe->hqk', query_block, key_rows, precision=lax.Precision.HIGHEST))
        scores = jnp.where(allowed(first_row, step_rows)[None], scores, masked_out)
        probs = low(jax.nn.softmax(scores, axis=-1))
        return jnp.einsum('hqk,khe->qhe', probs, value_rows, precision=lax.Precision.HIGHEST)
    starts = jnp.arange(length // step_rows, dtype=jnp.int32) * step_rows
    results = lax.map(jax.checkpoint(one_block), starts)
    return results.reshape(queries.shape)

def layer(param_set, tokens_in, enc_in, source_limit):
    w_self, w_self_out, w_cross_q, w_cross_kv, w_cross_out, w_up, w_down, biases, norm_gains, up_bias = param_set
    length = tokens_in.shape[0]
    sources = enc_in.shape[0]
    model_width = tokens_in.shape[1]
    query_scale = DH ** (-0.5)
    zero_row = jnp.zeros((model_width,), tokens_in.dtype)
    self_proj = product(tokens_in, w_self).reshape(length, 3, model_width) + jnp.stack([biases[0], zero_row, biases[1]])
    self_proj = self_proj * jnp.array([query_scale, 1.0, 1.0], tokens_in.dtype)[:, None]
    self_proj = rounded_both(self_proj).reshape(length, 3, H, DH)

    def causal(first_row, count):
        query_pos = first_row + jnp.arange(count, dtype=jnp.int32)[:, None]
        return jnp.arange(length, dtype=jnp.int32)[None, :] <= query_pos
    self_att = attend(self_proj[:, 0], self_proj[:, 1], self_proj[:, 2], causal)
    self_tokens = rounded_both(self_att.reshape(length, model_width))
    resid_one = tokens_in + low_back(product(self_tokens, w_self_out)) + biases[2]
    hidden_one = layer_norm(resid_one, norm_gains[0], biases[7])
    cross_query = rounded_both((product(low(hidden_one), w_cross_q) + biases[3]) * query_scale).reshape(length, H, DH)
    encoder_proj = product(enc_in, w_cross_kv).reshape(sources, 2, model_width) + jnp.stack([zero_row, biases[4]])
    encoder_proj = rounded_both(encoder_proj).reshape(sources, 2, H, DH)

    def visible(first_row, count):
        return jnp.broadcast_to(jnp.arange(sources, dtype=jnp.int32)[None, :] < source_limit, (count, sources))
    cross_att = attend(cross_query, encoder_proj[:, 0], encoder_proj[:, 1], visible)
    cross_tokens = rounded_both(cross_att.reshape(length, model_width))
    resid_two = hidden_one + low_back(product(cross_tokens, w_cross_out)) + biases[5]
    hidden_two = layer_norm(resid_two, norm_gains[1], biases[8])
    up_value = low_back(product(low(hidden_two), w_up) + up_bias)
    activation = low(jax.nn.silu(up_value))
    resid_three = hidden_two + low_back(product(activation, w_down)) + biases[6]
    return layer_norm(resid_three, norm_gains[2], biases[9])

def reference(inputs, encoder, cotangent, w_self, w_self_out, w_cross_q, w_cross_kv, w_cross_out, w_up, w_down, biases, norm_gains, up_bias, source_lengths):
    param_set = tuple((member.astype(jnp.float32) for member in (w_self, w_self_out, w_cross_q, w_cross_kv, w_cross_out, w_up, w_down, biases, norm_gains, up_bias)))

    def one_sequence(totals, sequence):
        tokens_in, enc_in, upstream, source_limit = sequence

        def forward(params_now, tokens_now, enc_now):
            return layer(params_now, tokens_now, enc_now, source_limit)
        result, pullback = jax.vjp(forward, param_set, tokens_in, enc_in)
        grad_params, grad_tokens, grad_enc = pullback(upstream)
        totals = jax.tree.map(jnp.add, totals, grad_params)
        return (totals, (result.astype(jnp.bfloat16), grad_tokens, grad_enc))
    zero_grads = jax.tree.map(jnp.zeros_like, param_set)
    totals, outputs = lax.scan(one_sequence, zero_grads, (inputs.astype(jnp.float32), encoder.astype(jnp.float32), cotangent.astype(jnp.float32), source_lengths))
    output, grad_inputs, grad_encoder = outputs
    return (output, grad_inputs, grad_encoder, totals[0], totals[1], totals[2], totals[3], totals[4], totals[5], totals[6], totals[7], totals[8], totals[9])
```

```python
import functools

import jax
import jax.numpy as jnp
from jax import lax
from jax.experimental import pallas as pl
from jax.experimental.pallas import tpu as pltpu
from jax.sharding import PartitionSpec as P

H = 8
DH = 64
PAIR = 128

eps_norm = 1e-05
masked_out = -1e30
bf16 = jnp.bfloat16
f32 = jnp.float32
SCALE = DH ** (-0.5)

VMEM_LIMIT = 60 * 2**20


def nn(left, right):
    return lax.dot_general(left, right, (((1,), (0,)), ((), ())), preferred_element_type=f32)


def nt(left, right):
    return lax.dot_general(left, right, (((1,), (1,)), ((), ())), preferred_element_type=f32)


def tn(left, right):
    return lax.dot_general(left, right, (((0,), (0,)), ((), ())), preferred_element_type=f32)


def norm_stats(resid):
    centred = resid - jnp.mean(resid, axis=-1, keepdims=True)
    inv_std = lax.rsqrt(jnp.mean(centred * centred, axis=-1, keepdims=True) + eps_norm)
    return centred * inv_std, inv_std


def norm_backward(upstream, normed, inv_std, gain):
    scaled = upstream * gain
    centre_term = jnp.mean(scaled, axis=-1, keepdims=True)
    slope_term = jnp.mean(scaled * normed, axis=-1, keepdims=True)
    return inv_std * (scaled - centre_term - normed * slope_term)


def col_sum(value):
    return jnp.sum(value, axis=0, keepdims=True)


def chunk_of(d, block, n):
    even = d if d % 2 == 0 else 2 * n - 1 - d
    return even if block == 0 else 2 * n - 1 - even


def lane_head(rows, cols=PAIR):
    return lax.broadcasted_iota(jnp.int32, (rows, cols), 1) // DH


def one_head(pair_value, head):
    return jnp.where(lane_head(*pair_value.shape) == head, pair_value, jnp.zeros_like(pair_value))


def pair_slice(pair):
    return pl.ds(pl.multiple_of(pair * PAIR, PAIR), PAIR)


def write_blocks(out_ref, value, col0, n_dp, n_sp):
    rows = value.shape[0] // n_dp
    cols = value.shape[1] // n_sp
    low = value.astype(bf16)
    for i in range(n_dp):
        for j in range(n_sp):
            out_ref[i, j, :, col0 : col0 + cols] = low[
                i * rows : (i + 1) * rows, j * cols : (j + 1) * cols
            ]


def attend_rows(q_ref, k_ref, v_ref, att_ref, lse_ref, row0, rows, parts, pair):
    cols = pair_slice(pair)
    q2 = q_ref[row0 : row0 + rows, cols]
    both = []
    lse_now = lse_ref[row0 : row0 + rows, :]
    lane = lax.broadcasted_iota(jnp.int32, (rows, PAIR), 1)
    for h in range(2):
        qm = one_head(q2, h)
        scores = []
        for start, size, mask in parts:
            s = nt(qm, k_ref[start : start + size, cols])
            if mask is not None:
                s = jnp.where(mask(rows, size), s, masked_out)
            scores.append(s)
        top = functools.reduce(
            jnp.maximum, [jnp.max(s, axis=-1, keepdims=True) for s in scores]
        )
        total = 0.0
        result = 0.0
        for s, (start, size, _) in zip(scores, parts):
            e = jnp.exp(s - top)
            total = total + jnp.sum(e, axis=-1, keepdims=True)
            result = result + nn(e.astype(bf16), v_ref[start : start + size, cols])
        both.append(result / total)
        lse_now = jnp.where(lane == pair * 2 + h, top + jnp.log(total), lse_now)
    lse_ref[row0 : row0 + rows, :] = lse_now
    att_ref[row0 : row0 + rows, cols] = jnp.where(
        lane_head(rows) == 0, both[0], both[1]
    ).astype(bf16)


def attend_rows_back(
    q_ref, k_ref, v_ref, att_ref, g_ref, lse_ref, qt_ref, gt_ref,
    dq_ref, dkt_ref, dvt_ref, row0, rows, parts, pair,
):
    cols = pair_slice(pair)
    q2 = q_ref[row0 : row0 + rows, cols]
    g2 = g_ref[row0 : row0 + rows, cols]
    prod = g2.astype(f32) * att_ref[row0 : row0 + rows, cols].astype(f32)
    lse_all = lse_ref[row0 : row0 + rows, :]
    lane = lax.broadcasted_iota(jnp.int32, (rows, PAIR), 1)
    both = []
    for h in range(2):
        head = pair * 2 + h
        hrows = pl.ds(pl.multiple_of(head * DH, DH), DH)
        qm = one_head(q2, h)
        gm = one_head(g2, h)
        qt = qt_ref[hrows, row0 : row0 + rows]
        gt = gt_ref[hrows, row0 : row0 + rows]
        lse = jnp.sum(jnp.where(lane == head, lse_all, 0.0), axis=-1, keepdims=True)
        delta = jnp.sum(jnp.where(lane // DH == h, prod, 0.0), axis=-1, keepdims=True)
        dq = 0.0
        for start, size, mask, adds in parts:
            k2 = k_ref[start : start + size, cols]
            v2 = v_ref[start : start + size, cols]
            p = jnp.exp(nt(qm, k2) - lse)
            if mask is not None:
                p = jnp.where(mask(rows, size), p, 0.0)
            ds = (p * (nt(gm, v2) - delta)).astype(bf16)
            dq = dq + nn(ds, k2)
            dk = nn(qt, ds)
            dv = nn(gt, p.astype(bf16))
            if adds:
                dk = dk + dkt_ref[hrows, start : start + size]
                dv = dv + dvt_ref[hrows, start : start + size]
            dkt_ref[hrows, start : start + size] = dk
            dvt_ref[hrows, start : start + size] = dv
        both.append(dq)
    dq_ref[row0 : row0 + rows, cols] = (
        jnp.where(lane_head(rows) == 0, both[0], both[1]).astype(bf16)
    )


def diagonal(rows, size):
    row = lax.broadcasted_iota(jnp.int32, (rows, size), 0)
    col = lax.broadcasted_iota(jnp.int32, (rows, size), 1)
    return col <= row


def causal_parts(chunk, size):
    parts = []
    if chunk:
        parts.append((0, chunk * size, None))
    parts.append((chunk * size, size, diagonal))
    return parts


def self_forward_kernel(n, d_ref, x_ref, w_ref, vec_ref, q_ref, k_ref, v_ref, att_ref, lse_ref):
    length, width = x_ref.shape
    rows = q_ref.shape[0]
    size = rows // 2
    d = d_ref[0]
    step = min(512, length)

    def project(i, carry):
        here = pl.ds(pl.multiple_of(i * step, step), step)
        kv = nn(x_ref[here, :], w_ref[:, width : 3 * width])
        k_ref[here, :] = kv[:, :width].astype(bf16)
        v_ref[here, :] = (kv[:, width:] + vec_ref[1:2, :]).astype(bf16)
        return carry

    lax.fori_loop(0, length // step, project, 0)
    even = jnp.where(d % 2 == 0, d, 2 * n - 1 - d)
    for block in range(2):
        chunk = even if block == 0 else 2 * n - 1 - even
        xb = x_ref[pl.ds(pl.multiple_of(chunk * size, size), size), :]
        q_ref[block * size : (block + 1) * size, :] = (
            (nn(xb, w_ref[:, :width]) + vec_ref[0:1, :]) * SCALE
        ).astype(bf16)
    lse_ref[...] = jnp.zeros_like(lse_ref)

    for which in range(n):

        @pl.when(d == which)
        def _(which=which):
            def pairs(pair, carry):
                for block in range(2):
                    chunk = chunk_of(which, block, n)
                    attend_rows(
                        q_ref, k_ref, v_ref, att_ref, lse_ref, block * size, size,
                        causal_parts(chunk, size), pair,
                    )
                return carry

            lax.fori_loop(0, H // 2, pairs, 0)


def cross_forward_kernel(
    n, d_ref, lim_ref, att_ref, x_ref, enc_ref, wso_ref, wcq_ref, wckv_ref, vec_ref,
    res_ref, cq_ref, ek_ref, ev_ref, catt_ref, clse_ref,
):
    length, width = enc_ref.shape
    rows = att_ref.shape[0]
    size = rows // 2
    d = d_ref[0]
    limit = lim_ref[0]
    even = jnp.where(d % 2 == 0, d, 2 * n - 1 - d)
    for block in range(2):
        chunk = even if block == 0 else 2 * n - 1 - even
        here = slice(block * size, (block + 1) * size)
        xb = x_ref[pl.ds(pl.multiple_of(chunk * size, size), size), :].astype(f32)
        res_ref[here, :] = xb + nn(att_ref[here, :], wso_ref[...]) + vec_ref[2:3, :]
    normed, _ = norm_stats(res_ref[...])
    hidden = (normed * vec_ref[10:11, :] + vec_ref[7:8, :]).astype(bf16)
    cq_ref[...] = ((nn(hidden, wcq_ref[...]) + vec_ref[3:4, :]) * SCALE).astype(bf16)
    step = min(512, length)

    def project(i, carry):
        here = pl.ds(pl.multiple_of(i * step, step), step)
        kv = nn(enc_ref[here, :], wckv_ref[...])
        ek_ref[here, :] = kv[:, :width].astype(bf16)
        ev_ref[here, :] = (kv[:, width:] + vec_ref[4:5, :]).astype(bf16)
        return carry

    lax.fori_loop(0, length // step, project, 0)
    clse_ref[...] = jnp.zeros_like(clse_ref)

    def visible(count, keys):
        return lax.broadcasted_iota(jnp.int32, (count, keys), 1) < limit

    def pairs(pair, carry):
        for block in range(2):
            attend_rows(
                cq_ref, ek_ref, ev_ref, catt_ref, clse_ref, block * size, size,
                [(0, length, visible)], pair,
            )
        return carry

    lax.fori_loop(0, H // 2, pairs, 0)


def feed_forward_kernel(
    n_dp, n_sp, res1_ref, catt_ref, wco_ref, wup_ref, wdn_ref, vec_ref, upb_ref, cot0_ref, cot1_ref,
    out0_ref, out1_ref, gtwo_ref, cgrad_ref, gw_ref, upsum_ref, small_ref,
    up_scr, act_scr, upl_scr,
):
    rows, width = res1_ref.shape
    size = rows // 2
    hidden_units = wup_ref.shape[1]
    step = min(512, hidden_units)
    blocks = hidden_units // step
    normed, _ = norm_stats(res1_ref[...])
    hidden_one = normed * vec_ref[10:11, :] + vec_ref[7:8, :]
    res2 = hidden_one + nn(catt_ref[...], wco_ref[...]) + vec_ref[5:6, :]
    normed2, inv2 = norm_stats(res2)
    hidden_two = normed2 * vec_ref[11:12, :] + vec_ref[8:9, :]
    h2_low = hidden_two.astype(bf16)
    down = jnp.zeros((rows, width), f32)
    for b in range(blocks):
        cols = slice(b * step, (b + 1) * step)
        up = nn(h2_low, wup_ref[:, cols]) + upb_ref[0:1, cols]
        up_scr[:, cols] = up
        act = (up * jax.nn.sigmoid(up)).astype(bf16)
        act_scr[:, cols] = act
        down = down + nn(act, wdn_ref[cols, :])
    res3 = hidden_two + down + vec_ref[6:7, :]
    normed3, inv3 = norm_stats(res3)
    result = (normed3 * vec_ref[12:13, :] + vec_ref[9:10, :]).astype(bf16)
    out0_ref[...] = result[:size]
    out1_ref[...] = result[size:]
    upstream = jnp.concatenate([cot0_ref[...], cot1_ref[...]], axis=0).astype(f32)
    small_ref[...] = jnp.zeros_like(small_ref)
    small_ref[12:13, :] = col_sum(upstream * normed3)
    small_ref[9:10, :] = col_sum(upstream)
    grad_three = norm_backward(upstream, normed3, inv3, vec_ref[12:13, :])
    small_ref[6:7, :] = col_sum(grad_three)
    down_low = grad_three.astype(bf16)
    h2_t = h2_low.T
    grad_h2 = grad_three
    part_rows = hidden_units // n_dp
    own_rows = width // n_dp
    groups = part_rows // own_rows
    piece = width // n_sp
    up_piece = hidden_units // n_sp
    for b in range(blocks):
        cols = slice(b * step, (b + 1) * step)
        gdown = tn(act_scr[:, cols], down_low).astype(bf16)
        for r in range(step // own_rows):
            at = b * step + r * own_rows
            i, g = at // part_rows, (at % part_rows) // own_rows
            for j in range(n_sp):
                base = piece + up_piece + g * piece
                gw_ref[i, j, :, base : base + piece] = gdown[
                    r * own_rows : (r + 1) * own_rows, j * piece : (j + 1) * piece
                ]
        up = up_scr[:, cols]
        sig = jax.nn.sigmoid(up)
        up_low = (
            nt(down_low, wdn_ref[cols, :]) * sig * (1.0 + up * (1.0 - sig))
        ).astype(bf16)
        upl_scr[:, cols] = up_low
        upsum_ref[0:1, cols] = col_sum(up_low.astype(f32))
        grad_h2 = grad_h2 + nt(up_low, wup_ref[:, cols])
    for j in range(n_sp):
        cols = slice(j * up_piece, (j + 1) * up_piece)
        gup = nn(h2_t, upl_scr[:, cols]).astype(bf16)
        for i in range(n_dp):
            gw_ref[i, j, :, piece : piece + up_piece] = gup[i * own_rows : (i + 1) * own_rows, :]
    small_ref[11:12, :] = col_sum(grad_h2 * normed2)
    small_ref[8:9, :] = col_sum(grad_h2)
    grad_two = norm_backward(grad_h2, normed2, inv2, vec_ref[11:12, :])
    small_ref[5:6, :] = col_sum(grad_two)
    gtwo_ref[...] = grad_two
    two_low = grad_two.astype(bf16)
    write_blocks(gw_ref, tn(catt_ref[...], two_low), 0, n_dp, n_sp)
    cgrad_ref[...] = nt(two_low, wco_ref[...]).astype(bf16)


def ones_sum(t_ref):
    return nt(jnp.ones((8, t_ref.shape[1]), bf16), t_ref[...])[0:1, :]


def cross_backward_kernel(
    n_dp, n_sp, lim_ref, cq_ref, ek_ref, ev_ref, catt_ref, cgrad_ref, clse_ref, enc_ref, wcq_ref, wckv_ref,
    wso_ref, vec_ref, res1_ref, att_ref, gtwo_ref, small_in_ref,
    genc_ref, gone_ref, sgrad_ref, gw_ref, small_ref,
    qt_scr, gt_scr, dq_scr, dkt_scr, dvt_scr, low_scr,
):
    length, width = enc_ref.shape
    rows = cq_ref.shape[0]
    size = rows // 2
    limit = lim_ref[0]
    qt_scr[...] = cq_ref[...].T
    gt_scr[...] = cgrad_ref[...].T
    half = length // 2

    def pairs(pair, carry):
        for block in range(2):
            parts = []
            for part in range(2):
                start = part * half

                def visible(count, keys, start=start):
                    return lax.broadcasted_iota(jnp.int32, (count, keys), 1) + start < limit

                parts.append((start, half, visible, block == 1))
            attend_rows_back(
                cq_ref, ek_ref, ev_ref, catt_ref, cgrad_ref, clse_ref, qt_scr, gt_scr,
                dq_scr, dkt_scr, dvt_scr, block * size, size, parts, pair,
            )
        return carry

    lax.fori_loop(0, H // 2, pairs, 0)
    low_scr[:width, :] = dkt_scr[...].astype(bf16)
    low_scr[width:, :] = dvt_scr[...].astype(bf16)
    query_grad = (dq_scr[...].astype(f32) * SCALE).astype(bf16)
    small_ref[...] = small_in_ref[...]
    small_ref[3:4, :] = col_sum(query_grad.astype(f32))
    small_ref[4:5, :] = ones_sum(low_scr.at[width:, :])
    normed, inv = norm_stats(res1_ref[...])
    hidden = (normed * vec_ref[10:11, :] + vec_ref[7:8, :]).astype(bf16)
    piece = width // n_sp
    write_blocks(gw_ref, tn(hidden, query_grad), 0, n_dp, n_sp)
    grad_h1 = gtwo_ref[...] + nt(query_grad, wcq_ref[...])
    small_ref[10:11, :] = col_sum(grad_h1 * normed)
    small_ref[7:8, :] = col_sum(grad_h1)
    grad_one = norm_backward(grad_h1, normed, inv, vec_ref[10:11, :])
    small_ref[2:3, :] = col_sum(grad_one)
    gone_ref[...] = grad_one
    one_low = grad_one.astype(bf16)
    write_blocks(gw_ref, tn(att_ref[...], one_low), 3 * piece, n_dp, n_sp)
    sgrad_ref[...] = nt(one_low, wso_ref[...]).astype(bf16)
    write_blocks(gw_ref, nn(low_scr[...], enc_ref[...]).T, piece, n_dp, n_sp)
    step = min(512, length)

    def back(i, carry):
        here = pl.ds(pl.multiple_of(i * step, step), step)
        genc_ref[here, :] = nn(wckv_ref[...], low_scr[:, here]).T.astype(bf16)
        return carry

    lax.fori_loop(0, length // step, back, 0)


def self_backward_kernel(
    n, n_dp, n_sp, d_ref, q_ref, k_ref, v_ref, att_ref, sgrad_ref, lse_ref, x_ref, w_ref, gone_ref, small_in_ref,
    gin_ref, gw_ref, small_ref,
    qt_scr, gt_scr, dq_scr, dkt_scr, dvt_scr, low_scr,
):
    length, width = x_ref.shape
    rows = q_ref.shape[0]
    size = rows // 2
    d = d_ref[0]
    qt_scr[...] = q_ref[...].T
    gt_scr[...] = sgrad_ref[...].T
    for which in range(n):

        @pl.when(d == which)
        def _(which=which):
            order = sorted(range(2), key=lambda block: -chunk_of(which, block, n))
            top = chunk_of(which, order[0], n)
            if top + 1 < 2 * n:
                rest = (2 * n - 1 - top) * size
                dkt_scr[:, (top + 1) * size :] = jnp.zeros((width, rest), f32)
                dvt_scr[:, (top + 1) * size :] = jnp.zeros((width, rest), f32)

            def pairs(pair, carry):
                for place, block in enumerate(order):
                    chunk = chunk_of(which, block, n)
                    parts = []
                    for start, count, mask in causal_parts(chunk, size):
                        while count > 4 * size:
                            parts.append((start, 4 * size, mask, place == 1))
                            start, count = start + 4 * size, count - 4 * size
                        parts.append((start, count, mask, place == 1))
                    attend_rows_back(
                        q_ref, k_ref, v_ref, att_ref, sgrad_ref, lse_ref, qt_scr, gt_scr,
                        dq_scr, dkt_scr, dvt_scr, block * size, size, parts, pair,
                    )
                return carry

            lax.fori_loop(0, H // 2, pairs, 0)

    low_scr[:width, :] = dkt_scr[...].astype(bf16)
    low_scr[width:, :] = dvt_scr[...].astype(bf16)
    q_grad = (dq_scr[...].astype(f32) * SCALE).astype(bf16)
    small_ref[...] = small_in_ref[...]
    small_ref[0:1, :] = col_sum(q_grad.astype(f32))
    small_ref[1:2, :] = ones_sum(low_scr.at[width:, :])
    kv_grad = nn(low_scr[...], x_ref[...]).T
    even = jnp.where(d % 2 == 0, d, 2 * n - 1 - d)
    step = min(512, length)

    def back(i, carry):
        here = pl.ds(pl.multiple_of(i * step, step), step)
        gin_ref[here, :] = nn(w_ref[:, width:], low_scr[:, here]).T.astype(bf16)
        return carry

    lax.fori_loop(0, length // step, back, 0)
    wq_grad = jnp.zeros((width, width), f32)
    for block in range(2):
        chunk = even if block == 0 else 2 * n - 1 - even
        here = pl.ds(pl.multiple_of(chunk * size, size), size)
        own = slice(block * size, (block + 1) * size)
        wq_grad = wq_grad + tn(x_ref[here, :], q_grad[own])
        gin_ref[here, :] = (
            gin_ref[here, :].astype(f32)
            + gone_ref[own, :]
            + nt(q_grad[own], w_ref[:, :width])
        ).astype(bf16)
    grads = jnp.concatenate([wq_grad, kv_grad], axis=1)
    write_blocks(gw_ref, grads, 0, n_dp, n_sp)


def run_kernel(kernel, outs, args, scratch=(), scalars=0, flops=0):
    whole = pl.BlockSpec(memory_space=pltpu.VMEM)
    scalar = pl.BlockSpec(memory_space=pltpu.SMEM)
    return pl.pallas_call(
        kernel,
        out_shape=tuple(jax.ShapeDtypeStruct(shape, kind) for shape, kind in outs),
        in_specs=[scalar] * scalars + [whole] * (len(args) - scalars),
        out_specs=tuple(whole for _ in outs),
        scratch_shapes=list(scratch),
        compiler_params=pltpu.CompilerParams(vmem_limit_bytes=VMEM_LIMIT),
        cost_estimate=pl.CostEstimate(flops=flops, bytes_accessed=10 * 2**20, transcendentals=0),
    )(*args)


def zigzag_pairs(n):
    def place(chunk):
        return chunk if chunk < n else 2 * n - 1 - chunk

    evens = [(i, place(2 * i)) for i in range(n)]
    odds = [(i, place(2 * i + 1)) for i in range(n)]
    return evens, odds


def on_device(
    inputs, encoder, cotangent, w_self, w_self_out, w_cross_q, w_cross_kv, w_cross_out, w_up, w_down,
    biases, norm_gains, up_bias, source_lengths,
):
    n = lax.axis_size("sp")
    n_dp = lax.axis_size("dp")
    _, rows, width = inputs.shape
    size = rows // 2
    length = n * rows
    hidden_units = w_up.shape[1]
    own = w_self.shape[0]
    d = lax.axis_index("sp").astype(jnp.int32).reshape(1)
    limit = source_lengths.astype(jnp.int32)

    groups = up_bias.shape[0] // own
    first = jnp.concatenate(
        [w_self, biases.T, norm_gains.T, up_bias.reshape(groups, own).T,
         jnp.zeros((own, PAIR - 13 - groups), bf16)], axis=1,
    )
    first = lax.all_gather(first, "dp", axis=0, tiled=True)
    x_full = lax.all_gather(inputs[0], "sp", axis=0, tiled=True)
    rest = jnp.concatenate([w_cross_kv, w_self_out, w_cross_q, w_cross_out, w_up], axis=1)
    rest = lax.all_gather(rest, "dp", axis=0, tiled=True)
    full_down = lax.all_gather(w_down, "dp", axis=0, tiled=True)
    enc_full = lax.all_gather(encoder[0], "sp", axis=0, tiled=True)
    evens, odds = zigzag_pairs(n)
    cot0 = lax.ppermute(cotangent[0, :size], "sp", evens)
    cot1 = lax.ppermute(cotangent[0, size:], "sp", odds)

    full_self = first[:, : 3 * width]
    vec = first[:, 3 * width :].T.astype(f32)
    upb = (
        vec[13 : 13 + groups].reshape(groups, n_dp, own).transpose(1, 0, 2).reshape(1, hidden_units)
    )
    wckv = rest[:, : 2 * width]
    wso = rest[:, 2 * width : 3 * width]
    wcq = rest[:, 3 * width : 4 * width]
    wco = rest[:, 4 * width : 5 * width]
    wup = rest[:, 5 * width :]

    q, k, v, att, lse = run_kernel(
        functools.partial(self_forward_kernel, n),
        [((rows, width), bf16), ((length, width), bf16), ((length, width), bf16),
         ((rows, width), bf16), ((rows, PAIR), f32)],
        (d, x_full, full_self, vec), scalars=1, flops=6 * 10**9,
    )
    res1, cq, ek, ev, catt, clse = run_kernel(
        functools.partial(cross_forward_kernel, n),
        [((rows, width), f32), ((rows, width), bf16), ((length, width), bf16),
         ((length, width), bf16), ((rows, width), bf16), ((rows, PAIR), f32)],
        (d, limit, att, x_full, enc_full, wso, wcq, wckv, vec), scalars=2, flops=12 * 10**9,
    )
    piece = width // n
    up_piece = hidden_units // n
    out0, out1, gtwo, cgrad, gw1, upsum, small = run_kernel(
        functools.partial(feed_forward_kernel, n_dp, n),
        [((size, width), bf16), ((size, width), bf16), ((rows, width), f32), ((rows, width), bf16),
         ((n_dp, n, own, piece + up_piece + groups * piece), bf16), ((8, hidden_units), f32),
         ((16, width), f32)],
        (res1, catt, wco, wup, full_down, vec, upb, cot0, cot1),
        scratch=[pltpu.VMEM((rows, hidden_units), f32), pltpu.VMEM((rows, hidden_units), bf16),
                 pltpu.VMEM((rows, hidden_units), bf16)],
        flops=8 * 10**9,
    )
    back_scratch = [
        pltpu.VMEM((width, rows), bf16), pltpu.VMEM((width, rows), bf16), pltpu.VMEM((rows, width), bf16),
        pltpu.VMEM((width, length), f32), pltpu.VMEM((width, length), f32),
        pltpu.VMEM((2 * width, length), bf16),
    ]
    genc, gone, sgrad, gw2, small = run_kernel(
        functools.partial(cross_backward_kernel, n_dp, n),
        [((length, width), bf16), ((rows, width), f32), ((rows, width), bf16),
         ((n_dp, n, own, 4 * piece), bf16), ((16, width), f32)],
        (limit, cq, ek, ev, catt, cgrad, clse, enc_full, wcq, wckv, wso, vec, res1, att, gtwo, small),
        scratch=back_scratch, scalars=1, flops=24 * 10**9,
    )
    gin, gw3, small = run_kernel(
        functools.partial(self_backward_kernel, n, n_dp, n),
        [((length, width), bf16), ((n_dp, n, own, 3 * piece), bf16), ((16, width), f32)],
        (d, q, k, v, att, sgrad, lse, x_full, full_self, gone, small),
        scratch=back_scratch, scalars=1, flops=16 * 10**9,
    )

    back0 = [(b, a) for a, b in evens]
    back1 = [(b, a) for a, b in odds]
    output = jnp.concatenate(
        [lax.ppermute(out0, "sp", back0), lax.ppermute(out1, "sp", back1)], axis=0
    )[None]
    grad_encoder = lax.psum_scatter(genc, "sp", scatter_dimension=0, tiled=True).astype(f32)[None]
    grad_inputs = lax.psum_scatter(gin, "sp", scatter_dimension=0, tiled=True).astype(f32)[None]

    def reduce_blocks(blocks):
        part = lax.psum_scatter(blocks, "dp", scatter_dimension=0)
        return lax.psum_scatter(part, "sp", scatter_dimension=0).astype(f32)

    one, two, three = reduce_blocks(gw1), reduce_blocks(gw2), reduce_blocks(gw3)
    cells = width // (n_dp * n)
    up_cells = hidden_units // (n_dp * n)
    tiny = jnp.concatenate(
        [small[:13].reshape(13, n_dp, n, cells).transpose(1, 2, 0, 3).reshape(n_dp, n, 13 * cells),
         upsum[0].reshape(n_dp, n, up_cells)], axis=-1,
    )
    tiny = reduce_blocks(tiny.astype(bf16))
    grad_rows = tiny[: 13 * cells].reshape(13, cells)
    return (
        output,
        grad_inputs,
        grad_encoder,
        three_split(three, piece, 0),
        two[:, 3 * piece :],
        two[:, :piece],
        two[:, piece : 3 * piece],
        one[:, :piece],
        one[:, piece : piece + up_piece],
        one[:, piece + up_piece :].reshape(own, groups, piece).transpose(1, 0, 2).reshape(groups * own, piece),
        grad_rows[:10],
        grad_rows[10:],
        tiny[13 * cells :],
    )


def three_split(blocks, piece, start):
    return blocks[:, start : start + 3 * piece]


def solution(mesh):
    weight = P("dp", None)
    tokens = P("dp", "sp", None)
    return jax.shard_map(
        on_device,
        mesh=mesh,
        in_specs=(tokens,) * 3 + (weight,) * 7 + (P(None, "dp"), P(None, "dp"), P("dp"), P("dp")),
        out_specs=(tokens,) * 3
        + (P("dp", "sp"),) * 7
        + (P(None, ("dp", "sp")), P(None, ("dp", "sp")), P(("dp", "sp"))),
        check_vma=False,
    )
```

```python
import functools

import jax
import jax.numpy as jnp
from jax import lax
from jax.experimental import pallas as pl
from jax.experimental.pallas import tpu as pltpu
from jax.sharding import PartitionSpec as P

H = 8
DH = 64
PAIR = 128

eps_norm = 1e-05
masked_out = -1e30
bf16 = jnp.bfloat16
f32 = jnp.float32
SCALE = DH ** (-0.5)

VMEM_LIMIT = 60 * 2**20


def nn(left, right):
    return lax.dot_general(left, right, (((1,), (0,)), ((), ())), preferred_element_type=f32)


def nt(left, right):
    return lax.dot_general(left, right, (((1,), (1,)), ((), ())), preferred_element_type=f32)


def tn(left, right):
    return lax.dot_general(left, right, (((0,), (0,)), ((), ())), preferred_element_type=f32)


def norm_stats(resid):
    centred = resid - jnp.mean(resid, axis=-1, keepdims=True)
    inv_std = lax.rsqrt(jnp.mean(centred * centred, axis=-1, keepdims=True) + eps_norm)
    return centred * inv_std, inv_std


def norm_backward(upstream, normed, inv_std, gain):
    scaled = upstream * gain
    centre_term = jnp.mean(scaled, axis=-1, keepdims=True)
    slope_term = jnp.mean(scaled * normed, axis=-1, keepdims=True)
    return inv_std * (scaled - centre_term - normed * slope_term)


def col_sum(value):
    return jnp.sum(value, axis=0, keepdims=True)


def chunk_of(d, block, n):
    even = d if d % 2 == 0 else 2 * n - 1 - d
    return even if block == 0 else 2 * n - 1 - even


def lane_head(rows, cols=PAIR):
    return lax.broadcasted_iota(jnp.int32, (rows, cols), 1) // DH


def one_head(pair_value, head):
    return jnp.where(lane_head(*pair_value.shape) == head, pair_value, jnp.zeros_like(pair_value))


def pair_slice(pair):
    return pl.ds(pl.multiple_of(pair * PAIR, PAIR), PAIR)


def write_blocks(out_ref, value, col0, n_dp, n_sp):
    rows = value.shape[0] // n_dp
    cols = value.shape[1] // n_sp
    low = value.astype(bf16)
    for i in range(n_dp):
        for j in range(n_sp):
            out_ref[i, j, :, col0 : col0 + cols] = low[
                i * rows : (i + 1) * rows, j * cols : (j + 1) * cols
            ]


def attend_rows(q_ref, k_ref, v_ref, att_ref, lse_ref, row0, rows, parts, pair):
    cols = pair_slice(pair)
    q2 = q_ref[row0 : row0 + rows, cols]
    both = []
    lse_now = lse_ref[row0 : row0 + rows, :]
    lane = lax.broadcasted_iota(jnp.int32, (rows, PAIR), 1)
    for h in range(2):
        qm = one_head(q2, h)
        scores = []
        for start, size, mask in parts:
            s = nt(qm, k_ref[start : start + size, cols])
            if mask is not None:
                s = jnp.where(mask(rows, size), s, masked_out)
            scores.append(s)
        top = functools.reduce(
            jnp.maximum, [jnp.max(s, axis=-1, keepdims=True) for s in scores]
        )
        total = 0.0
        result = 0.0
        for s, (start, size, _) in zip(scores, parts):
            e = jnp.exp(s - top)
            total = total + jnp.sum(e, axis=-1, keepdims=True)
            result = result + nn(e.astype(bf16), v_ref[start : start + size, cols])
        both.append(result / total)
        lse_now = jnp.where(lane == pair * 2 + h, top + jnp.log(total), lse_now)
    lse_ref[row0 : row0 + rows, :] = lse_now
    att_ref[row0 : row0 + rows, cols] = jnp.where(
        lane_head(rows) == 0, both[0], both[1]
    ).astype(bf16)


def attend_rows_back(
    q_ref, k_ref, v_ref, att_ref, g_ref, lse_ref, qt_ref, gt_ref,
    dq_ref, dkt_ref, dvt_ref, row0, rows, parts, pair,
):
    cols = pair_slice(pair)
    q2 = q_ref[row0 : row0 + rows, cols]
    g2 = g_ref[row0 : row0 + rows, cols]
    prod = g2.astype(f32) * att_ref[row0 : row0 + rows, cols].astype(f32)
    lse_all = lse_ref[row0 : row0 + rows, :]
    lane = lax.broadcasted_iota(jnp.int32, (rows, PAIR), 1)
    both = []
    for h in range(2):
        head = pair * 2 + h
        hrows = pl.ds(pl.multiple_of(head * DH, DH), DH)
        qm = one_head(q2, h)
        gm = one_head(g2, h)
        qt = qt_ref[hrows, row0 : row0 + rows]
        gt = gt_ref[hrows, row0 : row0 + rows]
        lse = jnp.sum(jnp.where(lane == head, lse_all, 0.0), axis=-1, keepdims=True)
        delta = jnp.sum(jnp.where(lane // DH == h, prod, 0.0), axis=-1, keepdims=True)
        dq = 0.0
        for start, size, mask, adds in parts:
            k2 = k_ref[start : start + size, cols]
            v2 = v_ref[start : start + size, cols]
            p = jnp.exp(nt(qm, k2) - lse)
            if mask is not None:
                p = jnp.where(mask(rows, size), p, 0.0)
            ds = (p * (nt(gm, v2) - delta)).astype(bf16)
            dq = dq + nn(ds, k2)
            dk = nn(qt, ds)
            dv = nn(gt, p.astype(bf16))
            if adds:
                dk = dk + dkt_ref[hrows, start : start + size]
                dv = dv + dvt_ref[hrows, start : start + size]
            dkt_ref[hrows, start : start + size] = dk
            dvt_ref[hrows, start : start + size] = dv
        both.append(dq)
    dq_ref[row0 : row0 + rows, cols] = (
        jnp.where(lane_head(rows) == 0, both[0], both[1]).astype(bf16)
    )


def diagonal(rows, size):
    row = lax.broadcasted_iota(jnp.int32, (rows, size), 0)
    col = lax.broadcasted_iota(jnp.int32, (rows, size), 1)
    return col <= row


def causal_parts(chunk, size):
    parts = []
    if chunk:
        parts.append((0, chunk * size, None))
    parts.append((chunk * size, size, diagonal))
    return parts


WORKER, CHIP, CORE, PLACE, SEQ = range(5)


def even_chunk(w, n):
    return jnp.where(w % 2 == 0, w, 2 * n - 1 - w)


def self_forward_kernel(n, n_dp, scal_ref, idx_ref, *refs):
    chips = n_dp // 2
    x_refs, refs = refs[:n], refs[n:]
    own_refs, refs = refs[:chips], refs[chips:]
    partner_ref, refs = refs[0], refs[1:]
    q_ref, k_ref, v_ref, att_ref, lse_ref, x_ref, xq_ref, w_ref, vec_ref, s_scr = refs
    length, width = x_ref.shape
    rows = q_ref.shape[0]
    size = rows // 2
    own = own_refs[0].shape[0]
    w, chip, core = scal_ref[WORKER], scal_ref[CHIP], scal_ref[CORE]
    for m in range(chips):
        for side in range(2):
            place = 2 * (chip ^ m) + (core ^ side)
            here = pl.ds(pl.multiple_of(place * own, own), own)
            block = own_refs[m][...] if side == 0 else partner_ref[m * own : (m + 1) * own, :]
            w_ref[here, :] = block[:, : 3 * width]
            s_scr[here, :] = block[:, 3 * width :]
    vec_ref[...] = s_scr[...].astype(f32).T[: vec_ref.shape[0], :]
    for t in range(n):
        here = pl.ds(pl.multiple_of(idx_ref[t] * rows, rows), rows)
        x_ref[here, :] = x_refs[t][...]
        kv = nn(x_refs[t][...], w_ref[:, width : 3 * width])
        k_ref[here, :] = kv[:, :width].astype(bf16)
        v_ref[here, :] = (kv[:, width:] + vec_ref[1:2, :]).astype(bf16)
    even = even_chunk(w, n)
    for block in range(2):
        chunk = even if block == 0 else 2 * n - 1 - even
        xb = x_ref[pl.ds(pl.multiple_of(chunk * size, size), size), :]
        own_rows = slice(block * size, (block + 1) * size)
        xq_ref[own_rows, :] = xb
        q_ref[own_rows, :] = ((nn(xb, w_ref[:, :width]) + vec_ref[0:1, :]) * SCALE).astype(bf16)
    lse_ref[...] = jnp.zeros_like(lse_ref)

    for which in range(n):

        @pl.when(w == which)
        def _(which=which):
            def pairs(pair, carry):
                for block in range(2):
                    chunk = chunk_of(which, block, n)
                    attend_rows(
                        q_ref, k_ref, v_ref, att_ref, lse_ref, block * size, size,
                        causal_parts(chunk, size), pair,
                    )
                return carry

            lax.fori_loop(0, H // 2, pairs, 0)


def length_limit(scal_ref, vec_ref, own):
    packed = vec_ref[17:18, :] * 64.0 + vec_ref[18:19, :]
    lane = lax.broadcasted_iota(jnp.int32, packed.shape, 1)
    picked = jnp.where(lane == scal_ref[SEQ] * own, packed, 0.0)
    return jnp.sum(picked, axis=-1, keepdims=True).astype(jnp.int32)


def cross_forward_kernel(n, own, scal_ref, idx_ref, *refs):
    enc_refs, refs = refs[:n], refs[n:]
    (att_ref, xq_ref, wso_ref, wcq_ref, wckv_ref, vec_ref,
     res_ref, cq_ref, ek_ref, ev_ref, catt_ref, clse_ref, enc_ref) = refs
    length, width = enc_ref.shape
    rows = att_ref.shape[0]
    size = rows // 2
    res_ref[...] = xq_ref[...].astype(f32) + nn(att_ref[...], wso_ref[...]) + vec_ref[2:3, :]
    normed, _ = norm_stats(res_ref[...])
    hidden = (normed * vec_ref[10:11, :] + vec_ref[7:8, :]).astype(bf16)
    cq_ref[...] = ((nn(hidden, wcq_ref[...]) + vec_ref[3:4, :]) * SCALE).astype(bf16)
    for t in range(n):
        here = pl.ds(pl.multiple_of(idx_ref[t] * rows, rows), rows)
        enc_ref[here, :] = enc_refs[t][...]
        kv = nn(enc_refs[t][...], wckv_ref[...])
        ek_ref[here, :] = kv[:, :width].astype(bf16)
        ev_ref[here, :] = (kv[:, width:] + vec_ref[4:5, :]).astype(bf16)
    clse_ref[...] = jnp.zeros_like(clse_ref)
    limit = length_limit(scal_ref, vec_ref, own)

    def visible(count, keys):
        return lax.broadcasted_iota(jnp.int32, (count, keys), 1) < limit

    def pairs(pair, carry):
        for block in range(2):
            attend_rows(
                cq_ref, ek_ref, ev_ref, catt_ref, clse_ref, block * size, size,
                [(0, length, visible)], pair,
            )
        return carry

    lax.fori_loop(0, H // 2, pairs, 0)


def feed_forward_kernel(
    n_dp, n_sp, res1_ref, catt_ref, wco_ref, wup_ref, wdn_ref, vec_ref, upb_ref, cot0_ref, cot1_ref,
    out0_ref, out1_ref, gtwo_ref, cgrad_ref, gw_ref, upsum_ref, small_ref,
    up_scr, act_scr, upl_scr,
):
    rows, width = res1_ref.shape
    size = rows // 2
    hidden_units = wup_ref.shape[1]
    step = min(512, hidden_units)
    blocks = hidden_units // step
    normed, _ = norm_stats(res1_ref[...])
    hidden_one = normed * vec_ref[10:11, :] + vec_ref[7:8, :]
    res2 = hidden_one + nn(catt_ref[...], wco_ref[...]) + vec_ref[5:6, :]
    normed2, inv2 = norm_stats(res2)
    hidden_two = normed2 * vec_ref[11:12, :] + vec_ref[8:9, :]
    h2_low = hidden_two.astype(bf16)
    down = jnp.zeros((rows, width), f32)
    for b in range(blocks):
        cols = slice(b * step, (b + 1) * step)
        up = nn(h2_low, wup_ref[:, cols]) + upb_ref[0:1, cols]
        up_scr[:, cols] = up
        act = (up * jax.nn.sigmoid(up)).astype(bf16)
        act_scr[:, cols] = act
        down = down + nn(act, wdn_ref[cols, :])
    res3 = hidden_two + down + vec_ref[6:7, :]
    normed3, inv3 = norm_stats(res3)
    result = (normed3 * vec_ref[12:13, :] + vec_ref[9:10, :]).astype(bf16)
    out0_ref[...] = result[:size]
    out1_ref[...] = result[size:]
    upstream = jnp.concatenate([cot0_ref[...], cot1_ref[...]], axis=0).astype(f32)
    small_ref[...] = jnp.zeros_like(small_ref)
    small_ref[12:13, :] = col_sum(upstream * normed3)
    small_ref[9:10, :] = col_sum(upstream)
    grad_three = norm_backward(upstream, normed3, inv3, vec_ref[12:13, :])
    small_ref[6:7, :] = col_sum(grad_three)
    down_low = grad_three.astype(bf16)
    h2_t = h2_low.T
    grad_h2 = grad_three
    part_rows = hidden_units // n_dp
    own_rows = width // n_dp
    groups = part_rows // own_rows
    piece = width // n_sp
    up_piece = hidden_units // n_sp
    for b in range(blocks):
        cols = slice(b * step, (b + 1) * step)
        gdown = tn(act_scr[:, cols], down_low).astype(bf16)
        for r in range(step // own_rows):
            at = b * step + r * own_rows
            i, g = at // part_rows, (at % part_rows) // own_rows
            for j in range(n_sp):
                base = piece + up_piece + g * piece
                gw_ref[i, j, :, base : base + piece] = gdown[
                    r * own_rows : (r + 1) * own_rows, j * piece : (j + 1) * piece
                ]
        up = up_scr[:, cols]
        sig = jax.nn.sigmoid(up)
        up_low = (
            nt(down_low, wdn_ref[cols, :]) * sig * (1.0 + up * (1.0 - sig))
        ).astype(bf16)
        upl_scr[:, cols] = up_low
        upsum_ref[0:1, cols] = col_sum(up_low.astype(f32))
        grad_h2 = grad_h2 + nt(up_low, wup_ref[:, cols])
    for j in range(n_sp):
        cols = slice(j * up_piece, (j + 1) * up_piece)
        gup = nn(h2_t, upl_scr[:, cols]).astype(bf16)
        for i in range(n_dp):
            gw_ref[i, j, :, piece : piece + up_piece] = gup[i * own_rows : (i + 1) * own_rows, :]
    small_ref[11:12, :] = col_sum(grad_h2 * normed2)
    small_ref[8:9, :] = col_sum(grad_h2)
    grad_two = norm_backward(grad_h2, normed2, inv2, vec_ref[11:12, :])
    small_ref[5:6, :] = col_sum(grad_two)
    gtwo_ref[...] = grad_two
    two_low = grad_two.astype(bf16)
    write_blocks(gw_ref, tn(catt_ref[...], two_low), 0, n_dp, n_sp)
    cgrad_ref[...] = nt(two_low, wco_ref[...]).astype(bf16)


def ones_sum(t_ref):
    return nt(jnp.ones((8, t_ref.shape[1]), bf16), t_ref[...])[0:1, :]


def cross_backward_kernel(
    n, own, scal_ref, idx_ref, cq_ref, ek_ref, ev_ref, catt_ref, cgrad_ref, clse_ref, enc_ref,
    wcq_ref, wckv_ref, wso_ref, vec_ref, res1_ref, att_ref, gtwo_ref, small_in_ref,
    mine_ref, theirs_ref, gone_ref, sgrad_ref, gw_ref, small_ref,
    qt_scr, gt_scr, dq_scr, dkt_scr, dvt_scr, low_scr,
):
    length, width = enc_ref.shape
    rows = cq_ref.shape[0]
    size = rows // 2
    qt_scr[...] = cq_ref[...].T
    gt_scr[...] = cgrad_ref[...].T
    half = length // 2
    limit = length_limit(scal_ref, vec_ref, own)

    def pairs(pair, carry):
        for block in range(2):
            parts = []
            for part in range(2):
                start = part * half

                def visible(count, keys, start=start):
                    return lax.broadcasted_iota(jnp.int32, (count, keys), 1) + start < limit

                parts.append((start, half, visible, block == 1))
            attend_rows_back(
                cq_ref, ek_ref, ev_ref, catt_ref, cgrad_ref, clse_ref, qt_scr, gt_scr,
                dq_scr, dkt_scr, dvt_scr, block * size, size, parts, pair,
            )
        return carry

    lax.fori_loop(0, H // 2, pairs, 0)
    low_scr[:width, :] = dkt_scr[...].astype(bf16)
    low_scr[width:, :] = dvt_scr[...].astype(bf16)
    query_grad = (dq_scr[...].astype(f32) * SCALE).astype(bf16)
    small_ref[...] = small_in_ref[...]
    small_ref[3:4, :] = col_sum(query_grad.astype(f32))
    small_ref[4:5, :] = ones_sum(low_scr.at[width:, :])
    normed, inv = norm_stats(res1_ref[...])
    hidden = (normed * vec_ref[10:11, :] + vec_ref[7:8, :]).astype(bf16)
    gw_ref[:, :width] = tn(hidden, query_grad).astype(bf16)
    grad_h1 = gtwo_ref[...] + nt(query_grad, wcq_ref[...])
    small_ref[10:11, :] = col_sum(grad_h1 * normed)
    small_ref[7:8, :] = col_sum(grad_h1)
    grad_one = norm_backward(grad_h1, normed, inv, vec_ref[10:11, :])
    small_ref[2:3, :] = col_sum(grad_one)
    gone_ref[...] = grad_one
    one_low = grad_one.astype(bf16)
    gw_ref[:, 3 * width : 4 * width] = tn(att_ref[...], one_low).astype(bf16)
    sgrad_ref[...] = nt(one_low, wso_ref[...]).astype(bf16)
    gw_ref[:, width : 3 * width] = nn(low_scr[...], enc_ref[...]).T.astype(bf16)
    for t in range(n):
        here = pl.ds(pl.multiple_of(idx_ref[t] * rows, rows), rows)
        out_ref, slot = (mine_ref, t) if t < n // 2 else (theirs_ref, t - n // 2)
        out_ref[slot * rows : (slot + 1) * rows, :] = (
            nn(wckv_ref[...], low_scr[:, here]).T.astype(bf16)
        )


def self_backward_kernel(
    n, n_dp, blocked, scal_ref, idx_ref, q_ref, k_ref, v_ref, att_ref, sgrad_ref, lse_ref, x_ref, w_ref, gone_ref,
    small_in_ref, gw_in_ref,
    mine_ref, theirs_ref, gmine_ref, gtheirs_ref,
    qt_scr, gt_scr, dq_scr, dkt_scr, dvt_scr, low_scr, gin_scr, g_scr, small_scr, small_t_scr,
):
    length, width = x_ref.shape
    rows = q_ref.shape[0]
    size = rows // 2
    w, chip, core, place = (scal_ref[i] for i in (WORKER, CHIP, CORE, PLACE))
    qt_scr[...] = q_ref[...].T
    gt_scr[...] = sgrad_ref[...].T
    for which in range(n):

        @pl.when(w == which)
        def _(which=which):
            order = sorted(range(2), key=lambda block: -chunk_of(which, block, n))
            top = chunk_of(which, order[0], n)
            if top + 1 < 2 * n:
                rest = (2 * n - 1 - top) * size
                dkt_scr[:, (top + 1) * size :] = jnp.zeros((width, rest), f32)
                dvt_scr[:, (top + 1) * size :] = jnp.zeros((width, rest), f32)

            def pairs(pair, carry):
                for order_place, block in enumerate(order):
                    chunk = chunk_of(which, block, n)
                    parts = []
                    for start, count, mask in causal_parts(chunk, size):
                        while count > 4 * size:
                            parts.append((start, 4 * size, mask, order_place == 1))
                            start, count = start + 4 * size, count - 4 * size
                        parts.append((start, count, mask, order_place == 1))
                    attend_rows_back(
                        q_ref, k_ref, v_ref, att_ref, sgrad_ref, lse_ref, qt_scr, gt_scr,
                        dq_scr, dkt_scr, dvt_scr, block * size, size, parts, pair,
                    )
                return carry

            lax.fori_loop(0, H // 2, pairs, 0)

    low_scr[:width, :] = dkt_scr[...].astype(bf16)
    low_scr[width:, :] = dvt_scr[...].astype(bf16)
    q_grad = (dq_scr[...].astype(f32) * SCALE).astype(bf16)
    small_scr[...] = jnp.zeros_like(small_scr)
    small_scr[: small_in_ref.shape[0], :] = small_in_ref[...]
    small_scr[0:1, :] = col_sum(q_grad.astype(f32))
    small_scr[1:2, :] = ones_sum(low_scr.at[width:, :])
    for t in range(n):
        here = pl.ds(pl.multiple_of(t * rows, rows), rows)
        gin_scr[here, :] = nn(w_ref[:, width:], low_scr[:, here]).T
    even = even_chunk(w, n)
    wq_grad = jnp.zeros((width, width), f32)
    for block in range(2):
        chunk = even if block == 0 else 2 * n - 1 - even
        here = pl.ds(pl.multiple_of(chunk * size, size), size)
        own_rows = slice(block * size, (block + 1) * size)
        wq_grad = wq_grad + tn(x_ref[here, :], q_grad[own_rows])
        gin_scr[here, :] += gone_ref[own_rows, :] + nt(q_grad[own_rows], w_ref[:, :width])
    for t in range(n):
        here = pl.ds(pl.multiple_of(idx_ref[t] * rows, rows), rows)
        out_ref, slot = (mine_ref, t) if t < n // 2 else (theirs_ref, t - n // 2)
        out_ref[slot * rows : (slot + 1) * rows, :] = gin_scr[here, :].astype(bf16)
    small_t_scr[...] = small_scr[...].T
    if not blocked:
        gmine_ref[:, :width] = wq_grad.astype(bf16)
        gmine_ref[:, width : 3 * width] = nn(low_scr[...], x_ref[...]).T.astype(bf16)
        gmine_ref[:, 3 * width :] = gw_in_ref[...]
        gtheirs_ref[...] = small_t_scr[...].astype(bf16)
        return
    g_scr[:, :width] = wq_grad.astype(bf16)
    g_scr[:, width : 3 * width] = nn(low_scr[...], x_ref[...]).T.astype(bf16)
    own = width // n_dp
    piece = width // n
    cells = own // n
    for side, out_ref in enumerate((gmine_ref, gtheirs_ref)):

        def chips(m, carry, side=side, out_ref=out_ref):
            part = 2 * (chip ^ m) + (core ^ side)
            here = pl.ds(pl.multiple_of(part * own, own), own)
            for s in range(n):
                j = (place + s) % n
                out_ref[m, s, :own, : 3 * piece] = g_scr[
                    here, pl.ds(pl.multiple_of(j * 3 * piece, 3 * piece), 3 * piece)
                ]
                for start, wide, at in (
                    (0, 1, 3), (width, 2, 4), (3 * width, 1, 6)
                ):
                    cols = pl.ds(pl.multiple_of(start + j * wide * piece, PAIR), wide * piece)
                    out_ref[m, s, :own, at * piece : (at + wide) * piece] = gw_in_ref[here, cols]
                tiny = pl.ds(pl.multiple_of(part * own + j * cells, cells), cells)
                out_ref[m, s, own:, :PAIR] = small_t_scr[tiny, :].astype(bf16)
                out_ref[m, s, own:, PAIR:] = jnp.zeros((cells, 7 * piece - PAIR), bf16)
            return carry

        lax.fori_loop(0, n_dp // 2, chips, 0)


def run_kernel(kernel, outs, args, scratch=(), scalars=0, flops=0):
    whole = pl.BlockSpec(memory_space=pltpu.VMEM)
    plain = [arg for arg in args if not isinstance(arg, tuple)]
    parts = [arg for arg in args if isinstance(arg, tuple)]
    sources = []
    for arg in parts:
        if not any(arg[0] is source for source in sources):
            sources.append(arg[0])
    specs = [pl.BlockSpec(memory_space=pltpu.SMEM)] * scalars + [whole] * (len(plain) - scalars)
    specs += [pl.BlockSpec(memory_space=pl.ANY)] * len(sources)
    held = [pltpu.VMEM((arg[0].shape[0], arg[2]), arg[0].dtype) for arg in parts]
    extra = held + ([pltpu.SemaphoreType.DMA((len(parts),))] if parts else [])

    def body(*refs):
        plain_refs, refs = refs[: len(plain)], refs[len(plain) :]
        source_refs, refs = refs[: len(sources)], refs[len(sources) :]
        extra_refs, refs = refs[len(refs) - len(extra) :], refs[: len(refs) - len(extra)]
        copies = []
        for i, (source, start, cols) in enumerate(parts):
            at = [i for i, other in enumerate(sources) if other is source][0]
            copies.append(
                pltpu.make_async_copy(
                    source_refs[at].at[:, start : start + cols], extra_refs[i], extra_refs[-1].at[i]
                )
            )
        for copy in copies:
            copy.start()
        for copy in copies:
            copy.wait()
        left, held_refs, in_refs = list(plain_refs), list(extra_refs), []
        for arg in args:
            in_refs.append(held_refs.pop(0) if isinstance(arg, tuple) else left.pop(0))
        kernel(*in_refs, *refs)

    return pl.pallas_call(
        body,
        out_shape=tuple(jax.ShapeDtypeStruct(shape, kind) for shape, kind in outs),
        in_specs=specs,
        out_specs=tuple(whole for _ in outs),
        scratch_shapes=list(scratch) + extra,
        compiler_params=pltpu.CompilerParams(vmem_limit_bytes=VMEM_LIMIT),
        cost_estimate=pl.CostEstimate(flops=flops, bytes_accessed=10 * 2**20, transcendentals=0),
    )(*plain, *sources)


class Routes:
    def __init__(self, n, n_dp):
        self.n, self.h = n, n // 2
        self.chips = n_dp // 2

    def all_chips(self, pairs):
        return [
            ((2 * k + c0) * self.n + z0, (2 * k + c1) * self.n + z1)
            for k in range(self.chips)
            for (c0, z0), (c1, z1) in pairs
        ]

    def gather(self, r):
        h = self.h
        pairs = []
        for c in range(2):
            for i in range(h):
                far = (c, (1 - c) * h + i)
                if r < h:
                    pairs.append(((c, c * h + i), (1 - c, c * h + (i + r) % h)))
                    pairs.append((far, (c, c * h + (i + r - 1) % h)))
                else:
                    pairs.append((far, (1 - c, c * h + (i + h - 1) % h)))
        return self.all_chips(pairs)

    def slots(self, z, core):
        h = self.h
        c, g = z // h, z % h

        def half(home):
            at_home = [z] + [(1 - c) * h + (g - (r - 1)) % h for r in range(1, h)]
            at_other = [(1 - c) * h + (g - (h - 1)) % h] + [c * h + (g - r) % h for r in range(1, h)]
            return [jnp.where(home, a, b) for a, b in zip(at_home, at_other)]

        home = core == c
        return half(home) + half(jnp.logical_not(home)), home

    def rows(self, odd):
        n, h = self.n, self.h
        pairs = []
        for c in range(2):
            for z in range(n):
                chunk = 2 * z + odd
                w = chunk if chunk < n else 2 * n - 1 - chunk
                pairs.append(((c, z), (w % 2, c * h + w // 2)))
        return self.all_chips(pairs)


def back(pairs):
    return [(b, a) for a, b in pairs]


BOTH = ("dp", "sp")


def after(first, then):
    return lax.optimization_barrier((first, then))[1]


def on_device(
    inputs, encoder, cotangent, w_self, w_self_out, w_cross_q, w_cross_kv, w_cross_out, w_up, w_down,
    biases, norm_gains, up_bias, source_lengths,
):
    n = lax.axis_size("sp")
    n_dp = lax.axis_size("dp")
    chips = n_dp // 2
    h = n // 2
    _, rows, width = inputs.shape
    size = rows // 2
    length = n * rows
    hidden_units = w_up.shape[1]
    own = w_self.shape[0]
    piece = width // n
    up_piece = hidden_units // n
    cells = own // n
    groups = up_bias.shape[0] // own
    blocked = piece % PAIR == 0 and cells % 16 == 0
    routes = Routes(n, n_dp)
    z = lax.axis_index("sp").astype(jnp.int32)
    dp = lax.axis_index("dp").astype(jnp.int32)
    chip, core = dp // 2, dp % 2
    seq_core = z // h
    slots, home = routes.slots(z, core)
    idx = jnp.stack(slots).astype(jnp.int32)
    scal = jnp.stack([2 * (z % h) + core, chip, core, z, 2 * chip + seq_core]).astype(jnp.int32)

    def swap(value):
        return lax.ppermute(value, "dp", [(i, i ^ 1) for i in range(n_dp)])

    def to_chip(value, m):
        return lax.ppermute(value, "dp", [(i, i ^ (2 * m)) for i in range(n_dp)])

    def shift(value, s):
        return lax.ppermute(value, "sp", [(i, (i + s) % n) for i in range(n)])

    def gather(value):
        arrived = [lax.ppermute(value, BOTH, routes.gather(r)) for r in range(1, h + 1)]
        first = jnp.where(home, value, arrived[-1])
        mine = [first] + arrived[:-1]
        return mine + [swap(part) for part in mine]

    lens = source_lengths.astype(jnp.int32).reshape(1, 1)
    first = jnp.concatenate(
        [w_self, biases.T, norm_gains.T, up_bias.reshape(groups, own).T,
         jnp.broadcast_to((lens // 64).astype(bf16), (own, 1)),
         jnp.broadcast_to((lens % 64).astype(bf16), (own, 1)),
         jnp.zeros((own, PAIR - 15 - groups), bf16)], axis=1,
    )
    x_pieces = gather(inputs[0])
    own_first = [first] + [to_chip(first, m) for m in range(1, chips)]
    partner_first = swap(jnp.concatenate(own_first, axis=0))
    rest = jnp.concatenate([w_up, w_cross_kv, w_self_out, w_cross_q, w_cross_out], axis=1)
    rest = lax.all_gather(rest, "dp", axis=0, tiled=True)
    full_down = lax.all_gather(w_down, "dp", axis=0, tiled=True)
    enc_pieces = gather(after(x_pieces[0], encoder[0]))
    late_cot = after(enc_pieces[0], cotangent[0])
    cot0 = lax.ppermute(late_cot[:size], BOTH, routes.rows(0))
    cot1 = lax.ppermute(late_cot[size:], BOTH, routes.rows(1))

    wup = (rest, 0, hidden_units)
    wckv = (rest, hidden_units, 2 * width)
    wso, wcq, wco = ((rest, hidden_units + (2 + i) * width, width) for i in range(3))

    q, k, v, att, lse, x_full, xq, full_self, vec = run_kernel(
        functools.partial(self_forward_kernel, n, n_dp),
        [((rows, width), bf16), ((length, width), bf16), ((length, width), bf16),
         ((rows, width), bf16), ((rows, PAIR), f32), ((length, width), bf16), ((rows, width), bf16),
         ((width, 3 * width), bf16), ((32, width), f32)],
        (scal, idx, *x_pieces, *own_first, partner_first),
        scratch=[pltpu.VMEM((width, PAIR), bf16)], scalars=2, flops=6 * 10**9,
    )
    upb = (
        vec[13 : 13 + groups].reshape(groups, n_dp, own).transpose(1, 0, 2).reshape(1, hidden_units)
    )
    res1, cq, ek, ev, catt, clse, enc_full = run_kernel(
        functools.partial(cross_forward_kernel, n, own),
        [((rows, width), f32), ((rows, width), bf16), ((length, width), bf16),
         ((length, width), bf16), ((rows, width), bf16), ((rows, PAIR), f32), ((length, width), bf16)],
        (scal, idx, *enc_pieces, att, xq, wso, wcq, wckv, vec), scalars=2, flops=12 * 10**9,
    )
    out0, out1, gtwo, cgrad, gw1, upsum, small = run_kernel(
        functools.partial(feed_forward_kernel, n_dp, n),
        [((size, width), bf16), ((size, width), bf16), ((rows, width), f32), ((rows, width), bf16),
         ((n_dp, n, own, piece + up_piece + groups * piece), bf16), ((8, hidden_units), f32),
         ((16, width), f32)],
        (res1, catt, wco, wup, full_down, vec, upb, cot0, cot1),
        scratch=[pltpu.VMEM((rows, hidden_units), f32), pltpu.VMEM((rows, hidden_units), bf16),
                 pltpu.VMEM((rows, hidden_units), bf16)],
        flops=8 * 10**9,
    )
    output = jnp.concatenate(
        [lax.ppermute(out0, BOTH, back(routes.rows(0))), lax.ppermute(out1, BOTH, back(routes.rows(1)))],
        axis=0,
    )[None]
    up_cells = hidden_units // (n_dp * n)
    up_rows = (
        upsum[0].reshape(n_dp * n, up_cells // cells, cells).transpose(1, 0, 2).reshape(groups, width)
    )
    back_scratch = [
        pltpu.VMEM((width, rows), bf16), pltpu.VMEM((width, rows), bf16), pltpu.VMEM((rows, width), bf16),
        pltpu.VMEM((width, length), f32), pltpu.VMEM((width, length), f32),
        pltpu.VMEM((2 * width, length), bf16),
    ]
    emine, etheirs, gone, sgrad, gw2, small = run_kernel(
        functools.partial(cross_backward_kernel, n, own),
        [((h * rows, width), bf16), ((h * rows, width), bf16), ((rows, width), f32), ((rows, width), bf16),
         ((width, 4 * width), bf16), ((16, width), f32)],
        (scal, idx, cq, ek, ev, catt, cgrad, clse, enc_full, wcq, wckv, wso, vec, res1, att, gtwo, small),
        scratch=back_scratch, scalars=2, flops=24 * 10**9,
    )

    def pieces_home(mine, theirs):
        arrived = swap(theirs)
        sums = [
            (mine[t * rows : (t + 1) * rows].astype(f32) + arrived[t * rows : (t + 1) * rows].astype(f32))
            .astype(bf16)
            for t in range(h)
        ]
        parts = [lax.ppermute(sums[r], BOTH, back(routes.gather(r))) for r in range(1, h)]
        last = lax.ppermute(sums[0], BOTH, back(routes.gather(h)))
        total = jnp.where(home, sums[0], last).astype(f32)
        for part in parts:
            total = total + part.astype(f32)
        return total[None]

    small = jnp.concatenate([small[:13], up_rows, jnp.zeros((3, width), f32)], axis=0)
    cols = 7 * piece
    if blocked:
        grad_outs = [((chips, n, own + cells, cols), bf16)] * 2
    else:
        grad_outs = [((width, 7 * width), bf16), ((width, PAIR), bf16)]
    gmine, gtheirs, block_mine, block_theirs = run_kernel(
        functools.partial(self_backward_kernel, n, n_dp, blocked),
        [((h * rows, width), bf16), ((h * rows, width), bf16), *grad_outs],
        (scal, idx, q, k, v, att, sgrad, lse, x_full, full_self, gone, small, gw2),
        scratch=back_scratch
        + [pltpu.VMEM((length, width), f32), pltpu.VMEM((width, 3 * width), bf16), pltpu.VMEM((PAIR, width), f32),
           pltpu.VMEM((width, PAIR), f32)],
        scalars=2, flops=16 * 10**9,
    )
    grad_encoder = pieces_home(emine, etheirs)
    grad_inputs = pieces_home(gmine, gtheirs)

    part = lax.psum_scatter(gw1, "dp", scatter_dimension=0)
    one = lax.psum_scatter(part, "sp", scatter_dimension=0).astype(f32)
    if blocked:
        arrived = swap(block_theirs)
        sums = [
            (block_mine[m].astype(f32) + arrived[m].astype(f32)).astype(bf16) for m in range(chips)
        ]
        total = sums[0].astype(f32)
        for m in range(1, chips):
            total = total + to_chip(sums[m], m).astype(f32)
        low = total.astype(bf16)
        final = low[0].astype(f32)
        for s in range(1, n):
            final = final + shift(low[s], s).astype(f32)
        main, tiny = final[:own], final[own:, :PAIR].T
        g_self, g_cq, g_ckv, g_so = (
            main[:, : 3 * piece], main[:, 3 * piece : 4 * piece], main[:, 4 * piece : 6 * piece],
            main[:, 6 * piece :],
        )
    else:

        def spread(value):
            part = lax.psum_scatter(value, "sp", scatter_dimension=1, tiled=True)
            return lax.psum_scatter(part, "dp", scatter_dimension=0, tiled=True).astype(f32)

        g_self = spread(block_mine[:, : 3 * width])
        g_cq = spread(block_mine[:, 3 * width : 4 * width])
        g_ckv = spread(block_mine[:, 4 * width : 6 * width])
        g_so = spread(block_mine[:, 6 * width :])
        everyone = lax.psum(block_theirs.astype(f32), BOTH)
        tiny = lax.dynamic_slice_in_dim(everyone, (dp * n + z) * cells, cells, 0).T
    return (
        output,
        grad_inputs,
        grad_encoder,
        g_self,
        g_so,
        g_cq,
        g_ckv,
        one[:, :piece],
        one[:, piece : piece + up_piece],
        one[:, piece + up_piece :].reshape(own, groups, piece).transpose(1, 0, 2).reshape(groups * own, piece),
        tiny[:10],
        tiny[10:13],
        tiny[13 : 13 + groups].reshape(up_cells),
    )


def solution(mesh):
    weight = P("dp", None)
    tokens = P("dp", "sp", None)
    return jax.shard_map(
        on_device,
        mesh=mesh,
        in_specs=(tokens,) * 3 + (weight,) * 7 + (P(None, "dp"), P(None, "dp"), P("dp"), P("dp")),
        out_specs=(tokens,) * 3
        + (P("dp", "sp"),) * 7
        + (P(None, ("dp", "sp")), P(None, ("dp", "sp")), P(("dp", "sp"))),
        check_vma=False,
    )
```

```python
import functools

import jax
import jax.numpy as jnp
from jax import lax
from jax.experimental import pallas as pl
from jax.experimental.pallas import tpu as pltpu
from jax.sharding import PartitionSpec as P

H = 8
DH = 64
PAIR = 128

eps_norm = 1e-05
masked_out = -1e30
bf16 = jnp.bfloat16
f32 = jnp.float32
SCALE = DH ** (-0.5)

VMEM = {
    "self_forward_kernel": 14,
    "cross_query_kernel": 10,
    "cross_forward_kernel": 14,
    "feed_forward_kernel": 26,
    "cross_backward_kernel": 17,
    "cross_backward_rest_kernel": 23,
    "norm_one_backward_kernel": 12,
    "self_backward_kernel": 28,
    "finish_kernel": 8,
    "pack_kernel": 60,
}


def nn(left, right):
    return lax.dot_general(left, right, (((1,), (0,)), ((), ())), preferred_element_type=f32)


def nt(left, right):
    return lax.dot_general(left, right, (((1,), (1,)), ((), ())), preferred_element_type=f32)


def tn(left, right):
    return lax.dot_general(left, right, (((0,), (0,)), ((), ())), preferred_element_type=f32)


def norm_stats(resid):
    centred = resid - jnp.mean(resid, axis=-1, keepdims=True)
    inv_std = lax.rsqrt(jnp.mean(centred * centred, axis=-1, keepdims=True) + eps_norm)
    return centred * inv_std, inv_std


def norm_backward(upstream, normed, inv_std, gain):
    scaled = upstream * gain
    centre_term = jnp.mean(scaled, axis=-1, keepdims=True)
    slope_term = jnp.mean(scaled * normed, axis=-1, keepdims=True)
    return inv_std * (scaled - centre_term - normed * slope_term)


def col_sum(value):
    return jnp.sum(value, axis=0, keepdims=True)


def chunk_of(d, block, n):
    even = d if d % 2 == 0 else 2 * n - 1 - d
    return even if block == 0 else 2 * n - 1 - even


def lane_head(rows, cols=PAIR):
    return lax.broadcasted_iota(jnp.int32, (rows, cols), 1) // DH


def one_head(pair_value, head):
    return jnp.where(lane_head(*pair_value.shape) == head, pair_value, jnp.zeros_like(pair_value))


def pair_slice(pair):
    return pl.ds(pl.multiple_of(pair * PAIR, PAIR), PAIR)


class Here:
    def __init__(self):
        self.n, self.n_dp = lax.axis_size("sp"), lax.axis_size("dp")
        dp = lax.axis_index("dp").astype(jnp.int32)
        self.z = lax.axis_index("sp").astype(jnp.int32)
        self.h = self.n // 2
        self.chip, self.core = dp // 2, dp % 2
        self.dp = dp
        self.half = self.z // self.h
        self.local = self.z % self.h
        self.worker = 2 * self.local + self.core
        self.seq = 2 * self.chip + self.half
        self.home = self.core == self.half

    def slots(self):
        h, c, g = self.h, self.half, self.local

        def part(home):
            at_home = [self.z] + [(1 - c) * h + (g + h - (r - 1)) % h for r in range(1, h)]
            at_other = [(1 - c) * h + (g + 1) % h] + [c * h + (g + h - r) % h for r in range(1, h)]
            return [jnp.where(home, a, b) for a, b in zip(at_home, at_other)]

        return part(self.home) + part(jnp.logical_not(self.home))

    def even_chunk(self):
        return jnp.where(self.worker % 2 == 0, self.worker, 2 * self.n - 1 - self.worker)


def write_grads(mine_ref, theirs_ref, here, value, col0):
    own = value.shape[0] // here.n_dp
    cols = value.shape[1] // here.n
    low = value.astype(bf16)
    first = here.core == 0
    for pair in range(here.n_dp // 2):
        m = pair ^ here.chip
        for j in range(here.n):
            s = (j + here.n - here.z) % here.n
            at = slice(j * cols, (j + 1) * cols)
            even = low[2 * pair * own : (2 * pair + 1) * own, at]
            odd = low[(2 * pair + 1) * own : (2 * pair + 2) * own, at]
            mine_ref[m, s, :own, col0 : col0 + cols] = jnp.where(first, even, odd)
            theirs_ref[m, s, :own, col0 : col0 + cols] = jnp.where(first, odd, even)


def attend_rows(q_ref, k_ref, v_ref, att_ref, lse_ref, row0, rows, parts, pair):
    cols = pair_slice(pair)
    q2 = q_ref[row0 : row0 + rows, cols]
    both = []
    lse_now = lse_ref[row0 : row0 + rows, :]
    lane = lax.broadcasted_iota(jnp.int32, (rows, PAIR), 1)
    for h in range(2):
        qm = one_head(q2, h)
        scores = []
        for start, size, mask in parts:
            s = nt(qm, k_ref[start : start + size, cols])
            if mask is not None:
                s = jnp.where(mask(rows, size), s, masked_out)
            scores.append(s)
        top = functools.reduce(
            jnp.maximum, [jnp.max(s, axis=-1, keepdims=True) for s in scores]
        )
        total = 0.0
        result = 0.0
        for s, (start, size, _) in zip(scores, parts):
            e = jnp.exp(s - top)
            total = total + jnp.sum(e, axis=-1, keepdims=True)
            result = result + nn(e.astype(bf16), v_ref[start : start + size, cols])
        both.append(result / total)
        lse_now = jnp.where(lane == pair * 2 + h, top + jnp.log(total), lse_now)
    lse_ref[row0 : row0 + rows, :] = lse_now
    att_ref[row0 : row0 + rows, cols] = jnp.where(
        lane_head(rows) == 0, both[0], both[1]
    ).astype(bf16)


def attend_rows_back(
    q_ref, k_ref, v_ref, att_ref, g_ref, lse_ref, qt_ref, gt_ref,
    dq_ref, dkt_ref, dvt_ref, row0, rows, parts, pair,
):
    cols = pair_slice(pair)
    q2 = q_ref[row0 : row0 + rows, cols]
    g2 = g_ref[row0 : row0 + rows, cols]
    prod = g2.astype(f32) * att_ref[row0 : row0 + rows, cols].astype(f32)
    lse_all = lse_ref[row0 : row0 + rows, :]
    lane = lax.broadcasted_iota(jnp.int32, (rows, PAIR), 1)
    both = []
    for h in range(2):
        head = pair * 2 + h
        hrows = pl.ds(pl.multiple_of(head * DH, DH), DH)
        qm = one_head(q2, h)
        gm = one_head(g2, h)
        qt = qt_ref[hrows, row0 : row0 + rows]
        gt = gt_ref[hrows, row0 : row0 + rows]
        lse = jnp.sum(jnp.where(lane == head, lse_all, 0.0), axis=-1, keepdims=True)
        delta = jnp.sum(jnp.where(lane // DH == h, prod, 0.0), axis=-1, keepdims=True)
        dq = 0.0
        for start, size, mask, adds in parts:
            k2 = k_ref[start : start + size, cols]
            v2 = v_ref[start : start + size, cols]
            p = jnp.exp(nt(qm, k2) - lse)
            if mask is not None:
                p = jnp.where(mask(rows, size), p, 0.0)
            ds = (p * (nt(gm, v2) - delta)).astype(bf16)
            dq = dq + nn(ds, k2)
            dk = nn(qt, ds)
            dv = nn(gt, p.astype(bf16))
            if adds:
                dk = dk + dkt_ref[hrows, start : start + size]
                dv = dv + dvt_ref[hrows, start : start + size]
            dkt_ref[hrows, start : start + size] = dk
            dvt_ref[hrows, start : start + size] = dv
        both.append(dq)
    dq_ref[row0 : row0 + rows, cols] = (
        jnp.where(lane_head(rows) == 0, both[0], both[1]).astype(bf16)
    )


def diagonal(rows, size):
    row = lax.broadcasted_iota(jnp.int32, (rows, size), 0)
    col = lax.broadcasted_iota(jnp.int32, (rows, size), 1)
    return col <= row


def causal_parts(chunk, size):
    parts = []
    if chunk:
        parts.append((0, chunk * size, None))
    parts.append((chunk * size, size, diagonal))
    return parts


def self_forward_kernel(*refs):
    here = Here()
    n = here.n
    halves, refs = refs[:2], refs[2:]
    w_ref, s_ref, q_ref, k_ref, v_ref, att_ref, lse_ref, x_ref, xq_ref, vec_ref = refs
    length, width = x_ref.shape
    rows = q_ref.shape[0]
    size = rows // 2
    vec_ref[...] = s_ref[...].astype(f32).T[: vec_ref.shape[0], :]
    for t, piece in enumerate(here.slots()):
        at = pl.ds(pl.multiple_of(piece * rows, rows), rows)
        block = halves[t // here.h][(t % here.h) * rows : (t % here.h + 1) * rows, :]
        x_ref[at, :] = block
        kv = nn(block, w_ref[:, width : 3 * width])
        k_ref[at, :] = kv[:, :width].astype(bf16)
        v_ref[at, :] = (kv[:, width:] + vec_ref[1:2, :]).astype(bf16)
    even = here.even_chunk()
    for block in range(2):
        chunk = even if block == 0 else 2 * n - 1 - even
        xb = x_ref[pl.ds(pl.multiple_of(chunk * size, size), size), :]
        own_rows = slice(block * size, (block + 1) * size)
        xq_ref[own_rows, :] = xb
        q_ref[own_rows, :] = ((nn(xb, w_ref[:, :width]) + vec_ref[0:1, :]) * SCALE).astype(bf16)
    lse_ref[...] = jnp.zeros_like(lse_ref)

    for which in range(n):

        @pl.when(here.worker == which)
        def _(which=which):
            def pairs(pair, carry):
                for block in range(2):
                    chunk = chunk_of(which, block, n)
                    attend_rows(
                        q_ref, k_ref, v_ref, att_ref, lse_ref, block * size, size,
                        causal_parts(chunk, size), pair,
                    )
                return carry

            lax.fori_loop(0, H // 2, pairs, 0)


def cross_query_kernel(att_ref, xq_ref, wso_ref, wcq_ref, vec_ref, res_ref, cq_ref):
    res_ref[...] = xq_ref[...].astype(f32) + nn(att_ref[...], wso_ref[...]) + vec_ref[2:3, :]
    normed, _ = norm_stats(res_ref[...])
    hidden = (normed * vec_ref[10:11, :] + vec_ref[7:8, :]).astype(bf16)
    cq_ref[...] = ((nn(hidden, wcq_ref[...]) + vec_ref[3:4, :]) * SCALE).astype(bf16)


def length_limit(here, vec_ref):
    packed = vec_ref[17:18, :] * 64.0 + vec_ref[18:19, :]
    lane = lax.broadcasted_iota(jnp.int32, packed.shape, 1)
    picked = jnp.where(lane == here.seq * (packed.shape[1] // here.n_dp), packed, 0.0)
    return jnp.sum(picked, axis=-1, keepdims=True).astype(jnp.int32)


def cross_forward_kernel(*refs):
    here = Here()
    n = here.n
    halves, refs = refs[:2], refs[2:]
    cq_ref, wckv_ref, vec_ref, ek_ref, ev_ref, catt_ref, clse_ref, enc_ref = refs
    length, width = enc_ref.shape
    rows = cq_ref.shape[0]
    size = rows // 2
    for t, piece in enumerate(here.slots()):
        at = pl.ds(pl.multiple_of(piece * rows, rows), rows)
        block = halves[t // here.h][(t % here.h) * rows : (t % here.h + 1) * rows, :]
        enc_ref[at, :] = block
        kv = nn(block, wckv_ref[...])
        ek_ref[at, :] = kv[:, :width].astype(bf16)
        ev_ref[at, :] = (kv[:, width:] + vec_ref[4:5, :]).astype(bf16)
    clse_ref[...] = jnp.zeros_like(clse_ref)
    limit = length_limit(here, vec_ref)

    def visible(count, keys):
        return lax.broadcasted_iota(jnp.int32, (count, keys), 1) < limit

    def pairs(pair, carry):
        for block in range(2):
            attend_rows(
                cq_ref, ek_ref, ev_ref, catt_ref, clse_ref, block * size, size,
                [(0, length, visible)], pair,
            )
        return carry

    lax.fori_loop(0, H // 2, pairs, 0)


def feed_forward_kernel(
    res1_ref, catt_ref, wco_ref, wup_ref, wdn_ref, vec_ref, cot0_ref, cot1_ref,
    out0_ref, out1_ref, gtwo_ref, cgrad_ref, mine_ref, theirs_ref, small_ref,
    up_scr, act_scr, upl_scr,
):
    here = Here()
    rows, width = res1_ref.shape
    size = rows // 2
    hidden_units = wup_ref.shape[1]
    step = width
    blocks = hidden_units // step
    own = width // here.n_dp
    groups = hidden_units // width
    normed, _ = norm_stats(res1_ref[...])
    hidden_one = normed * vec_ref[10:11, :] + vec_ref[7:8, :]
    res2 = hidden_one + nn(catt_ref[...], wco_ref[...]) + vec_ref[5:6, :]
    normed2, inv2 = norm_stats(res2)
    hidden_two = normed2 * vec_ref[11:12, :] + vec_ref[8:9, :]
    h2_low = hidden_two.astype(bf16)
    down = jnp.zeros((rows, width), f32)
    for b in range(blocks):
        cols = slice(b * step, (b + 1) * step)
        shift = jnp.concatenate(
            [
                vec_ref[13 + q : 14 + q, i * own : (i + 1) * own]
                for i in range(b * here.n_dp // blocks, (b + 1) * here.n_dp // blocks)
                for q in range(groups)
            ],
            axis=1,
        )
        up = nn(h2_low, wup_ref[:, cols]) + shift
        up_scr[:, cols] = up
        act = (up * jax.nn.sigmoid(up)).astype(bf16)
        act_scr[:, cols] = act
        down = down + nn(act, wdn_ref[cols, :])
    res3 = hidden_two + down + vec_ref[6:7, :]
    normed3, inv3 = norm_stats(res3)
    result = (normed3 * vec_ref[12:13, :] + vec_ref[9:10, :]).astype(bf16)
    out0_ref[...] = result[:size]
    out1_ref[...] = result[size:]
    upstream = jnp.concatenate([cot0_ref[...], cot1_ref[...]], axis=0).astype(f32)
    small_ref[...] = jnp.zeros_like(small_ref)
    small_ref[12:13, :] = col_sum(upstream * normed3)
    small_ref[9:10, :] = col_sum(upstream)
    grad_three = norm_backward(upstream, normed3, inv3, vec_ref[12:13, :])
    small_ref[6:7, :] = col_sum(grad_three)
    down_low = grad_three.astype(bf16)
    h2_t = h2_low.T
    grad_h2 = grad_three
    piece = width // here.n
    up_piece = hidden_units // here.n
    part_rows = hidden_units // here.n_dp
    first = here.core == 0
    for b in range(blocks):
        cols = slice(b * step, (b + 1) * step)
        gdown = tn(act_scr[:, cols], down_low).astype(bf16)
        for pair in range(here.n_dp // 2 // blocks):
            m = (b * (here.n_dp // 2 // blocks) + pair) ^ here.chip
            for j in range(here.n):
                s = (j + here.n - here.z) % here.n
                for g in range(groups):
                    at = 2 * pair * part_rows + g * own
                    lanes = slice(j * piece, (j + 1) * piece)
                    even = gdown[at : at + own, lanes]
                    odd = gdown[at + part_rows : at + part_rows + own, lanes]
                    base = piece + up_piece + g * piece
                    mine_ref[m, s, :, base : base + piece] = jnp.where(first, even, odd)
                    theirs_ref[m, s, :, base : base + piece] = jnp.where(first, odd, even)
        up = up_scr[:, cols]
        sig = jax.nn.sigmoid(up)
        up_low = (
            nt(down_low, wdn_ref[cols, :]) * sig * (1.0 + up * (1.0 - sig))
        ).astype(bf16)
        upl_scr[:, cols] = up_low
        small_ref[16 + b : 17 + b, :] = col_sum(up_low.astype(f32))
        grad_h2 = grad_h2 + nt(up_low, wup_ref[:, cols])
    write_grads(mine_ref, theirs_ref, here, nn(h2_t, upl_scr[...]), piece)
    small_ref[11:12, :] = col_sum(grad_h2 * normed2)
    small_ref[8:9, :] = col_sum(grad_h2)
    grad_two = norm_backward(grad_h2, normed2, inv2, vec_ref[11:12, :])
    small_ref[5:6, :] = col_sum(grad_two)
    gtwo_ref[...] = grad_two
    two_low = grad_two.astype(bf16)
    write_grads(mine_ref, theirs_ref, here, tn(catt_ref[...], two_low), 0)
    cgrad_ref[...] = nt(two_low, wco_ref[...]).astype(bf16)


def ones_sum(t_ref):
    return nt(jnp.ones((8, t_ref.shape[1]), bf16), t_ref[...])[0:1, :]


def cross_backward_pairs(here, q_ref, k_ref, v_ref, att_ref, g_ref, lse_ref, vec_ref, scratch, first, last):
    qt_scr, gt_scr, dq_scr, dkt_scr, dvt_scr = scratch
    length = k_ref.shape[0]
    size = q_ref.shape[0] // 2
    qt_scr[...] = q_ref[...].T
    gt_scr[...] = g_ref[...].T
    half = length // 2
    limit = length_limit(here, vec_ref)

    def pairs(pair, carry):
        for block in range(2):
            parts = []
            for part in range(2):
                start = part * half

                def visible(count, keys, start=start):
                    return lax.broadcasted_iota(jnp.int32, (count, keys), 1) + start < limit

                parts.append((start, half, visible, block == 1))
            attend_rows_back(
                q_ref, k_ref, v_ref, att_ref, g_ref, lse_ref, qt_scr, gt_scr,
                dq_scr, dkt_scr, dvt_scr, block * size, size, parts, pair,
            )
        return carry

    lax.fori_loop(first, last, pairs, 0)


def cross_backward_kernel(
    first, last, cq_ref, ek_ref, ev_ref, catt_ref, cgrad_ref, clse_ref, vec_ref,
    dq_ref, low_ref, *scratch,
):
    cross_backward_pairs(
        Here(), cq_ref, ek_ref, ev_ref, catt_ref, cgrad_ref, clse_ref, vec_ref, scratch, first, last
    )
    _, _, dq_scr, dkt_scr, dvt_scr = scratch
    done = last * PAIR
    dq_ref[:, :done] = dq_scr[:, :done]
    low_ref[:done, :] = dkt_scr[:done, :].astype(bf16)
    low_ref[done:, :] = dvt_scr[:done, :].astype(bf16)


def cross_backward_rest_kernel(
    cq_ref, ek_ref, ev_ref, catt_ref, cgrad_ref, clse_ref, vec_ref, dq_in_ref, low_in_ref, enc_ref, wckv_ref,
    mine_ref, theirs_ref, qgrad_ref, gw_ref, evsum_ref, *scratch,
):
    here = Here()
    low_scr = scratch[-1]
    length, width = enc_ref.shape
    rows = cq_ref.shape[0]
    done = width // 2
    cross_backward_pairs(
        here, cq_ref, ek_ref, ev_ref, catt_ref, cgrad_ref, clse_ref, vec_ref, scratch[:-1], H // 4, H // 2
    )
    _, _, dq_scr, dkt_scr, dvt_scr = scratch[:-1]
    dq_scr[:, :done] = dq_in_ref[:, :done]
    low_scr[:done, :] = low_in_ref[:done, :]
    low_scr[done:width, :] = dkt_scr[done:, :].astype(bf16)
    low_scr[width : width + done, :] = low_in_ref[done:, :]
    low_scr[width + done :, :] = dvt_scr[done:, :].astype(bf16)
    for t, piece in enumerate(here.slots()):
        at = pl.ds(pl.multiple_of(piece * rows, rows), rows)
        out_ref, slot = (mine_ref, t) if t < here.h else (theirs_ref, t - here.h)
        out_ref[slot * rows : (slot + 1) * rows, :] = (
            nn(wckv_ref[...], low_scr[:, at]).T.astype(bf16)
        )
    qgrad_ref[...] = (dq_scr[...].astype(f32) * SCALE).astype(bf16)
    evsum_ref[...] = jnp.zeros_like(evsum_ref)
    evsum_ref[0:1, :] = ones_sum(low_scr.at[width:, :])
    gw_ref[...] = nn(low_scr[...], enc_ref[...]).T.astype(bf16)


def norm_one_backward_kernel(
    qgrad_ref, wcq_ref, wso_ref, vec_ref, res1_ref, att_ref, gtwo_ref, small_in_ref, evsum_ref,
    gone_ref, sgrad_ref, gcq_ref, gso_ref, small_ref,
):
    small_ref[...] = small_in_ref[...]
    small_ref[3:4, :] = col_sum(qgrad_ref[...].astype(f32))
    small_ref[4:5, :] = evsum_ref[0:1, :]
    normed, inv = norm_stats(res1_ref[...])
    grad_h1 = gtwo_ref[...] + nt(qgrad_ref[...], wcq_ref[...])
    small_ref[10:11, :] = col_sum(grad_h1 * normed)
    small_ref[7:8, :] = col_sum(grad_h1)
    grad_one = norm_backward(grad_h1, normed, inv, vec_ref[10:11, :])
    small_ref[2:3, :] = col_sum(grad_one)
    gone_ref[...] = grad_one
    one_low = grad_one.astype(bf16)
    sgrad_ref[...] = nt(one_low, wso_ref[...]).astype(bf16)
    hidden = (normed * vec_ref[10:11, :] + vec_ref[7:8, :]).astype(bf16)
    gcq_ref[...] = tn(hidden, qgrad_ref[...]).astype(bf16)
    gso_ref[...] = tn(att_ref[...], one_low).astype(bf16)


def self_backward_kernel(
    q_ref, k_ref, v_ref, att_ref, sgrad_ref, lse_ref, x_ref, w_ref, gone_ref,
    small_in_ref, gckv_ref, gcq_ref, gso_ref,
    mine_ref, theirs_ref, gmine_ref, gtheirs_ref,
    qt_scr, gt_scr, dq_scr, dkt_scr, dvt_scr, low_scr, gin_scr, small_scr, small_t_scr,
):
    here = Here()
    n = here.n
    length, width = x_ref.shape
    rows = q_ref.shape[0]
    size = rows // 2
    qt_scr[...] = q_ref[...].T
    gt_scr[...] = sgrad_ref[...].T
    for which in range(n):

        @pl.when(here.worker == which)
        def _(which=which):
            order = sorted(range(2), key=lambda block: -chunk_of(which, block, n))
            top = chunk_of(which, order[0], n)
            if top + 1 < 2 * n:
                rest = (2 * n - 1 - top) * size
                dkt_scr[:, (top + 1) * size :] = jnp.zeros((width, rest), f32)
                dvt_scr[:, (top + 1) * size :] = jnp.zeros((width, rest), f32)

            def pairs(pair, carry):
                for order_place, block in enumerate(order):
                    chunk = chunk_of(which, block, n)
                    parts = []
                    for start, count, mask in causal_parts(chunk, size):
                        while count > 4 * size:
                            parts.append((start, 4 * size, mask, order_place == 1))
                            start, count = start + 4 * size, count - 4 * size
                        parts.append((start, count, mask, order_place == 1))
                    attend_rows_back(
                        q_ref, k_ref, v_ref, att_ref, sgrad_ref, lse_ref, qt_scr, gt_scr,
                        dq_scr, dkt_scr, dvt_scr, block * size, size, parts, pair,
                    )
                return carry

            lax.fori_loop(0, H // 2, pairs, 0)

    low_scr[:width, :] = dkt_scr[...].astype(bf16)
    low_scr[width:, :] = dvt_scr[...].astype(bf16)
    q_grad = (dq_scr[...].astype(f32) * SCALE).astype(bf16)
    small_scr[...] = jnp.zeros_like(small_scr)
    small_scr[: small_in_ref.shape[0], :] = small_in_ref[...]
    small_scr[0:1, :] = col_sum(q_grad.astype(f32))
    small_scr[1:2, :] = ones_sum(low_scr.at[width:, :])
    for t in range(n):
        at = slice(t * rows, (t + 1) * rows)
        gin_scr[at, :] = nn(w_ref[:, width:], low_scr[:, at]).T
    even = here.even_chunk()
    wq_grad = jnp.zeros((width, width), f32)
    for block in range(2):
        chunk = even if block == 0 else 2 * n - 1 - even
        at = pl.ds(pl.multiple_of(chunk * size, size), size)
        own_rows = slice(block * size, (block + 1) * size)
        wq_grad = wq_grad + tn(x_ref[at, :], q_grad[own_rows])
        gin_scr[at, :] += gone_ref[own_rows, :] + nt(q_grad[own_rows], w_ref[:, :width])
    for t, piece in enumerate(here.slots()):
        at = pl.ds(pl.multiple_of(piece * rows, rows), rows)
        out_ref, slot = (mine_ref, t) if t < here.h else (theirs_ref, t - here.h)
        out_ref[slot * rows : (slot + 1) * rows, :] = gin_scr[at, :].astype(bf16)
    kv_grad = nn(low_scr[...], x_ref[...]).T.astype(bf16)
    piece = width // n
    own = width // here.n_dp
    grads = jnp.concatenate([wq_grad.astype(bf16), kv_grad], axis=1)
    write_grads(gmine_ref, gtheirs_ref, here, grads, 0)
    write_grads(gmine_ref, gtheirs_ref, here, gcq_ref[...], 3 * piece)
    write_grads(gmine_ref, gtheirs_ref, here, gckv_ref[...], 4 * piece)
    write_grads(gmine_ref, gtheirs_ref, here, gso_ref[...], 6 * piece)
    small_t_scr[width:, :] = jnp.zeros((TINY, PAIR), f32)
    small_t_scr[:width, :] = small_scr[...].T
    cells = own // n
    groups = GROUPS
    first = here.core == 0
    cols = gmine_ref.shape[3]

    def tiny(i, j):
        blocks = [small_t_scr[i * own + j * cells : i * own + j * cells + TINY, :]]
        up0 = (i * groups * own + j * groups * cells) % width
        for q in range(groups):
            blocks.append(small_t_scr[up0 + q * cells : up0 + q * cells + TINY, :])
        return jnp.concatenate(blocks, axis=1).astype(bf16)

    for pair in range(here.n_dp // 2):
        m = pair ^ here.chip
        for j in range(n):
            s = (j + n - here.z) % n
            even_block, odd_block = tiny(2 * pair, j), tiny(2 * pair + 1, j)
            used = even_block.shape[1]
            gmine_ref[m, s, own:, :used] = jnp.where(first, even_block, odd_block)
            gtheirs_ref[m, s, own:, :used] = jnp.where(first, odd_block, even_block)
            if used < cols:
                gmine_ref[m, s, own:, used:] = jnp.zeros((TINY, cols - used), bf16)
                gtheirs_ref[m, s, own:, used:] = jnp.zeros((TINY, cols - used), bf16)


def finish_kernel(*refs):
    here = Here()
    n = here.n
    one_refs, refs = refs[:n], refs[n:]
    two_refs, refs = refs[:n], refs[n:]
    self_ref, so_ref, cq_ref, kv_ref, co_ref, up_ref, dn_ref, bias_ref, gain_ref, upb_ref, square_scr = refs
    own, piece = so_ref.shape
    groups = upb_ref.shape[0]
    cells = bias_ref.shape[1]
    one = functools.reduce(jnp.add, [ref[...].astype(f32) for ref in one_refs])
    two = functools.reduce(jnp.add, [ref[...].astype(f32) for ref in two_refs])
    up_piece = up_ref.shape[1]
    co_ref[...] = one[:, :piece]
    up_ref[...] = one[:, piece : piece + up_piece]
    for g in range(groups):
        base = piece + up_piece + g * piece
        dn_ref[g * own : (g + 1) * own, :] = one[:, base : base + piece]
    main = two[:own]
    self_ref[...] = main[:, : 3 * piece]
    cq_ref[...] = main[:, 3 * piece : 4 * piece]
    kv_ref[...] = main[:, 4 * piece : 6 * piece]
    so_ref[...] = main[:, 6 * piece : 7 * piece]
    small = two[own:, :PAIR]
    lane = lax.broadcasted_iota(jnp.int32, small.shape, 1)
    column = 16 + (here.dp * groups * own + here.z * groups * cells) // (own * here.n_dp)
    for q in range(groups):
        block = two[own:, (1 + q) * PAIR : (2 + q) * PAIR]
        value = jnp.sum(jnp.where(lane == column, block, 0.0), axis=-1, keepdims=True)
        small = jnp.where(lane == 24 + q, value, small)
    square_scr[...] = jnp.zeros_like(square_scr)
    square_scr[: small.shape[0], :] = small
    turned = square_scr[...].T
    bias_ref[...] = turned[0:10, :cells]
    gain_ref[...] = turned[10:13, :cells]
    upb_ref[...] = turned[24 : 24 + groups, :cells]


TINY = 16
GROUPS = 4


class Gathered:
    def __init__(self, blocks, partner, start, cols, groups=1):
        self.blocks, self.partner, self.start, self.cols, self.groups = blocks, partner, start, cols, groups
        self.own = blocks[0].shape[0]
        self.rows = 2 * len(blocks) * self.own * groups

    def arrays(self):
        return [*self.blocks, self.partner]

    def started(self, refs, held_ref, here, sems):
        own = self.own
        chips = len(self.blocks)
        copies = []
        for m in range(chips):
            for side in range(2):
                place = 2 * (here.chip ^ m) + (here.core ^ side)
                source = refs[m] if side == 0 else refs[chips].at[m * own : (m + 1) * own, :]
                for g in range(self.groups):
                    row = pl.multiple_of((place * self.groups + g) * own, own)
                    start = self.start + g * self.cols
                    copies.append(
                        pltpu.make_async_copy(
                            source.at[:, start : start + self.cols],
                            held_ref.at[pl.ds(row, own), :],
                            sems[len(copies)],
                        )
                    )
                    copies[-1].start()
        return copies


def run_kernel(kernel, outs, args, scratch=()):
    name = getattr(kernel, "func", kernel).__name__
    whole = pl.BlockSpec(memory_space=pltpu.VMEM)
    plain = [arg for arg in args if not isinstance(arg, Gathered)]
    parts = [arg for arg in args if isinstance(arg, Gathered)]
    sources = []
    for part in parts:
        for array in part.arrays():
            if not any(array is source for source in sources):
                sources.append(array)
    where = [
        [[i for i, source in enumerate(sources) if source is array][0] for array in part.arrays()]
        for part in parts
    ]
    specs = [whole] * len(plain) + [pl.BlockSpec(memory_space=pl.ANY)] * len(sources)
    held = [pltpu.VMEM((part.rows, part.cols), bf16) for part in parts]
    counts = [2 * len(part.blocks) * part.groups for part in parts]
    extra = held + ([pltpu.SemaphoreType.DMA((sum(counts),))] if parts else [])

    def body(*refs):
        plain_refs, refs = refs[: len(plain)], refs[len(plain) :]
        source_refs, refs = refs[: len(sources)], refs[len(sources) :]
        extra_refs, refs = refs[len(refs) - len(extra) :], refs[: len(refs) - len(extra)]
        copies = []
        if parts:
            here = Here()
            for part, places, held_ref, count in zip(parts, where, extra_refs, counts):
                part_refs = [source_refs[i] for i in places]
                sems = [extra_refs[-1].at[len(copies) + i] for i in range(count)]
                copies += part.started(part_refs, held_ref, here, sems)
        for copy in copies:
            copy.wait()
        left, held_refs, in_refs = list(plain_refs), list(extra_refs), []
        for arg in args:
            in_refs.append(held_refs.pop(0) if isinstance(arg, Gathered) else left.pop(0))
        kernel(*in_refs, *refs)

    return pl.pallas_call(
        body,
        out_shape=tuple(jax.ShapeDtypeStruct(shape, kind) for shape, kind in outs),
        in_specs=specs,
        out_specs=tuple(whole for _ in outs),
        scratch_shapes=list(scratch) + extra,
        compiler_params=pltpu.CompilerParams(vmem_limit_bytes=VMEM[name] * 2**20),
        cost_estimate=pl.CostEstimate(flops=1, bytes_accessed=1, transcendentals=0),
    )(*plain, *sources)


def pack_kernel(
    lens_ref, self_ref, kv_ref, so_ref, cq_ref, up_ref, co_ref, dn_ref, bias_ref, gain_ref, upb_ref,
    one_ref, three_ref, rows_scr,
):
    own = self_ref.shape[0]
    groups = upb_ref.shape[0]
    at = self_ref.shape[1]
    one_ref[:, :at] = self_ref[...]
    start = at + PAIR
    for ref in (kv_ref, so_ref, cq_ref):
        one_ref[:, start : start + ref.shape[1]] = ref[...]
        start += ref.shape[1]
    start = 0
    for ref in [up_ref, co_ref] + [dn_ref.at[g * own : (g + 1) * own, :] for g in range(groups)]:
        three_ref[:, start : start + ref.shape[1]] = ref[...]
        start += ref.shape[1]
    rows_scr[...] = jnp.zeros_like(rows_scr)
    rows_scr[0:10, :own] = bias_ref[...].astype(f32)
    rows_scr[10:13, :own] = gain_ref[...].astype(f32)
    rows_scr[13 : 13 + groups, :own] = upb_ref[...].astype(f32)
    length = lens_ref[0]
    rows_scr[17:18, :own] = jnp.full((1, own), length // 64, jnp.int32).astype(f32)
    rows_scr[18:19, :own] = jnp.full((1, own), length % 64, jnp.int32).astype(f32)
    one_ref[:, at : at + PAIR] = rows_scr[...].T[:own, :].astype(bf16)


def pack_weights(
    w_self, w_cross_kv, w_self_out, w_cross_q, w_up, w_cross_out, w_down, biases, gains, up_bias, lens, wide1, wide3
):
    own = w_self.shape[0]
    whole = pl.BlockSpec(memory_space=pltpu.VMEM)
    return pl.pallas_call(
        pack_kernel,
        out_shape=(jax.ShapeDtypeStruct((own, wide1), bf16), jax.ShapeDtypeStruct((own, wide3), bf16)),
        in_specs=[pl.BlockSpec(memory_space=pltpu.SMEM)] + [whole] * 10,
        out_specs=(whole, whole),
        scratch_shapes=[pltpu.VMEM((PAIR, PAIR), f32)],
        compiler_params=pltpu.CompilerParams(vmem_limit_bytes=VMEM["pack_kernel"] * 2**20),
        cost_estimate=pl.CostEstimate(flops=1, bytes_accessed=1, transcendentals=0),
    )(lens, w_self, w_cross_kv, w_self_out, w_cross_q, w_up, w_cross_out, w_down, biases, gains, up_bias)


class Routes:
    def __init__(self, n, n_dp):
        self.n, self.h = n, n // 2
        self.chips = n_dp // 2

    def all_chips(self, pairs):
        return [
            ((2 * k + c0) * self.n + z0, (2 * k + c1) * self.n + z1)
            for k in range(self.chips)
            for (c0, z0), (c1, z1) in pairs
        ]

    def gather(self, r):
        h = self.h
        pairs = []
        for c in range(2):
            for i in range(h):
                far = (c, (1 - c) * h + i)
                if r < h:
                    pairs.append(((c, c * h + i), (1 - c, c * h + (i + r) % h)))
                    pairs.append((far, (c, c * h + (i + r - 1) % h)))
                else:
                    pairs.append((far, (1 - c, c * h + (i + h - 1) % h)))
        return self.all_chips(pairs)

    def rows(self, odd):
        n, h = self.n, self.h
        pairs = []
        for c in range(2):
            for z in range(n):
                chunk = 2 * z + odd
                w = chunk if chunk < n else 2 * n - 1 - chunk
                pairs.append(((c, z), (w % 2, c * h + w // 2)))
        return self.all_chips(pairs)


def back(pairs):
    return [(b, a) for a, b in pairs]


BOTH = ("dp", "sp")


def after(first, then):
    return lax.optimization_barrier((first, then))[1]


def on_device(
    inputs, encoder, cotangent, w_self, w_self_out, w_cross_q, w_cross_kv, w_cross_out, w_up, w_down,
    biases, norm_gains, up_bias, source_lengths,
):
    here = Here()
    n, n_dp, h = here.n, here.n_dp, here.h
    chips = n_dp // 2
    _, rows, width = inputs.shape
    size = rows // 2
    length = n * rows
    hidden_units = w_up.shape[1]
    own = w_self.shape[0]
    piece = width // n
    up_piece = hidden_units // n
    cells = own // n
    groups = up_bias.shape[0] // own
    routes = Routes(n, n_dp)

    def swap(value):
        return lax.ppermute(value, "dp", [(i, i ^ 1) for i in range(n_dp)])

    def to_chip(value, m):
        return lax.ppermute(value, "dp", [(i, i ^ (2 * m)) for i in range(n_dp)])

    def shift(value, s):
        return lax.ppermute(value, "sp", [(i, (i + s) % n) for i in range(n)])

    def gather(value):
        return [lax.ppermute(value, BOTH, routes.gather(r)) for r in range(1, h + 1)]

    def together(value, arrived):
        return jnp.concatenate([jnp.where(here.home, value, arrived[-1])] + arrived[:-1], axis=0)

    def chip_blocks(value):
        return [value] + [to_chip(value, m) for m in range(1, chips)]

    def swap_blocks(blocks):
        return swap(jnp.concatenate(blocks, axis=0))

    wide1 = 3 * width + PAIR + 4 * width
    wide3 = hidden_units + width + groups * width
    pack1, pack3 = pack_weights(
        w_self, w_cross_kv, w_self_out, w_cross_q, w_up, w_cross_out, w_down,
        biases, norm_gains, up_bias.reshape(groups, own), source_lengths.astype(jnp.int32), wide1, wide3,
    )
    x_arrived = gather(inputs[0])
    own1 = chip_blocks(pack1)
    x_arrived, own1, pack3, enc_own = lax.optimization_barrier((x_arrived, own1, pack3, encoder[0]))
    x_mine = together(inputs[0], x_arrived)
    partner1 = swap_blocks(own1)
    x_theirs = swap(x_mine)
    enc_arrived = gather(enc_own)
    own3 = chip_blocks(pack3)

    q, k, v, att, lse, x_full, xq, vec = run_kernel(
        self_forward_kernel,
        [((rows, width), bf16), ((length, width), bf16), ((length, width), bf16),
         ((rows, width), bf16), ((rows, PAIR), f32), ((length, width), bf16), ((rows, width), bf16),
         ((32, width), f32)],
        (x_mine, x_theirs, Gathered(own1, partner1, 0, 3 * width), Gathered(own1, partner1, 3 * width, PAIR)),
    )
    at2 = 3 * width + PAIR
    wckv = Gathered(own1, partner1, at2, 2 * width)
    wso = Gathered(own1, partner1, at2 + 2 * width, width)
    wcq = Gathered(own1, partner1, at2 + 3 * width, width)
    enc_arrived, own3, att = lax.optimization_barrier((enc_arrived, own3, att))
    enc_mine = together(enc_own, enc_arrived)
    enc_theirs = swap(enc_mine)
    res1, cq = run_kernel(
        cross_query_kernel,
        [((rows, width), f32), ((rows, width), bf16)],
        (att, xq, wso, wcq, vec),
    )
    partner3 = swap_blocks(own3)
    late_cot = after(enc_mine, cotangent[0])
    cot0 = lax.ppermute(late_cot[:size], BOTH, routes.rows(0))
    cot1 = lax.ppermute(late_cot[size:], BOTH, routes.rows(1))
    ek, ev, catt, clse, enc_full = run_kernel(
        cross_forward_kernel,
        [((length, width), bf16), ((length, width), bf16), ((rows, width), bf16), ((rows, PAIR), f32),
         ((length, width), bf16)],
        (enc_mine, enc_theirs, cq, wckv, vec),
    )
    wup = Gathered(own3, partner3, 0, hidden_units)
    wco = Gathered(own3, partner3, hidden_units, width)
    wdn = Gathered(own3, partner3, hidden_units + width, width, groups)
    block1 = (chips, n, own, piece + up_piece + groups * piece)
    out0, out1, gtwo, cgrad, mine1, theirs1, small = run_kernel(
        feed_forward_kernel,
        [((size, width), bf16), ((size, width), bf16), ((rows, width), f32), ((rows, width), bf16),
         (block1, bf16), (block1, bf16), ((24, width), f32)],
        (res1, catt, wco, wup, wdn, vec, cot0, cot1),
        scratch=[pltpu.VMEM((rows, hidden_units), f32), pltpu.VMEM((rows, hidden_units), bf16),
                 pltpu.VMEM((rows, hidden_units), bf16)],
    )

    def add(a, b):
        return (a.astype(f32) + b.astype(f32)).astype(bf16)

    def between_chips(mine, arrived):
        sums = [add(mine[m], arrived[m]) for m in range(chips)]
        return sums[0], [to_chip(sums[m], m) for m in range(1, chips)]

    def between_places(first, parts):
        total = first.astype(f32)
        for part in parts:
            total = total + part.astype(f32)
        low = total.astype(bf16)
        return low[0], [shift(low[s], s) for s in range(1, n)]

    def finish(first, parts):
        total = first.astype(f32)
        for part in parts:
            total = total + part.astype(f32)
        return total

    def pieces_home(mine, arrived):
        sums = [add(mine[t * rows : (t + 1) * rows], arrived[t * rows : (t + 1) * rows]) for t in range(h)]
        parts = [lax.ppermute(sums[r], BOTH, back(routes.gather(r))) for r in range(1, h)]
        last = lax.ppermute(sums[0], BOTH, back(routes.gather(h)))
        return jnp.where(here.home, sums[0], last), parts

    half_low = (width, length)
    back_scratch = [
        pltpu.VMEM((width, rows), bf16), pltpu.VMEM((width, rows), bf16), pltpu.VMEM((rows, width), bf16),
        pltpu.VMEM((width, length), f32), pltpu.VMEM((width, length), f32),
    ]
    low_scratch = [pltpu.VMEM((2 * width, length), bf16)]
    arrived1 = swap(theirs1)
    out_parts = (
        lax.ppermute(out0, BOTH, back(routes.rows(0))), lax.ppermute(out1, BOTH, back(routes.rows(1)))
    )
    dq_a, low_a = run_kernel(
        functools.partial(cross_backward_kernel, 0, H // 4),
        [((rows, width), bf16), (half_low, bf16)],
        (cq, ek, ev, catt, cgrad, clse, vec), scratch=back_scratch,
    )
    mine1, arrived1, out_parts, low_a = lax.optimization_barrier((mine1, arrived1, out_parts, low_a))
    chips1 = between_chips(mine1, arrived1)
    emine, etheirs, qgrad, gckv, evsum = run_kernel(
        cross_backward_rest_kernel,
        [((h * rows, width), bf16), ((h * rows, width), bf16), ((rows, width), bf16),
         ((width, 2 * width), bf16), ((8, width), f32)],
        (cq, ek, ev, catt, cgrad, clse, vec, dq_a, low_a, enc_full, wckv),
        scratch=back_scratch + low_scratch,
    )
    chips1, etheirs, qgrad = lax.optimization_barrier((chips1, etheirs, qgrad))
    output = jnp.concatenate(out_parts, axis=0)[None]
    earrived = swap(etheirs)
    gone, sgrad, gcq, gso, small = run_kernel(
        norm_one_backward_kernel,
        [((rows, width), f32), ((rows, width), bf16), ((width, width), bf16), ((width, width), bf16),
         ((24, width), f32)],
        (qgrad, wcq, wso, vec, res1, att, gtwo, small, evsum),
    )
    emine, earrived, sgrad = lax.optimization_barrier((emine, earrived, sgrad))
    enc_home = pieces_home(emine, earrived)
    places1 = between_places(*chips1)
    block2 = (chips, n, own + TINY, max(7 * piece, (1 + groups) * PAIR))
    gmine, gtheirs, mine2, theirs2 = run_kernel(
        self_backward_kernel,
        [((h * rows, width), bf16), ((h * rows, width), bf16), (block2, bf16), (block2, bf16)],
        (q, k, v, att, sgrad, lse, x_full, Gathered(own1, partner1, 0, 3 * width), gone, small,
         gckv, gcq, gso),
        scratch=back_scratch + low_scratch
        + [pltpu.VMEM((length, width), f32), pltpu.VMEM((PAIR, width), f32),
           pltpu.VMEM((width + TINY, PAIR), f32)],
    )
    enc_home, places1, gtheirs, theirs2 = lax.optimization_barrier((enc_home, places1, gtheirs, theirs2))
    garrived = swap(gtheirs)
    arrived2 = swap(theirs2)
    in_home = pieces_home(gmine, garrived)
    places2 = between_places(*between_chips(mine2, arrived2))
    g_self, g_so, g_cq, g_ckv, g_co, g_up, g_dn, g_bias, g_gain, g_upb = run_kernel(
        finish_kernel,
        [(shape, f32) for shape in (
            (own, 3 * piece), (own, piece), (own, piece), (own, 2 * piece), (own, piece), (own, up_piece),
            (groups * own, piece), (10, cells), (3, cells), (groups, cells),
        )],
        (places1[0], *places1[1], places2[0], *places2[1]),
        scratch=[pltpu.VMEM((PAIR, PAIR), f32)],
    )
    return (
        output,
        finish(*in_home)[None],
        finish(*enc_home)[None],
        g_self,
        g_so,
        g_cq,
        g_ckv,
        g_co,
        g_up,
        g_dn,
        g_bias,
        g_gain,
        g_upb.reshape(groups * cells),
    )


def solution(mesh):
    weight = P("dp", None)
    tokens = P("dp", "sp", None)
    return jax.shard_map(
        on_device,
        mesh=mesh,
        in_specs=(tokens,) * 3 + (weight,) * 7 + (P(None, "dp"), P(None, "dp"), P("dp"), P("dp")),
        out_specs=(tokens,) * 3
        + (P("dp", "sp"),) * 7
        + (P(None, ("dp", "sp")), P(None, ("dp", "sp")), P(("dp", "sp"))),
        check_vma=False,
    )
```

```python
import functools

import jax
import jax.numpy as jnp
from jax import lax
from jax.experimental import pallas as pl
from jax.experimental.pallas import tpu as pltpu
from jax.sharding import PartitionSpec as P

H = 8
DH = 64
PAIR = 128

eps_norm = 1e-05
masked_out = -1e30
bf16 = jnp.bfloat16
f32 = jnp.float32
SCALE = DH ** (-0.5)

VMEM = {
    "self_forward_kernel": 11,
    "cross_query_kernel": 10,
    "cross_forward_kernel": 12,
    "feed_forward_kernel": 26,
    "cross_backward_kernel": 16,
    "cross_backward_rest_kernel": 23,
    "norm_one_backward_kernel": 12,
    "self_backward_kernel": 28,
    "finish_kernel": 6,
    "pack_kernel": 60,
    "stack_kernel": 4,
    "together_kernel": 2,
}


def nn(left, right):
    return lax.dot_general(left, right, (((1,), (0,)), ((), ())), preferred_element_type=f32)


def nt(left, right):
    return lax.dot_general(left, right, (((1,), (1,)), ((), ())), preferred_element_type=f32)


def tn(left, right):
    return lax.dot_general(left, right, (((0,), (0,)), ((), ())), preferred_element_type=f32)


def norm_stats(resid):
    centred = resid - jnp.mean(resid, axis=-1, keepdims=True)
    inv_std = lax.rsqrt(jnp.mean(centred * centred, axis=-1, keepdims=True) + eps_norm)
    return centred * inv_std, inv_std


def norm_backward(upstream, normed, inv_std, gain):
    scaled = upstream * gain
    centre_term = jnp.mean(scaled, axis=-1, keepdims=True)
    slope_term = jnp.mean(scaled * normed, axis=-1, keepdims=True)
    return inv_std * (scaled - centre_term - normed * slope_term)


def col_sum(value):
    return jnp.sum(value, axis=0, keepdims=True)


def chunk_of(d, block, n):
    even = d if d % 2 == 0 else 2 * n - 1 - d
    return even if block == 0 else 2 * n - 1 - even


def lane_head(rows, cols=PAIR):
    return lax.broadcasted_iota(jnp.int32, (rows, cols), 1) // DH


def one_head(pair_value, head):
    return jnp.where(lane_head(*pair_value.shape) == head, pair_value, jnp.zeros_like(pair_value))


def pair_slice(pair):
    return pl.ds(pl.multiple_of(pair * PAIR, PAIR), PAIR)


class Here:
    def __init__(self):
        self.n, self.n_dp = lax.axis_size("sp"), lax.axis_size("dp")
        dp = lax.axis_index("dp").astype(jnp.int32)
        self.z = lax.axis_index("sp").astype(jnp.int32)
        self.h = self.n // 2
        self.chip, self.core = dp // 2, dp % 2
        self.dp = dp
        self.half = self.z // self.h
        self.local = self.z % self.h
        self.worker = 2 * self.local + self.core
        self.seq = 2 * self.chip + self.half
        self.home = self.core == self.half

    def slots(self):
        h, c, g = self.h, self.half, self.local

        def part(home):
            at_home = [self.z] + [(1 - c) * h + (g + h - (r - 1)) % h for r in range(1, h)]
            at_other = [(1 - c) * h + (g + 1) % h] + [c * h + (g + h - r) % h for r in range(1, h)]
            return [jnp.where(home, a, b) for a, b in zip(at_home, at_other)]

        return part(self.home) + part(jnp.logical_not(self.home))

    def even_chunk(self):
        return jnp.where(self.worker % 2 == 0, self.worker, 2 * self.n - 1 - self.worker)


def write_grads(mine_ref, theirs_ref, here, value, col0):
    own = value.shape[0] // here.n_dp
    cols = value.shape[1] // here.n
    low = value.astype(bf16)
    first = here.core == 0
    for pair in range(here.n_dp // 2):
        m = pair ^ here.chip
        for j in range(here.n):
            s = (j + here.n - here.z) % here.n
            at = slice(j * cols, (j + 1) * cols)
            even = low[2 * pair * own : (2 * pair + 1) * own, at]
            odd = low[(2 * pair + 1) * own : (2 * pair + 2) * own, at]
            mine_ref[m, s, :own, col0 : col0 + cols] = jnp.where(first, even, odd)
            theirs_ref[m, s, :own, col0 : col0 + cols] = jnp.where(first, odd, even)


def attend_rows(q_ref, k_ref, v_ref, att_ref, lse_ref, row0, rows, parts, pair):
    cols = pair_slice(pair)
    q2 = q_ref[row0 : row0 + rows, cols]
    both = []
    lse_now = lse_ref[row0 : row0 + rows, :]
    lane = lax.broadcasted_iota(jnp.int32, (rows, PAIR), 1)
    for h in range(2):
        qm = one_head(q2, h)
        scores = []
        for start, size, mask in parts:
            s = nt(qm, k_ref[start : start + size, cols])
            if mask is not None:
                s = jnp.where(mask(rows, size), s, masked_out)
            scores.append(s)
        top = functools.reduce(
            jnp.maximum, [jnp.max(s, axis=-1, keepdims=True) for s in scores]
        )
        total = 0.0
        result = 0.0
        for s, (start, size, _) in zip(scores, parts):
            e = jnp.exp(s - top)
            total = total + jnp.sum(e, axis=-1, keepdims=True)
            result = result + nn(e.astype(bf16), v_ref[start : start + size, cols])
        both.append(result / total)
        lse_now = jnp.where(lane == pair * 2 + h, top + jnp.log(total), lse_now)
    lse_ref[row0 : row0 + rows, :] = lse_now
    att_ref[row0 : row0 + rows, cols] = jnp.where(
        lane_head(rows) == 0, both[0], both[1]
    ).astype(bf16)


def attend_rows_back(
    q_ref, k_ref, v_ref, att_ref, g_ref, lse_ref, qt_ref, gt_ref,
    dq_ref, dkt_ref, dvt_ref, row0, rows, parts, pair,
):
    cols = pair_slice(pair)
    q2 = q_ref[row0 : row0 + rows, cols]
    g2 = g_ref[row0 : row0 + rows, cols]
    prod = g2.astype(f32) * att_ref[row0 : row0 + rows, cols].astype(f32)
    lse_all = lse_ref[row0 : row0 + rows, :]
    lane = lax.broadcasted_iota(jnp.int32, (rows, PAIR), 1)
    both = []
    for h in range(2):
        head = pair * 2 + h
        hrows = pl.ds(pl.multiple_of(head * DH, DH), DH)
        qm = one_head(q2, h)
        gm = one_head(g2, h)
        qt = qt_ref[hrows, row0 : row0 + rows]
        gt = gt_ref[hrows, row0 : row0 + rows]
        lse = jnp.sum(jnp.where(lane == head, lse_all, 0.0), axis=-1, keepdims=True)
        delta = jnp.sum(jnp.where(lane // DH == h, prod, 0.0), axis=-1, keepdims=True)
        dq = 0.0
        for start, size, mask, adds in parts:
            k2 = k_ref[start : start + size, cols]
            v2 = v_ref[start : start + size, cols]
            p = jnp.exp(nt(qm, k2) - lse)
            if mask is not None:
                p = jnp.where(mask(rows, size), p, 0.0)
            ds = (p * (nt(gm, v2) - delta)).astype(bf16)
            dq = dq + nn(ds, k2)
            dk = nn(qt, ds)
            dv = nn(gt, p.astype(bf16))
            if adds:
                dk = dk + dkt_ref[hrows, start : start + size]
                dv = dv + dvt_ref[hrows, start : start + size]
            dkt_ref[hrows, start : start + size] = dk
            dvt_ref[hrows, start : start + size] = dv
        both.append(dq)
    dq_ref[row0 : row0 + rows, cols] = (
        jnp.where(lane_head(rows) == 0, both[0], both[1]).astype(bf16)
    )


def diagonal(rows, size):
    row = lax.broadcasted_iota(jnp.int32, (rows, size), 0)
    col = lax.broadcasted_iota(jnp.int32, (rows, size), 1)
    return col <= row


def causal_parts(chunk, size):
    parts = []
    if chunk:
        parts.append((0, chunk * size, None))
    parts.append((chunk * size, size, diagonal))
    return parts


def self_forward_kernel(*refs):
    here = Here()
    n = here.n
    halves, refs = refs[:2], refs[2:]
    w_ref, s_ref, q_ref, k_ref, v_ref, att_ref, lse_ref, x_ref, xq_ref, vec_ref = refs
    length, width = x_ref.shape
    rows = q_ref.shape[0]
    size = rows // 2
    vec_ref[...] = s_ref[...].astype(f32).T[: vec_ref.shape[0], :]
    for t, piece in enumerate(here.slots()):
        at = pl.ds(pl.multiple_of(piece * rows, rows), rows)
        block = halves[t // here.h][(t % here.h) * rows : (t % here.h + 1) * rows, :]
        x_ref[at, :] = block
        kv = nn(block, w_ref[:, width : 3 * width])
        k_ref[at, :] = kv[:, :width].astype(bf16)
        v_ref[at, :] = (kv[:, width:] + vec_ref[1:2, :]).astype(bf16)
    even = here.even_chunk()
    for block in range(2):
        chunk = even if block == 0 else 2 * n - 1 - even
        xb = x_ref[pl.ds(pl.multiple_of(chunk * size, size), size), :]
        own_rows = slice(block * size, (block + 1) * size)
        xq_ref[own_rows, :] = xb
        q_ref[own_rows, :] = ((nn(xb, w_ref[:, :width]) + vec_ref[0:1, :]) * SCALE).astype(bf16)
    lse_ref[...] = jnp.zeros_like(lse_ref)

    for which in range(n):

        @pl.when(here.worker == which)
        def _(which=which):
            def pairs(pair, carry):
                for block in range(2):
                    chunk = chunk_of(which, block, n)
                    attend_rows(
                        q_ref, k_ref, v_ref, att_ref, lse_ref, block * size, size,
                        causal_parts(chunk, size), pair,
                    )
                return carry

            lax.fori_loop(0, H // 2, pairs, 0)


def cross_query_kernel(att_ref, xq_ref, wso_ref, wcq_ref, vec_ref, res_ref, cq_ref):
    res_ref[...] = xq_ref[...].astype(f32) + nn(att_ref[...], wso_ref[...]) + vec_ref[2:3, :]
    normed, _ = norm_stats(res_ref[...])
    hidden = (normed * vec_ref[10:11, :] + vec_ref[7:8, :]).astype(bf16)
    cq_ref[...] = ((nn(hidden, wcq_ref[...]) + vec_ref[3:4, :]) * SCALE).astype(bf16)


def length_limit(here, vec_ref):
    packed = vec_ref[17:18, :] * 64.0 + vec_ref[18:19, :]
    lane = lax.broadcasted_iota(jnp.int32, packed.shape, 1)
    picked = jnp.where(lane == here.seq * (packed.shape[1] // here.n_dp), packed, 0.0)
    return jnp.sum(picked, axis=-1, keepdims=True).astype(jnp.int32)


def cross_forward_kernel(*refs):
    here = Here()
    n = here.n
    halves, refs = refs[:2], refs[2:]
    cq_ref, wckv_ref, vec_ref, ek_ref, ev_ref, catt_ref, clse_ref, enc_ref = refs
    length, width = enc_ref.shape
    rows = cq_ref.shape[0]
    size = rows // 2
    for t, piece in enumerate(here.slots()):
        at = pl.ds(pl.multiple_of(piece * rows, rows), rows)
        block = halves[t // here.h][(t % here.h) * rows : (t % here.h + 1) * rows, :]
        enc_ref[at, :] = block
        kv = nn(block, wckv_ref[...])
        ek_ref[at, :] = kv[:, :width].astype(bf16)
        ev_ref[at, :] = (kv[:, width:] + vec_ref[4:5, :]).astype(bf16)
    clse_ref[...] = jnp.zeros_like(clse_ref)
    limit = length_limit(here, vec_ref)

    def visible(count, keys):
        return lax.broadcasted_iota(jnp.int32, (count, keys), 1) < limit

    def pairs(pair, carry):
        for block in range(2):
            attend_rows(
                cq_ref, ek_ref, ev_ref, catt_ref, clse_ref, block * size, size,
                [(0, length, visible)], pair,
            )
        return carry

    lax.fori_loop(0, H // 2, pairs, 0)


def feed_forward_kernel(
    res1_ref, catt_ref, wco_ref, wup_ref, wdn_ref, vec_ref, cot0_ref, cot1_ref,
    out0_ref, out1_ref, gtwo_ref, cgrad_ref, mine_ref, theirs_ref, small_ref,
    up_scr, act_scr, upl_scr,
):
    here = Here()
    rows, width = res1_ref.shape
    size = rows // 2
    hidden_units = wup_ref.shape[1]
    step = width
    blocks = hidden_units // step
    own = width // here.n_dp
    groups = hidden_units // width
    normed, _ = norm_stats(res1_ref[...])
    hidden_one = normed * vec_ref[10:11, :] + vec_ref[7:8, :]
    res2 = hidden_one + nn(catt_ref[...], wco_ref[...]) + vec_ref[5:6, :]
    normed2, inv2 = norm_stats(res2)
    hidden_two = normed2 * vec_ref[11:12, :] + vec_ref[8:9, :]
    h2_low = hidden_two.astype(bf16)
    down = jnp.zeros((rows, width), f32)
    for b in range(blocks):
        cols = slice(b * step, (b + 1) * step)
        shift = jnp.concatenate(
            [
                vec_ref[13 + q : 14 + q, i * own : (i + 1) * own]
                for i in range(b * here.n_dp // blocks, (b + 1) * here.n_dp // blocks)
                for q in range(groups)
            ],
            axis=1,
        )
        up = nn(h2_low, wup_ref[:, cols]) + shift
        up_scr[:, cols] = up
        act = (up * jax.nn.sigmoid(up)).astype(bf16)
        act_scr[:, cols] = act
        down = down + nn(act, wdn_ref[cols, :])
    res3 = hidden_two + down + vec_ref[6:7, :]
    normed3, inv3 = norm_stats(res3)
    result = (normed3 * vec_ref[12:13, :] + vec_ref[9:10, :]).astype(bf16)
    out0_ref[...] = result[:size]
    out1_ref[...] = result[size:]
    upstream = jnp.concatenate([cot0_ref[...], cot1_ref[...]], axis=0).astype(f32)
    small_ref[...] = jnp.zeros_like(small_ref)
    small_ref[12:13, :] = col_sum(upstream * normed3)
    small_ref[9:10, :] = col_sum(upstream)
    grad_three = norm_backward(upstream, normed3, inv3, vec_ref[12:13, :])
    small_ref[6:7, :] = col_sum(grad_three)
    down_low = grad_three.astype(bf16)
    h2_t = h2_low.T
    grad_h2 = grad_three
    piece = width // here.n
    up_piece = hidden_units // here.n
    part_rows = hidden_units // here.n_dp
    first = here.core == 0
    for b in range(blocks):
        cols = slice(b * step, (b + 1) * step)
        gdown = tn(act_scr[:, cols], down_low).astype(bf16)
        for pair in range(here.n_dp // 2 // blocks):
            m = (b * (here.n_dp // 2 // blocks) + pair) ^ here.chip
            for j in range(here.n):
                s = (j + here.n - here.z) % here.n
                for g in range(groups):
                    at = 2 * pair * part_rows + g * own
                    lanes = slice(j * piece, (j + 1) * piece)
                    even = gdown[at : at + own, lanes]
                    odd = gdown[at + part_rows : at + part_rows + own, lanes]
                    base = piece + up_piece + g * piece
                    mine_ref[m, s, :, base : base + piece] = jnp.where(first, even, odd)
                    theirs_ref[m, s, :, base : base + piece] = jnp.where(first, odd, even)
        up = up_scr[:, cols]
        sig = jax.nn.sigmoid(up)
        up_low = (
            nt(down_low, wdn_ref[cols, :]) * sig * (1.0 + up * (1.0 - sig))
        ).astype(bf16)
        upl_scr[:, cols] = up_low
        small_ref[16 + b : 17 + b, :] = col_sum(up_low.astype(f32))
        grad_h2 = grad_h2 + nt(up_low, wup_ref[:, cols])
    write_grads(mine_ref, theirs_ref, here, nn(h2_t, upl_scr[...]), piece)
    small_ref[11:12, :] = col_sum(grad_h2 * normed2)
    small_ref[8:9, :] = col_sum(grad_h2)
    grad_two = norm_backward(grad_h2, normed2, inv2, vec_ref[11:12, :])
    small_ref[5:6, :] = col_sum(grad_two)
    gtwo_ref[...] = grad_two
    two_low = grad_two.astype(bf16)
    write_grads(mine_ref, theirs_ref, here, tn(catt_ref[...], two_low), 0)
    cgrad_ref[...] = nt(two_low, wco_ref[...]).astype(bf16)


def ones_sum(t_ref):
    return nt(jnp.ones((8, t_ref.shape[1]), bf16), t_ref[...])[0:1, :]


def cross_backward_pairs(here, q_ref, k_ref, v_ref, att_ref, g_ref, lse_ref, vec_ref, scratch, first, last):
    qt_scr, gt_scr, dq_scr, dkt_scr, dvt_scr = scratch
    length = k_ref.shape[0]
    size = q_ref.shape[0] // 2
    qt_scr[...] = q_ref[...].T
    gt_scr[...] = g_ref[...].T
    half = length // 2
    limit = length_limit(here, vec_ref)

    def pairs(pair, carry):
        for block in range(2):
            parts = []
            for part in range(2):
                start = part * half

                def visible(count, keys, start=start):
                    return lax.broadcasted_iota(jnp.int32, (count, keys), 1) + start < limit

                parts.append((start, half, visible, block == 1))
            attend_rows_back(
                q_ref, k_ref, v_ref, att_ref, g_ref, lse_ref, qt_scr, gt_scr,
                dq_scr, dkt_scr, dvt_scr, block * size, size, parts, pair,
            )
        return carry

    lax.fori_loop(first, last, pairs, 0)


def cross_backward_kernel(
    first, last, cq_ref, ek_ref, ev_ref, catt_ref, cgrad_ref, clse_ref, vec_ref,
    dq_ref, low_ref, *scratch,
):
    cross_backward_pairs(
        Here(), cq_ref, ek_ref, ev_ref, catt_ref, cgrad_ref, clse_ref, vec_ref, scratch, first, last
    )
    _, _, dq_scr, dkt_scr, dvt_scr = scratch
    done = last * PAIR
    dq_ref[:, :done] = dq_scr[:, :done]
    low_ref[:done, :] = dkt_scr[:done, :].astype(bf16)
    low_ref[done:, :] = dvt_scr[:done, :].astype(bf16)


def cross_backward_rest_kernel(
    cq_ref, ek_ref, ev_ref, catt_ref, cgrad_ref, clse_ref, vec_ref, dq_in_ref, low_in_ref, enc_ref, wckv_ref,
    mine_ref, theirs_ref, qgrad_ref, gw_ref, evsum_ref, *scratch,
):
    here = Here()
    low_scr = scratch[-1]
    length, width = enc_ref.shape
    rows = cq_ref.shape[0]
    done = PAIR
    cross_backward_pairs(
        here, cq_ref, ek_ref, ev_ref, catt_ref, cgrad_ref, clse_ref, vec_ref, scratch[:-1], 1, H // 2
    )
    _, _, dq_scr, dkt_scr, dvt_scr = scratch[:-1]
    dq_scr[:, :done] = dq_in_ref[:, :done]
    low_scr[:done, :] = low_in_ref[:done, :]
    low_scr[done:width, :] = dkt_scr[done:, :].astype(bf16)
    low_scr[width : width + done, :] = low_in_ref[done:, :]
    low_scr[width + done :, :] = dvt_scr[done:, :].astype(bf16)
    for t, piece in enumerate(here.slots()):
        at = pl.ds(pl.multiple_of(piece * rows, rows), rows)
        out_ref, slot = (mine_ref, t) if t < here.h else (theirs_ref, t - here.h)
        out_ref[slot * rows : (slot + 1) * rows, :] = (
            nn(wckv_ref[...], low_scr[:, at]).T.astype(bf16)
        )
    qgrad_ref[...] = (dq_scr[...].astype(f32) * SCALE).astype(bf16)
    evsum_ref[...] = jnp.zeros_like(evsum_ref)
    evsum_ref[0:1, :] = ones_sum(low_scr.at[width:, :])
    gw_ref[...] = nn(low_scr[...], enc_ref[...]).T.astype(bf16)


def norm_one_backward_kernel(
    qgrad_ref, wcq_ref, wso_ref, vec_ref, res1_ref, att_ref, gtwo_ref, small_in_ref, evsum_ref,
    gone_ref, sgrad_ref, gcq_ref, gso_ref, small_ref,
):
    small_ref[...] = small_in_ref[...]
    small_ref[3:4, :] = col_sum(qgrad_ref[...].astype(f32))
    small_ref[4:5, :] = evsum_ref[0:1, :]
    normed, inv = norm_stats(res1_ref[...])
    grad_h1 = gtwo_ref[...] + nt(qgrad_ref[...], wcq_ref[...])
    small_ref[10:11, :] = col_sum(grad_h1 * normed)
    small_ref[7:8, :] = col_sum(grad_h1)
    grad_one = norm_backward(grad_h1, normed, inv, vec_ref[10:11, :])
    small_ref[2:3, :] = col_sum(grad_one)
    gone_ref[...] = grad_one
    one_low = grad_one.astype(bf16)
    sgrad_ref[...] = nt(one_low, wso_ref[...]).astype(bf16)
    hidden = (normed * vec_ref[10:11, :] + vec_ref[7:8, :]).astype(bf16)
    gcq_ref[...] = tn(hidden, qgrad_ref[...]).astype(bf16)
    gso_ref[...] = tn(att_ref[...], one_low).astype(bf16)


def self_backward_kernel(
    q_ref, k_ref, v_ref, att_ref, sgrad_ref, lse_ref, x_ref, w_ref, gone_ref,
    small_in_ref, gckv_ref, gcq_ref, gso_ref,
    mine_ref, theirs_ref, gmine_ref, gtheirs_ref,
    qt_scr, gt_scr, dq_scr, dkt_scr, dvt_scr, low_scr, gin_scr, small_scr, small_t_scr,
):
    here = Here()
    n = here.n
    length, width = x_ref.shape
    rows = q_ref.shape[0]
    size = rows // 2
    qt_scr[...] = q_ref[...].T
    gt_scr[...] = sgrad_ref[...].T
    for which in range(n):

        @pl.when(here.worker == which)
        def _(which=which):
            order = sorted(range(2), key=lambda block: -chunk_of(which, block, n))
            top = chunk_of(which, order[0], n)
            if top + 1 < 2 * n:
                rest = (2 * n - 1 - top) * size
                dkt_scr[:, (top + 1) * size :] = jnp.zeros((width, rest), f32)
                dvt_scr[:, (top + 1) * size :] = jnp.zeros((width, rest), f32)

            def pairs(pair, carry):
                for order_place, block in enumerate(order):
                    chunk = chunk_of(which, block, n)
                    parts = []
                    for start, count, mask in causal_parts(chunk, size):
                        while count > 4 * size:
                            parts.append((start, 4 * size, mask, order_place == 1))
                            start, count = start + 4 * size, count - 4 * size
                        parts.append((start, count, mask, order_place == 1))
                    attend_rows_back(
                        q_ref, k_ref, v_ref, att_ref, sgrad_ref, lse_ref, qt_scr, gt_scr,
                        dq_scr, dkt_scr, dvt_scr, block * size, size, parts, pair,
                    )
                return carry

            lax.fori_loop(0, H // 2, pairs, 0)

    low_scr[:width, :] = dkt_scr[...].astype(bf16)
    low_scr[width:, :] = dvt_scr[...].astype(bf16)
    q_grad = (dq_scr[...].astype(f32) * SCALE).astype(bf16)
    small_scr[...] = jnp.zeros_like(small_scr)
    small_scr[: small_in_ref.shape[0], :] = small_in_ref[...]
    small_scr[0:1, :] = col_sum(q_grad.astype(f32))
    small_scr[1:2, :] = ones_sum(low_scr.at[width:, :])
    for t in range(n):
        at = slice(t * rows, (t + 1) * rows)
        gin_scr[at, :] = nn(w_ref[:, width:], low_scr[:, at]).T
    even = here.even_chunk()
    wq_grad = jnp.zeros((width, width), f32)
    for block in range(2):
        chunk = even if block == 0 else 2 * n - 1 - even
        at = pl.ds(pl.multiple_of(chunk * size, size), size)
        own_rows = slice(block * size, (block + 1) * size)
        wq_grad = wq_grad + tn(x_ref[at, :], q_grad[own_rows])
        gin_scr[at, :] += gone_ref[own_rows, :] + nt(q_grad[own_rows], w_ref[:, :width])
    for t, piece in enumerate(here.slots()):
        at = pl.ds(pl.multiple_of(piece * rows, rows), rows)
        out_ref, slot = (mine_ref, t) if t < here.h else (theirs_ref, t - here.h)
        out_ref[slot * rows : (slot + 1) * rows, :] = gin_scr[at, :].astype(bf16)
    kv_grad = nn(low_scr[...], x_ref[...]).T.astype(bf16)
    piece = width // n
    own = width // here.n_dp
    grads = jnp.concatenate([wq_grad.astype(bf16), kv_grad], axis=1)
    write_grads(gmine_ref, gtheirs_ref, here, grads, 0)
    write_grads(gmine_ref, gtheirs_ref, here, gcq_ref[...], 3 * piece)
    write_grads(gmine_ref, gtheirs_ref, here, gckv_ref[...], 4 * piece)
    write_grads(gmine_ref, gtheirs_ref, here, gso_ref[...], 6 * piece)
    small_t_scr[width:, :] = jnp.zeros((TINY, PAIR), f32)
    small_t_scr[:width, :] = small_scr[...].T
    cells = own // n
    groups = GROUPS
    first = here.core == 0
    cols = gmine_ref.shape[3]

    def tiny(i, j):
        blocks = [small_t_scr[i * own + j * cells : i * own + j * cells + TINY, :]]
        up0 = (i * groups * own + j * groups * cells) % width
        for q in range(groups):
            blocks.append(small_t_scr[up0 + q * cells : up0 + q * cells + TINY, :])
        return jnp.concatenate(blocks, axis=1).astype(bf16)

    for pair in range(here.n_dp // 2):
        m = pair ^ here.chip
        for j in range(n):
            s = (j + n - here.z) % n
            even_block, odd_block = tiny(2 * pair, j), tiny(2 * pair + 1, j)
            used = even_block.shape[1]
            gmine_ref[m, s, own:, :used] = jnp.where(first, even_block, odd_block)
            gtheirs_ref[m, s, own:, :used] = jnp.where(first, odd_block, even_block)
            if used < cols:
                gmine_ref[m, s, own:, used:] = jnp.zeros((TINY, cols - used), bf16)
                gtheirs_ref[m, s, own:, used:] = jnp.zeros((TINY, cols - used), bf16)


def finish_kernel(*refs):
    here = Here()
    n = here.n
    one_refs, refs = refs[:n], refs[n:]
    two_refs, refs = refs[:n], refs[n:]
    self_ref, so_ref, cq_ref, kv_ref, co_ref, up_ref, dn_ref, bias_ref, gain_ref, upb_ref, square_scr = refs
    own, piece = so_ref.shape
    groups = upb_ref.shape[0]
    cells = bias_ref.shape[1]
    one = functools.reduce(jnp.add, [ref[...].astype(f32) for ref in one_refs])
    two = functools.reduce(jnp.add, [ref[...].astype(f32) for ref in two_refs])
    up_piece = up_ref.shape[1]
    co_ref[...] = one[:, :piece]
    up_ref[...] = one[:, piece : piece + up_piece]
    for g in range(groups):
        base = piece + up_piece + g * piece
        dn_ref[g * own : (g + 1) * own, :] = one[:, base : base + piece]
    main = two[:own]
    self_ref[...] = main[:, : 3 * piece]
    cq_ref[...] = main[:, 3 * piece : 4 * piece]
    kv_ref[...] = main[:, 4 * piece : 6 * piece]
    so_ref[...] = main[:, 6 * piece : 7 * piece]
    small = two[own:, :PAIR]
    lane = lax.broadcasted_iota(jnp.int32, small.shape, 1)
    column = 16 + (here.dp * groups * own + here.z * groups * cells) // (own * here.n_dp)
    for q in range(groups):
        block = two[own:, (1 + q) * PAIR : (2 + q) * PAIR]
        value = jnp.sum(jnp.where(lane == column, block, 0.0), axis=-1, keepdims=True)
        small = jnp.where(lane == 24 + q, value, small)
    square_scr[...] = jnp.zeros_like(square_scr)
    square_scr[: small.shape[0], :] = small
    turned = square_scr[...].T
    bias_ref[...] = turned[0:10, :cells]
    gain_ref[...] = turned[10:13, :cells]
    upb_ref[...] = turned[24 : 24 + groups, :cells]


TINY = 16
GROUPS = 4


class Gathered:
    def __init__(self, blocks, partners, start, cols, groups=1):
        self.blocks, self.partners, self.start, self.cols, self.groups = blocks, partners, start, cols, groups
        self.own = blocks[0].shape[0]
        self.rows = 2 * len(blocks) * self.own * groups

    def arrays(self):
        return [*self.blocks, *self.partners]

    def started(self, refs, held_ref, here, sems):
        own = self.own
        chips = len(self.blocks)
        copies = []
        others = [
            ref.at[i * own : (i + 1) * own, :] for ref in refs[chips:] for i in range(ref.shape[0] // own)
        ]
        for m in range(chips):
            for side in range(2):
                place = 2 * (here.chip ^ m) + (here.core ^ side)
                source = refs[m] if side == 0 else others[m]
                for g in range(self.groups):
                    row = pl.multiple_of((place * self.groups + g) * own, own)
                    start = self.start + g * self.cols
                    copies.append(
                        pltpu.make_async_copy(
                            source.at[:, start : start + self.cols],
                            held_ref.at[pl.ds(row, own), :],
                            sems[len(copies)],
                        )
                    )
                    copies[-1].start()
        return copies


def run_kernel(kernel, outs, args, scratch=()):
    name = getattr(kernel, "func", kernel).__name__
    whole = pl.BlockSpec(memory_space=pltpu.VMEM)
    plain = [arg for arg in args if not isinstance(arg, Gathered)]
    parts = [arg for arg in args if isinstance(arg, Gathered)]
    sources = []
    for part in parts:
        for array in part.arrays():
            if not any(array is source for source in sources):
                sources.append(array)
    where = [
        [[i for i, source in enumerate(sources) if source is array][0] for array in part.arrays()]
        for part in parts
    ]
    specs = [whole] * len(plain) + [pl.BlockSpec(memory_space=pltpu.HBM)] * len(sources)
    held = [pltpu.VMEM((part.rows, part.cols), bf16) for part in parts]
    counts = [2 * len(part.blocks) * part.groups for part in parts]
    extra = held + ([pltpu.SemaphoreType.DMA((sum(counts),))] if parts else [])

    def body(*refs):
        plain_refs, refs = refs[: len(plain)], refs[len(plain) :]
        source_refs, refs = refs[: len(sources)], refs[len(sources) :]
        extra_refs, refs = refs[len(refs) - len(extra) :], refs[: len(refs) - len(extra)]
        copies = []
        if parts:
            here = Here()
            for part, places, held_ref, count in zip(parts, where, extra_refs, counts):
                part_refs = [source_refs[i] for i in places]
                sems = [extra_refs[-1].at[len(copies) + i] for i in range(count)]
                copies += part.started(part_refs, held_ref, here, sems)
        for copy in copies:
            copy.wait()
        left, held_refs, in_refs = list(plain_refs), list(extra_refs), []
        for arg in args:
            in_refs.append(held_refs.pop(0) if isinstance(arg, Gathered) else left.pop(0))
        kernel(*in_refs, *refs)

    return pl.pallas_call(
        body,
        out_shape=tuple(jax.ShapeDtypeStruct(shape, kind) for shape, kind in outs),
        in_specs=specs,
        out_specs=tuple(whole for _ in outs),
        scratch_shapes=list(scratch) + extra,
        compiler_params=pltpu.CompilerParams(vmem_limit_bytes=VMEM[name] * 2**20),
        cost_estimate=pl.CostEstimate(flops=1, bytes_accessed=1, transcendentals=0),
    )(*plain, *sources)


def stack_kernel(*refs):
    out_ref = refs[-1]
    start = 0
    for ref in refs[:-1]:
        out_ref[start : start + ref.shape[0], :] = ref[...]
        start += ref.shape[0]


def together_kernel(own_ref, *refs):
    here = Here()
    arrived_refs, out_ref = refs[:-1], refs[-1]
    rows = own_ref.shape[0]

    @pl.when(here.home)
    def _():
        out_ref[:rows, :] = own_ref[...]

    @pl.when(jnp.logical_not(here.home))
    def _():
        out_ref[:rows, :] = arrived_refs[-1][...]

    for t, ref in enumerate(arrived_refs[:-1]):
        out_ref[(t + 1) * rows : (t + 2) * rows, :] = ref[...]


def pack_kernel(
    lens_ref, self_ref, kv_ref, so_ref, cq_ref, up_ref, co_ref, dn_ref, bias_ref, gain_ref, upb_ref,
    one_ref, three_ref, rows_scr,
):
    own = self_ref.shape[0]
    groups = upb_ref.shape[0]
    at = self_ref.shape[1]
    one_ref[:, :at] = self_ref[...]
    start = at + PAIR
    for ref in (kv_ref, so_ref, cq_ref):
        one_ref[:, start : start + ref.shape[1]] = ref[...]
        start += ref.shape[1]
    start = 0
    for ref in [up_ref, co_ref] + [dn_ref.at[g * own : (g + 1) * own, :] for g in range(groups)]:
        three_ref[:, start : start + ref.shape[1]] = ref[...]
        start += ref.shape[1]
    rows_scr[...] = jnp.zeros_like(rows_scr)
    rows_scr[0:10, :own] = bias_ref[...].astype(f32)
    rows_scr[10:13, :own] = gain_ref[...].astype(f32)
    rows_scr[13 : 13 + groups, :own] = upb_ref[...].astype(f32)
    length = lens_ref[0]
    rows_scr[17:18, :own] = jnp.full((1, own), length // 64, jnp.int32).astype(f32)
    rows_scr[18:19, :own] = jnp.full((1, own), length % 64, jnp.int32).astype(f32)
    one_ref[:, at : at + PAIR] = rows_scr[...].T[:own, :].astype(bf16)


def pack_weights(
    w_self, w_cross_kv, w_self_out, w_cross_q, w_up, w_cross_out, w_down, biases, gains, up_bias, lens, wide1, wide3
):
    own = w_self.shape[0]
    whole = pl.BlockSpec(memory_space=pltpu.VMEM)
    return pl.pallas_call(
        pack_kernel,
        out_shape=(jax.ShapeDtypeStruct((own, wide1), bf16), jax.ShapeDtypeStruct((own, wide3), bf16)),
        in_specs=[pl.BlockSpec(memory_space=pltpu.SMEM)] + [whole] * 10,
        out_specs=(whole, whole),
        scratch_shapes=[pltpu.VMEM((PAIR, PAIR), f32)],
        compiler_params=pltpu.CompilerParams(vmem_limit_bytes=VMEM["pack_kernel"] * 2**20),
        cost_estimate=pl.CostEstimate(flops=1, bytes_accessed=1, transcendentals=0),
    )(lens, w_self, w_cross_kv, w_self_out, w_cross_q, w_up, w_cross_out, w_down, biases, gains, up_bias)


class Routes:
    def __init__(self, n, n_dp):
        self.n, self.h = n, n // 2
        self.chips = n_dp // 2

    def all_chips(self, pairs):
        return [
            ((2 * k + c0) * self.n + z0, (2 * k + c1) * self.n + z1)
            for k in range(self.chips)
            for (c0, z0), (c1, z1) in pairs
        ]

    def gather(self, r):
        h = self.h
        pairs = []
        for c in range(2):
            for i in range(h):
                far = (c, (1 - c) * h + i)
                if r < h:
                    pairs.append(((c, c * h + i), (1 - c, c * h + (i + r) % h)))
                    pairs.append((far, (c, c * h + (i + r - 1) % h)))
                else:
                    pairs.append((far, (1 - c, c * h + (i + h - 1) % h)))
        return self.all_chips(pairs)

    def rows(self, odd):
        n, h = self.n, self.h
        pairs = []
        for c in range(2):
            for z in range(n):
                chunk = 2 * z + odd
                w = chunk if chunk < n else 2 * n - 1 - chunk
                pairs.append(((c, z), (w % 2, c * h + w // 2)))
        return self.all_chips(pairs)


def back(pairs):
    return [(b, a) for a, b in pairs]


BOTH = ("dp", "sp")


def after(first, then):
    return lax.optimization_barrier((first, then))[1]


def on_device(
    inputs, encoder, cotangent, w_self, w_self_out, w_cross_q, w_cross_kv, w_cross_out, w_up, w_down,
    biases, norm_gains, up_bias, source_lengths,
):
    here = Here()
    n, n_dp, h = here.n, here.n_dp, here.h
    chips = n_dp // 2
    _, rows, width = inputs.shape
    size = rows // 2
    length = n * rows
    hidden_units = w_up.shape[1]
    own = w_self.shape[0]
    piece = width // n
    up_piece = hidden_units // n
    cells = own // n
    groups = up_bias.shape[0] // own
    routes = Routes(n, n_dp)

    def swap(value):
        return lax.ppermute(value, "dp", [(i, i ^ 1) for i in range(n_dp)])

    def to_chip(value, m):
        return lax.ppermute(value, "dp", [(i, i ^ (2 * m)) for i in range(n_dp)])

    def shift(value, s):
        return lax.ppermute(value, "sp", [(i, (i + s) % n) for i in range(n)])

    def gather(value):
        return [lax.ppermute(value, BOTH, routes.gather(r)) for r in range(1, h + 1)]

    def together(value, arrived):
        return jnp.concatenate([jnp.where(here.home, value, arrived[-1])] + arrived[:-1], axis=0)

    def chip_blocks(value):
        return [value] + [to_chip(value, m) for m in range(1, chips)]

    def swap_blocks(blocks):
        shape = (sum(block.shape[0] for block in blocks), blocks[0].shape[1])
        return swap(run_kernel(stack_kernel, [(shape, bf16)], blocks)[0])

    wide1 = 3 * width + PAIR + 4 * width
    wide3 = hidden_units + width + groups * width
    pack1, pack3 = pack_weights(
        w_self, w_cross_kv, w_self_out, w_cross_q, w_up, w_cross_out, w_down,
        biases, norm_gains, up_bias.reshape(groups, own), source_lengths.astype(jnp.int32), wide1, wide3,
    )
    x_arrived = gather(inputs[0])
    own1 = chip_blocks(pack1)
    x_arrived, own1, pack3, enc_own = lax.optimization_barrier((x_arrived, own1, pack3, encoder[0]))
    x_mine = together(inputs[0], x_arrived)
    partner1 = [swap_blocks(own1)]
    x_theirs = swap(x_mine)
    enc_arrived = gather(enc_own)
    near3 = [to_chip(pack3, m) for m in range(1, chips - 1)]

    q, k, v, att, lse, x_full, xq, vec = run_kernel(
        self_forward_kernel,
        [((rows, width), bf16), ((length, width), bf16), ((length, width), bf16),
         ((rows, width), bf16), ((rows, PAIR), f32), ((length, width), bf16), ((rows, width), bf16),
         ((32, width), f32)],
        (x_mine, x_theirs, Gathered(own1, partner1, 0, 3 * width), Gathered(own1, partner1, 3 * width, PAIR)),
    )
    at2 = 3 * width + PAIR
    wckv = Gathered(own1, partner1, at2, 2 * width)
    wso = Gathered(own1, partner1, at2 + 2 * width, width)
    wcq = Gathered(own1, partner1, at2 + 3 * width, width)
    enc_arrived, near3, att = lax.optimization_barrier((enc_arrived, near3, att))
    enc_mine = together(enc_own, enc_arrived)
    enc_theirs = swap(enc_mine)
    res1, cq = run_kernel(
        cross_query_kernel,
        [((rows, width), f32), ((rows, width), bf16)],
        (att, xq, wso, wcq, vec),
    )
    enc_theirs, cq = lax.optimization_barrier((enc_theirs, cq))
    near3 = [pack3] + near3
    partner3 = [swap_blocks(near3)]
    far3 = to_chip(after(enc_mine, pack3), chips - 1)
    late_cot = after(enc_mine, cotangent[0])
    cot0 = lax.ppermute(late_cot[:size], BOTH, routes.rows(0))
    cot1 = lax.ppermute(late_cot[size:], BOTH, routes.rows(1))
    ek, ev, catt, clse, enc_full = run_kernel(
        cross_forward_kernel,
        [((length, width), bf16), ((length, width), bf16), ((rows, width), bf16), ((rows, PAIR), f32),
         ((length, width), bf16)],
        (enc_mine, enc_theirs, cq, wckv, vec),
    )
    far3, partner3, cot0, cot1, catt = lax.optimization_barrier((far3, partner3, cot0, cot1, catt))
    own3 = near3 + [far3]
    partner3 = partner3 + [swap(far3)]
    wup = Gathered(own3, partner3, 0, hidden_units)
    wco = Gathered(own3, partner3, hidden_units, width)
    wdn = Gathered(own3, partner3, hidden_units + width, width, groups)
    block1 = (chips, n, own, piece + up_piece + groups * piece)
    out0, out1, gtwo, cgrad, mine1, theirs1, small = run_kernel(
        feed_forward_kernel,
        [((size, width), bf16), ((size, width), bf16), ((rows, width), f32), ((rows, width), bf16),
         (block1, bf16), (block1, bf16), ((24, width), f32)],
        (res1, catt, wco, wup, wdn, vec, cot0, cot1),
        scratch=[pltpu.VMEM((rows, hidden_units), f32), pltpu.VMEM((rows, hidden_units), bf16),
                 pltpu.VMEM((rows, hidden_units), bf16)],
    )

    def add(a, b):
        return (a.astype(f32) + b.astype(f32)).astype(bf16)

    def between_chips(mine, arrived):
        sums = [add(mine[m], arrived[m]) for m in range(chips)]
        return sums[0], [to_chip(sums[m], m) for m in range(1, chips)]

    def between_places(first, parts):
        total = first.astype(f32)
        for part in parts:
            total = total + part.astype(f32)
        low = total.astype(bf16)
        return low[0], [shift(low[s], s) for s in range(1, n)]

    def finish(first, parts):
        total = first.astype(f32)
        for part in parts:
            total = total + part.astype(f32)
        return total

    def pieces_home(mine, arrived):
        sums = [add(mine[t * rows : (t + 1) * rows], arrived[t * rows : (t + 1) * rows]) for t in range(h)]
        parts = [lax.ppermute(sums[r], BOTH, back(routes.gather(r))) for r in range(1, h)]
        last = lax.ppermute(sums[0], BOTH, back(routes.gather(h)))
        return sums, (jnp.where(here.home, sums[0], last), parts)

    half_low = (2 * PAIR, length)
    back_scratch = [
        pltpu.VMEM((width, rows), bf16), pltpu.VMEM((width, rows), bf16), pltpu.VMEM((rows, width), bf16),
        pltpu.VMEM((width, length), f32), pltpu.VMEM((width, length), f32),
    ]
    low_scratch = [pltpu.VMEM((2 * width, length), bf16)]
    arrived1 = swap(theirs1)
    dq_a, low_a = run_kernel(
        functools.partial(cross_backward_kernel, 0, 1),
        [((rows, width), bf16), (half_low, bf16)],
        (cq, ek, ev, catt, cgrad, clse, vec), scratch=back_scratch,
    )
    mine1, arrived1, low_a, out0, out1 = lax.optimization_barrier((mine1, arrived1, low_a, out0, out1))
    chips1 = between_chips(mine1, arrived1)
    out_parts = (
        lax.ppermute(out0, BOTH, back(routes.rows(0))), lax.ppermute(out1, BOTH, back(routes.rows(1)))
    )
    emine, etheirs, qgrad, gckv, evsum = run_kernel(
        cross_backward_rest_kernel,
        [((h * rows, width), bf16), ((h * rows, width), bf16), ((rows, width), bf16),
         ((width, 2 * width), bf16), ((8, width), f32)],
        (cq, ek, ev, catt, cgrad, clse, vec, dq_a, low_a, enc_full, wckv),
        scratch=back_scratch + low_scratch,
    )
    chips1, out_parts, etheirs, qgrad = lax.optimization_barrier((chips1, out_parts, etheirs, qgrad))
    earrived = swap(etheirs)
    gone, sgrad, gcq, gso, small = run_kernel(
        norm_one_backward_kernel,
        [((rows, width), f32), ((rows, width), bf16), ((width, width), bf16), ((width, width), bf16),
         ((24, width), f32)],
        (qgrad, wcq, wso, vec, res1, att, gtwo, small, evsum),
    )
    emine, earrived, sgrad = lax.optimization_barrier((emine, earrived, sgrad))
    _, enc_home = pieces_home(emine, earrived)
    places1 = between_places(*chips1)
    block2 = (chips, n, own + TINY, max(7 * piece, (1 + groups) * PAIR))
    gmine, gtheirs, mine2, theirs2 = run_kernel(
        self_backward_kernel,
        [((h * rows, width), bf16), ((h * rows, width), bf16), (block2, bf16), (block2, bf16)],
        (q, k, v, att, sgrad, lse, x_full, Gathered(own1, partner1, 0, 3 * width), gone, small,
         gckv, gcq, gso),
        scratch=back_scratch + low_scratch
        + [pltpu.VMEM((length, width), f32), pltpu.VMEM((PAIR, width), f32),
           pltpu.VMEM((width + TINY, PAIR), f32)],
    )
    enc_home, places1, gtheirs, theirs2 = lax.optimization_barrier((enc_home, places1, gtheirs, theirs2))
    garrived = swap(gtheirs)
    arrived2 = swap(theirs2)
    in_sums, in_home = pieces_home(gmine, garrived)
    out_parts, enc_home = after(in_sums, (out_parts, enc_home))
    output = jnp.concatenate(out_parts, axis=0)[None]
    places2 = between_places(*between_chips(mine2, arrived2))
    g_self, g_so, g_cq, g_ckv, g_co, g_up, g_dn, g_bias, g_gain, g_upb = run_kernel(
        finish_kernel,
        [(shape, f32) for shape in (
            (own, 3 * piece), (own, piece), (own, piece), (own, 2 * piece), (own, piece), (own, up_piece),
            (groups * own, piece), (10, cells), (3, cells), (groups, cells),
        )],
        (places1[0], *places1[1], places2[0], *places2[1]),
        scratch=[pltpu.VMEM((PAIR, PAIR), f32)],
    )
    return (
        output,
        finish(*in_home)[None],
        finish(*enc_home)[None],
        g_self,
        g_so,
        g_cq,
        g_ckv,
        g_co,
        g_up,
        g_dn,
        g_bias,
        g_gain,
        g_upb.reshape(groups * cells),
    )


def solution(mesh):
    weight = P("dp", None)
    tokens = P("dp", "sp", None)
    return jax.shard_map(
        on_device,
        mesh=mesh,
        in_specs=(tokens,) * 3 + (weight,) * 7 + (P(None, "dp"), P(None, "dp"), P("dp"), P("dp")),
        out_specs=(tokens,) * 3
        + (P("dp", "sp"),) * 7
        + (P(None, ("dp", "sp")), P(None, ("dp", "sp")), P(("dp", "sp"))),
        check_vma=False,
    )
```

```python
import functools

import jax
import jax.numpy as jnp
from jax import lax
from jax.experimental import pallas as pl
from jax.experimental.pallas import tpu as pltpu
from jax.sharding import PartitionSpec as P

H = 8
DH = 64
PAIR = 128

eps_norm = 1e-05
masked_out = -1e30
bf16 = jnp.bfloat16
f32 = jnp.float32
SCALE = DH ** (-0.5)

VMEM = {
    "self_forward_kernel": 11,
    "cross_query_kernel": 10,
    "cross_forward_kernel": 12,
    "feed_forward_kernel": 26,
    "cross_backward_kernel": 20,
    "cross_backward_rest_kernel": 27,
    "norm_one_backward_kernel": 12,
    "self_backward_kernel": 28,
    "finish_kernel": 6,
    "pack_kernel": 60,
    "stack_kernel": 4,
    "together_kernel": 2,
}


def nn(left, right):
    return lax.dot_general(left, right, (((1,), (0,)), ((), ())), preferred_element_type=f32)


def nt(left, right):
    return lax.dot_general(left, right, (((1,), (1,)), ((), ())), preferred_element_type=f32)


def tn(left, right):
    return lax.dot_general(left, right, (((0,), (0,)), ((), ())), preferred_element_type=f32)


def norm_stats(resid):
    centred = resid - jnp.mean(resid, axis=-1, keepdims=True)
    inv_std = lax.rsqrt(jnp.mean(centred * centred, axis=-1, keepdims=True) + eps_norm)
    return centred * inv_std, inv_std


def norm_backward(upstream, normed, inv_std, gain):
    scaled = upstream * gain
    centre_term = jnp.mean(scaled, axis=-1, keepdims=True)
    slope_term = jnp.mean(scaled * normed, axis=-1, keepdims=True)
    return inv_std * (scaled - centre_term - normed * slope_term)


def col_sum(value):
    return jnp.sum(value, axis=0, keepdims=True)


def chunk_of(d, block, n):
    even = d if d % 2 == 0 else 2 * n - 1 - d
    return even if block == 0 else 2 * n - 1 - even


def lane_head(rows, cols=PAIR):
    return lax.broadcasted_iota(jnp.int32, (rows, cols), 1) // DH


def one_head(pair_value, head):
    return jnp.where(lane_head(*pair_value.shape) == head, pair_value, jnp.zeros_like(pair_value))


def pair_slice(pair):
    return pl.ds(pl.multiple_of(pair * PAIR, PAIR), PAIR)


class Here:
    def __init__(self):
        self.n, self.n_dp = lax.axis_size("sp"), lax.axis_size("dp")
        dp = lax.axis_index("dp").astype(jnp.int32)
        self.z = lax.axis_index("sp").astype(jnp.int32)
        self.h = self.n // 2
        self.chip, self.core = dp // 2, dp % 2
        self.dp = dp
        self.half = self.z // self.h
        self.local = self.z % self.h
        self.worker = 2 * self.local + self.core
        self.seq = 2 * self.chip + self.half
        self.home = self.core == self.half

    def slots(self):
        h, c, g = self.h, self.half, self.local

        def part(home):
            at_home = [self.z] + [(1 - c) * h + (g + h - (r - 1)) % h for r in range(1, h)]
            at_other = [(1 - c) * h + (g + 1) % h] + [c * h + (g + h - r) % h for r in range(1, h)]
            return [jnp.where(home, a, b) for a, b in zip(at_home, at_other)]

        return part(self.home) + part(jnp.logical_not(self.home))

    def even_chunk(self):
        return jnp.where(self.worker % 2 == 0, self.worker, 2 * self.n - 1 - self.worker)


def write_grads(mine_ref, theirs_ref, here, value, col0):
    own = value.shape[0] // here.n_dp
    cols = value.shape[1] // here.n
    low = value.astype(bf16)
    first = here.core == 0
    for pair in range(here.n_dp // 2):
        m = pair ^ here.chip
        for j in range(here.n):
            s = (j + here.n - here.z) % here.n
            at = slice(j * cols, (j + 1) * cols)
            even = low[2 * pair * own : (2 * pair + 1) * own, at]
            odd = low[(2 * pair + 1) * own : (2 * pair + 2) * own, at]
            mine_ref[m, s, :own, col0 : col0 + cols] = jnp.where(first, even, odd)
            theirs_ref[m, s, :own, col0 : col0 + cols] = jnp.where(first, odd, even)


def attend_rows(q_ref, k_ref, v_ref, att_ref, lse_ref, row0, rows, parts, pair):
    cols = pair_slice(pair)
    q2 = q_ref[row0 : row0 + rows, cols]
    both = []
    lse_now = lse_ref[row0 : row0 + rows, :]
    lane = lax.broadcasted_iota(jnp.int32, (rows, PAIR), 1)
    for h in range(2):
        qm = one_head(q2, h)
        scores = []
        for start, size, mask in parts:
            s = nt(qm, k_ref[start : start + size, cols])
            if mask is not None:
                s = jnp.where(mask(rows, size), s, masked_out)
            scores.append(s)
        top = functools.reduce(
            jnp.maximum, [jnp.max(s, axis=-1, keepdims=True) for s in scores]
        )
        total = 0.0
        result = 0.0
        for s, (start, size, _) in zip(scores, parts):
            e = jnp.exp(s - top)
            total = total + jnp.sum(e, axis=-1, keepdims=True)
            result = result + nn(e.astype(bf16), v_ref[start : start + size, cols])
        both.append(result / total)
        lse_now = jnp.where(lane == pair * 2 + h, top + jnp.log(total), lse_now)
    lse_ref[row0 : row0 + rows, :] = lse_now
    att_ref[row0 : row0 + rows, cols] = jnp.where(
        lane_head(rows) == 0, both[0], both[1]
    ).astype(bf16)


def attend_rows_back(
    q_ref, k_ref, v_ref, att_ref, g_ref, lse_ref, qt_ref, gt_ref,
    dq_ref, dkt_ref, dvt_ref, row0, rows, parts, pair,
):
    cols = pair_slice(pair)
    q2 = q_ref[row0 : row0 + rows, cols]
    g2 = g_ref[row0 : row0 + rows, cols]
    prod = g2.astype(f32) * att_ref[row0 : row0 + rows, cols].astype(f32)
    lse_all = lse_ref[row0 : row0 + rows, :]
    lane = lax.broadcasted_iota(jnp.int32, (rows, PAIR), 1)
    both = []
    for h in range(2):
        head = pair * 2 + h
        hrows = pl.ds(pl.multiple_of(head * DH, DH), DH)
        qm = one_head(q2, h)
        gm = one_head(g2, h)
        qt = qt_ref[hrows, row0 : row0 + rows]
        gt = gt_ref[hrows, row0 : row0 + rows]
        lse = jnp.sum(jnp.where(lane == head, lse_all, 0.0), axis=-1, keepdims=True)
        delta = jnp.sum(jnp.where(lane // DH == h, prod, 0.0), axis=-1, keepdims=True)
        dq = 0.0
        for start, size, mask, adds in parts:
            k2 = k_ref[start : start + size, cols]
            v2 = v_ref[start : start + size, cols]
            p = jnp.exp(nt(qm, k2) - lse)
            if mask is not None:
                p = jnp.where(mask(rows, size), p, 0.0)
            ds = (p * (nt(gm, v2) - delta)).astype(bf16)
            dq = dq + nn(ds, k2)
            dk = nn(qt, ds)
            dv = nn(gt, p.astype(bf16))
            if adds:
                dk = dk + dkt_ref[hrows, start : start + size]
                dv = dv + dvt_ref[hrows, start : start + size]
            dkt_ref[hrows, start : start + size] = dk
            dvt_ref[hrows, start : start + size] = dv
        both.append(dq)
    dq_ref[row0 : row0 + rows, cols] = (
        jnp.where(lane_head(rows) == 0, both[0], both[1]).astype(bf16)
    )


def diagonal(rows, size):
    row = lax.broadcasted_iota(jnp.int32, (rows, size), 0)
    col = lax.broadcasted_iota(jnp.int32, (rows, size), 1)
    return col <= row


def causal_parts(chunk, size):
    parts = []
    if chunk:
        parts.append((0, chunk * size, None))
    parts.append((chunk * size, size, diagonal))
    return parts


def self_forward_kernel(*refs):
    here = Here()
    n = here.n
    halves, refs = refs[:2], refs[2:]
    w_ref, s_ref, q_ref, k_ref, v_ref, att_ref, lse_ref, x_ref, xq_ref, vec_ref = refs
    length, width = x_ref.shape
    rows = q_ref.shape[0]
    size = rows // 2
    vec_ref[...] = s_ref[...].astype(f32).T[: vec_ref.shape[0], :]
    for t, piece in enumerate(here.slots()):
        at = pl.ds(pl.multiple_of(piece * rows, rows), rows)
        block = halves[t // here.h][(t % here.h) * rows : (t % here.h + 1) * rows, :]
        x_ref[at, :] = block
        kv = nn(block, w_ref[:, width : 3 * width])
        k_ref[at, :] = kv[:, :width].astype(bf16)
        v_ref[at, :] = (kv[:, width:] + vec_ref[1:2, :]).astype(bf16)
    even = here.even_chunk()
    for block in range(2):
        chunk = even if block == 0 else 2 * n - 1 - even
        xb = x_ref[pl.ds(pl.multiple_of(chunk * size, size), size), :]
        own_rows = slice(block * size, (block + 1) * size)
        xq_ref[own_rows, :] = xb
        q_ref[own_rows, :] = ((nn(xb, w_ref[:, :width]) + vec_ref[0:1, :]) * SCALE).astype(bf16)
    lse_ref[...] = jnp.zeros_like(lse_ref)

    for which in range(n):

        @pl.when(here.worker == which)
        def _(which=which):
            def pairs(pair, carry):
                for block in range(2):
                    chunk = chunk_of(which, block, n)
                    attend_rows(
                        q_ref, k_ref, v_ref, att_ref, lse_ref, block * size, size,
                        causal_parts(chunk, size), pair,
                    )
                return carry

            lax.fori_loop(0, H // 2, pairs, 0)


def cross_query_kernel(att_ref, xq_ref, wso_ref, wcq_ref, vec_ref, res_ref, cq_ref):
    res_ref[...] = xq_ref[...].astype(f32) + nn(att_ref[...], wso_ref[...]) + vec_ref[2:3, :]
    normed, _ = norm_stats(res_ref[...])
    hidden = (normed * vec_ref[10:11, :] + vec_ref[7:8, :]).astype(bf16)
    cq_ref[...] = ((nn(hidden, wcq_ref[...]) + vec_ref[3:4, :]) * SCALE).astype(bf16)


def length_limit(here, vec_ref):
    packed = vec_ref[17:18, :] * 64.0 + vec_ref[18:19, :]
    lane = lax.broadcasted_iota(jnp.int32, packed.shape, 1)
    picked = jnp.where(lane == here.seq * (packed.shape[1] // here.n_dp), packed, 0.0)
    return jnp.sum(picked, axis=-1, keepdims=True).astype(jnp.int32)


def cross_forward_kernel(*refs):
    here = Here()
    n = here.n
    halves, refs = refs[:2], refs[2:]
    cq_ref, wckv_ref, vec_ref, ek_ref, ev_ref, catt_ref, clse_ref, enc_ref = refs
    length, width = enc_ref.shape
    rows = cq_ref.shape[0]
    size = rows // 2
    for t, piece in enumerate(here.slots()):
        at = pl.ds(pl.multiple_of(piece * rows, rows), rows)
        block = halves[t // here.h][(t % here.h) * rows : (t % here.h + 1) * rows, :]
        enc_ref[at, :] = block
        kv = nn(block, wckv_ref[...])
        ek_ref[at, :] = kv[:, :width].astype(bf16)
        ev_ref[at, :] = (kv[:, width:] + vec_ref[4:5, :]).astype(bf16)
    clse_ref[...] = jnp.zeros_like(clse_ref)
    limit = length_limit(here, vec_ref)

    def visible(count, keys):
        return lax.broadcasted_iota(jnp.int32, (count, keys), 1) < limit

    def pairs(pair, carry):
        for block in range(2):
            attend_rows(
                cq_ref, ek_ref, ev_ref, catt_ref, clse_ref, block * size, size,
                [(0, length, visible)], pair,
            )
        return carry

    lax.fori_loop(0, H // 2, pairs, 0)


def feed_forward_kernel(
    res1_ref, catt_ref, wco_ref, wup_ref, wdn_ref, vec_ref, cot0_ref, cot1_ref,
    out0_ref, out1_ref, gtwo_ref, cgrad_ref, mine_ref, theirs_ref, small_ref,
    up_scr, act_scr, upl_scr,
):
    here = Here()
    rows, width = res1_ref.shape
    size = rows // 2
    hidden_units = wup_ref.shape[1]
    step = width
    blocks = hidden_units // step
    own = width // here.n_dp
    groups = hidden_units // width
    normed, _ = norm_stats(res1_ref[...])
    hidden_one = normed * vec_ref[10:11, :] + vec_ref[7:8, :]
    res2 = hidden_one + nn(catt_ref[...], wco_ref[...]) + vec_ref[5:6, :]
    normed2, inv2 = norm_stats(res2)
    hidden_two = normed2 * vec_ref[11:12, :] + vec_ref[8:9, :]
    h2_low = hidden_two.astype(bf16)
    down = jnp.zeros((rows, width), f32)
    for b in range(blocks):
        cols = slice(b * step, (b + 1) * step)
        shift = jnp.concatenate(
            [
                vec_ref[13 + q : 14 + q, i * own : (i + 1) * own]
                for i in range(b * here.n_dp // blocks, (b + 1) * here.n_dp // blocks)
                for q in range(groups)
            ],
            axis=1,
        )
        up = nn(h2_low, wup_ref[:, cols]) + shift
        up_scr[:, cols] = up
        act = (up * jax.nn.sigmoid(up)).astype(bf16)
        act_scr[:, cols] = act
        down = down + nn(act, wdn_ref[cols, :])
    res3 = hidden_two + down + vec_ref[6:7, :]
    normed3, inv3 = norm_stats(res3)
    result = (normed3 * vec_ref[12:13, :] + vec_ref[9:10, :]).astype(bf16)
    out0_ref[...] = result[:size]
    out1_ref[...] = result[size:]
    upstream = jnp.concatenate([cot0_ref[...], cot1_ref[...]], axis=0).astype(f32)
    small_ref[...] = jnp.zeros_like(small_ref)
    small_ref[12:13, :] = col_sum(upstream * normed3)
    small_ref[9:10, :] = col_sum(upstream)
    grad_three = norm_backward(upstream, normed3, inv3, vec_ref[12:13, :])
    small_ref[6:7, :] = col_sum(grad_three)
    down_low = grad_three.astype(bf16)
    h2_t = h2_low.T
    grad_h2 = grad_three
    piece = width // here.n
    up_piece = hidden_units // here.n
    part_rows = hidden_units // here.n_dp
    first = here.core == 0
    for b in range(blocks):
        cols = slice(b * step, (b + 1) * step)
        gdown = tn(act_scr[:, cols], down_low).astype(bf16)
        for pair in range(here.n_dp // 2 // blocks):
            m = (b * (here.n_dp // 2 // blocks) + pair) ^ here.chip
            for j in range(here.n):
                s = (j + here.n - here.z) % here.n
                for g in range(groups):
                    at = 2 * pair * part_rows + g * own
                    lanes = slice(j * piece, (j + 1) * piece)
                    even = gdown[at : at + own, lanes]
                    odd = gdown[at + part_rows : at + part_rows + own, lanes]
                    base = piece + up_piece + g * piece
                    mine_ref[m, s, :, base : base + piece] = jnp.where(first, even, odd)
                    theirs_ref[m, s, :, base : base + piece] = jnp.where(first, odd, even)
        up = up_scr[:, cols]
        sig = jax.nn.sigmoid(up)
        up_low = (
            nt(down_low, wdn_ref[cols, :]) * sig * (1.0 + up * (1.0 - sig))
        ).astype(bf16)
        upl_scr[:, cols] = up_low
        small_ref[16 + b : 17 + b, :] = col_sum(up_low.astype(f32))
        grad_h2 = grad_h2 + nt(up_low, wup_ref[:, cols])
    write_grads(mine_ref, theirs_ref, here, nn(h2_t, upl_scr[...]), piece)
    small_ref[11:12, :] = col_sum(grad_h2 * normed2)
    small_ref[8:9, :] = col_sum(grad_h2)
    grad_two = norm_backward(grad_h2, normed2, inv2, vec_ref[11:12, :])
    small_ref[5:6, :] = col_sum(grad_two)
    gtwo_ref[...] = grad_two
    two_low = grad_two.astype(bf16)
    write_grads(mine_ref, theirs_ref, here, tn(catt_ref[...], two_low), 0)
    cgrad_ref[...] = nt(two_low, wco_ref[...]).astype(bf16)


def ones_sum(t_ref):
    return nt(jnp.ones((8, t_ref.shape[1]), bf16), t_ref[...])[0:1, :]


def cross_backward_pairs(here, q_ref, k_ref, v_ref, att_ref, g_ref, lse_ref, vec_ref, scratch, first, last):
    qt_scr, gt_scr, dq_scr, dkt_scr, dvt_scr = scratch
    length = k_ref.shape[0]
    qt_scr[...] = q_ref[...].T
    gt_scr[...] = g_ref[...].T
    step = length // 4
    limit = length_limit(here, vec_ref)

    def pairs(pair, carry):
        parts = []
        for part in range(4):
            start = part * step

            def visible(count, keys, start=start):
                return lax.broadcasted_iota(jnp.int32, (count, keys), 1) + start < limit

            parts.append((start, step, visible, False))
        attend_rows_back(
            q_ref, k_ref, v_ref, att_ref, g_ref, lse_ref, qt_scr, gt_scr,
            dq_scr, dkt_scr, dvt_scr, 0, q_ref.shape[0], parts, pair,
        )
        return carry

    lax.fori_loop(first, last, pairs, 0)


def cross_backward_kernel(
    first, last, cq_ref, ek_ref, ev_ref, catt_ref, cgrad_ref, clse_ref, vec_ref,
    dq_ref, low_ref, *scratch,
):
    cross_backward_pairs(
        Here(), cq_ref, ek_ref, ev_ref, catt_ref, cgrad_ref, clse_ref, vec_ref, scratch, first, last
    )
    _, _, dq_scr, dkt_scr, dvt_scr = scratch
    done = last * PAIR
    dq_ref[:, :done] = dq_scr[:, :done]
    low_ref[:done, :] = dkt_scr[:done, :].astype(bf16)
    low_ref[done:, :] = dvt_scr[:done, :].astype(bf16)


def cross_backward_rest_kernel(
    cq_ref, ek_ref, ev_ref, catt_ref, cgrad_ref, clse_ref, vec_ref, dq_in_ref, low_in_ref, enc_ref, wckv_ref,
    mine_ref, theirs_ref, qgrad_ref, gw_ref, evsum_ref, *scratch,
):
    here = Here()
    low_scr = scratch[-1]
    length, width = enc_ref.shape
    rows = cq_ref.shape[0]
    done = PAIR
    cross_backward_pairs(
        here, cq_ref, ek_ref, ev_ref, catt_ref, cgrad_ref, clse_ref, vec_ref, scratch[:-1], 1, H // 2
    )
    _, _, dq_scr, dkt_scr, dvt_scr = scratch[:-1]
    dq_scr[:, :done] = dq_in_ref[:, :done]
    low_scr[:done, :] = low_in_ref[:done, :]
    low_scr[done:width, :] = dkt_scr[done:, :].astype(bf16)
    low_scr[width : width + done, :] = low_in_ref[done:, :]
    low_scr[width + done :, :] = dvt_scr[done:, :].astype(bf16)
    for t, piece in enumerate(here.slots()):
        at = pl.ds(pl.multiple_of(piece * rows, rows), rows)
        out_ref, slot = (mine_ref, t) if t < here.h else (theirs_ref, t - here.h)
        out_ref[slot * rows : (slot + 1) * rows, :] = (
            nn(wckv_ref[...], low_scr[:, at]).T.astype(bf16)
        )
    qgrad_ref[...] = (dq_scr[...].astype(f32) * SCALE).astype(bf16)
    evsum_ref[...] = jnp.zeros_like(evsum_ref)
    evsum_ref[0:1, :] = ones_sum(low_scr.at[width:, :])
    gw_ref[...] = nn(low_scr[...], enc_ref[...]).T.astype(bf16)


def norm_one_backward_kernel(
    qgrad_ref, wcq_ref, wso_ref, vec_ref, res1_ref, att_ref, gtwo_ref, small_in_ref, evsum_ref,
    gone_ref, sgrad_ref, gcq_ref, gso_ref, small_ref,
):
    small_ref[...] = small_in_ref[...]
    small_ref[3:4, :] = col_sum(qgrad_ref[...].astype(f32))
    small_ref[4:5, :] = evsum_ref[0:1, :]
    normed, inv = norm_stats(res1_ref[...])
    grad_h1 = gtwo_ref[...] + nt(qgrad_ref[...], wcq_ref[...])
    small_ref[10:11, :] = col_sum(grad_h1 * normed)
    small_ref[7:8, :] = col_sum(grad_h1)
    grad_one = norm_backward(grad_h1, normed, inv, vec_ref[10:11, :])
    small_ref[2:3, :] = col_sum(grad_one)
    gone_ref[...] = grad_one
    one_low = grad_one.astype(bf16)
    sgrad_ref[...] = nt(one_low, wso_ref[...]).astype(bf16)
    hidden = (normed * vec_ref[10:11, :] + vec_ref[7:8, :]).astype(bf16)
    gcq_ref[...] = tn(hidden, qgrad_ref[...]).astype(bf16)
    gso_ref[...] = tn(att_ref[...], one_low).astype(bf16)


def self_backward_kernel(
    q_ref, k_ref, v_ref, att_ref, sgrad_ref, lse_ref, x_ref, w_ref, gone_ref,
    small_in_ref, gckv_ref, gcq_ref, gso_ref,
    mine_ref, theirs_ref, gmine_ref, gtheirs_ref,
    qt_scr, gt_scr, dq_scr, dkt_scr, dvt_scr, low_scr, gin_scr, small_scr, small_t_scr,
):
    here = Here()
    n = here.n
    length, width = x_ref.shape
    rows = q_ref.shape[0]
    size = rows // 2
    qt_scr[...] = q_ref[...].T
    gt_scr[...] = sgrad_ref[...].T
    for which in range(n):

        @pl.when(here.worker == which)
        def _(which=which):
            order = sorted(range(2), key=lambda block: -chunk_of(which, block, n))
            top = chunk_of(which, order[0], n)
            if top + 1 < 2 * n:
                rest = (2 * n - 1 - top) * size
                dkt_scr[:, (top + 1) * size :] = jnp.zeros((width, rest), f32)
                dvt_scr[:, (top + 1) * size :] = jnp.zeros((width, rest), f32)

            def pairs(pair, carry):
                for order_place, block in enumerate(order):
                    chunk = chunk_of(which, block, n)
                    parts = []
                    for start, count, mask in causal_parts(chunk, size):
                        while count > 4 * size:
                            parts.append((start, 4 * size, mask, order_place == 1))
                            start, count = start + 4 * size, count - 4 * size
                        parts.append((start, count, mask, order_place == 1))
                    attend_rows_back(
                        q_ref, k_ref, v_ref, att_ref, sgrad_ref, lse_ref, qt_scr, gt_scr,
                        dq_scr, dkt_scr, dvt_scr, block * size, size, parts, pair,
                    )
                return carry

            lax.fori_loop(0, H // 2, pairs, 0)

    low_scr[:width, :] = dkt_scr[...].astype(bf16)
    low_scr[width:, :] = dvt_scr[...].astype(bf16)
    q_grad = (dq_scr[...].astype(f32) * SCALE).astype(bf16)
    small_scr[...] = jnp.zeros_like(small_scr)
    small_scr[: small_in_ref.shape[0], :] = small_in_ref[...]
    small_scr[0:1, :] = col_sum(q_grad.astype(f32))
    small_scr[1:2, :] = ones_sum(low_scr.at[width:, :])
    for t in range(n):
        at = slice(t * rows, (t + 1) * rows)
        gin_scr[at, :] = nn(w_ref[:, width:], low_scr[:, at]).T
    even = here.even_chunk()
    wq_grad = jnp.zeros((width, width), f32)
    for block in range(2):
        chunk = even if block == 0 else 2 * n - 1 - even
        at = pl.ds(pl.multiple_of(chunk * size, size), size)
        own_rows = slice(block * size, (block + 1) * size)
        wq_grad = wq_grad + tn(x_ref[at, :], q_grad[own_rows])
        gin_scr[at, :] += gone_ref[own_rows, :] + nt(q_grad[own_rows], w_ref[:, :width])
    for t, piece in enumerate(here.slots()):
        at = pl.ds(pl.multiple_of(piece * rows, rows), rows)
        out_ref, slot = (mine_ref, t) if t < here.h else (theirs_ref, t - here.h)
        out_ref[slot * rows : (slot + 1) * rows, :] = gin_scr[at, :].astype(bf16)
    kv_grad = nn(low_scr[...], x_ref[...]).T.astype(bf16)
    piece = width // n
    own = width // here.n_dp
    grads = jnp.concatenate([wq_grad.astype(bf16), kv_grad], axis=1)
    write_grads(gmine_ref, gtheirs_ref, here, grads, 0)
    write_grads(gmine_ref, gtheirs_ref, here, gcq_ref[...], 3 * piece)
    write_grads(gmine_ref, gtheirs_ref, here, gckv_ref[...], 4 * piece)
    write_grads(gmine_ref, gtheirs_ref, here, gso_ref[...], 6 * piece)
    small_t_scr[width:, :] = jnp.zeros((own, PAIR), f32)
    small_t_scr[:width, :] = small_scr[...].T
    cells = own // n
    up_cells = GROUPS * cells
    first = here.core == 0
    lane = lax.broadcasted_iota(jnp.int32, (own, PAIR), 1)

    def tiny(i, j):
        at = i * own + j * cells
        up = (i * GROUPS * own + j * up_cells) % width
        return jnp.where(lane < 16, small_t_scr[at : at + own, :], small_t_scr[up : up + own, :]).astype(bf16)

    for pair in range(here.n_dp // 2):
        m = pair ^ here.chip
        for j in range(n):
            s = (j + n - here.z) % n
            even_block, odd_block = tiny(2 * pair, j), tiny(2 * pair + 1, j)
            gmine_ref[m, s, :, 7 * piece :] = jnp.where(first, even_block, odd_block)
            gtheirs_ref[m, s, :, 7 * piece :] = jnp.where(first, odd_block, even_block)


def finish_kernel(*refs):
    here = Here()
    n = here.n
    one_refs, refs = refs[:n], refs[n:]
    two_refs, refs = refs[:n], refs[n:]
    self_ref, so_ref, cq_ref, kv_ref, co_ref, up_ref, dn_ref, bias_ref, gain_ref, upb_ref, square_scr = refs
    own, piece = so_ref.shape
    cells = bias_ref.shape[1]
    one = functools.reduce(jnp.add, [ref[...].astype(f32) for ref in one_refs])
    two = functools.reduce(jnp.add, [ref[...].astype(f32) for ref in two_refs])
    up_piece = up_ref.shape[1]
    co_ref[...] = one[:, :piece]
    up_ref[...] = one[:, piece : piece + up_piece]
    for g in range(GROUPS):
        base = piece + up_piece + g * piece
        dn_ref[g * own : (g + 1) * own, :] = one[:, base : base + piece]
    self_ref[...] = two[:, : 3 * piece]
    cq_ref[...] = two[:, 3 * piece : 4 * piece]
    kv_ref[...] = two[:, 4 * piece : 6 * piece]
    so_ref[...] = two[:, 6 * piece : 7 * piece]
    small = two[:, 7 * piece :]
    lane = lax.broadcasted_iota(jnp.int32, small.shape, 1)
    column = 16 + (here.dp * GROUPS * own + here.z * GROUPS * cells) // (own * here.n_dp)
    value = jnp.sum(jnp.where(lane == column, small, 0.0), axis=-1, keepdims=True)
    square_scr[...] = jnp.zeros_like(square_scr)
    square_scr[:own, :] = jnp.where(lane == 24, value, small)
    turned = square_scr[...].T
    bias_ref[...] = turned[0:10, :cells]
    gain_ref[...] = turned[10:13, :cells]
    upb_ref[...] = turned[24:25, : GROUPS * cells]


GROUPS = 4


class Gathered:
    def __init__(self, blocks, partners, start, cols, groups=1):
        self.blocks, self.partners, self.start, self.cols, self.groups = blocks, partners, start, cols, groups
        self.own = blocks[0].shape[0]
        self.rows = 2 * len(blocks) * self.own * groups

    def arrays(self):
        return [*self.blocks, *self.partners]

    def started(self, refs, held_ref, here, sems):
        own = self.own
        chips = len(self.blocks)
        copies = []
        others = [
            ref.at[i * own : (i + 1) * own, :] for ref in refs[chips:] for i in range(ref.shape[0] // own)
        ]
        for m in range(chips):
            for side in range(2):
                place = 2 * (here.chip ^ m) + (here.core ^ side)
                source = refs[m] if side == 0 else others[m]
                for g in range(self.groups):
                    row = pl.multiple_of((place * self.groups + g) * own, own)
                    start = self.start + g * self.cols
                    copies.append(
                        pltpu.make_async_copy(
                            source.at[:, start : start + self.cols],
                            held_ref.at[pl.ds(row, own), :],
                            sems[len(copies)],
                        )
                    )
                    copies[-1].start()
        return copies


def run_kernel(kernel, outs, args, scratch=()):
    name = getattr(kernel, "func", kernel).__name__
    whole = pl.BlockSpec(memory_space=pltpu.VMEM)
    plain = [arg for arg in args if not isinstance(arg, Gathered)]
    parts = [arg for arg in args if isinstance(arg, Gathered)]
    sources = []
    for part in parts:
        for array in part.arrays():
            if not any(array is source for source in sources):
                sources.append(array)
    where = [
        [[i for i, source in enumerate(sources) if source is array][0] for array in part.arrays()]
        for part in parts
    ]
    specs = [whole] * len(plain) + [pl.BlockSpec(memory_space=pltpu.HBM)] * len(sources)
    held = [pltpu.VMEM((part.rows, part.cols), bf16) for part in parts]
    counts = [2 * len(part.blocks) * part.groups for part in parts]
    extra = held + ([pltpu.SemaphoreType.DMA((sum(counts),))] if parts else [])

    def body(*refs):
        plain_refs, refs = refs[: len(plain)], refs[len(plain) :]
        source_refs, refs = refs[: len(sources)], refs[len(sources) :]
        extra_refs, refs = refs[len(refs) - len(extra) :], refs[: len(refs) - len(extra)]
        copies = []
        if parts:
            here = Here()
            for part, places, held_ref, count in zip(parts, where, extra_refs, counts):
                part_refs = [source_refs[i] for i in places]
                sems = [extra_refs[-1].at[len(copies) + i] for i in range(count)]
                copies += part.started(part_refs, held_ref, here, sems)
        for copy in copies:
            copy.wait()
        left, held_refs, in_refs = list(plain_refs), list(extra_refs), []
        for arg in args:
            in_refs.append(held_refs.pop(0) if isinstance(arg, Gathered) else left.pop(0))
        kernel(*in_refs, *refs)

    return pl.pallas_call(
        body,
        out_shape=tuple(jax.ShapeDtypeStruct(shape, kind) for shape, kind in outs),
        in_specs=specs,
        out_specs=tuple(whole for _ in outs),
        scratch_shapes=list(scratch) + extra,
        compiler_params=pltpu.CompilerParams(vmem_limit_bytes=VMEM[name] * 2**20),
        cost_estimate=pl.CostEstimate(flops=1, bytes_accessed=1, transcendentals=0),
    )(*plain, *sources)


def stack_kernel(*refs):
    out_ref = refs[-1]
    start = 0
    for ref in refs[:-1]:
        out_ref[start : start + ref.shape[0], :] = ref[...]
        start += ref.shape[0]


def together_kernel(own_ref, *refs):
    here = Here()
    arrived_refs, out_ref = refs[:-1], refs[-1]
    rows = own_ref.shape[0]

    @pl.when(here.home)
    def _():
        out_ref[:rows, :] = own_ref[...]

    @pl.when(jnp.logical_not(here.home))
    def _():
        out_ref[:rows, :] = arrived_refs[-1][...]

    for t, ref in enumerate(arrived_refs[:-1]):
        out_ref[(t + 1) * rows : (t + 2) * rows, :] = ref[...]


def pack_kernel(
    lens_ref, self_ref, kv_ref, so_ref, cq_ref, up_ref, co_ref, dn_ref, bias_ref, gain_ref, upb_ref,
    one_ref, three_ref, rows_scr,
):
    own = self_ref.shape[0]
    groups = GROUPS
    at = self_ref.shape[1]
    one_ref[:, :at] = self_ref[...]
    start = at + PAIR
    for ref in (kv_ref, so_ref, cq_ref):
        one_ref[:, start : start + ref.shape[1]] = ref[...]
        start += ref.shape[1]
    start = 0
    for ref in [up_ref, co_ref] + [dn_ref.at[g * own : (g + 1) * own, :] for g in range(groups)]:
        three_ref[:, start : start + ref.shape[1]] = ref[...]
        start += ref.shape[1]
    rows_scr[...] = jnp.zeros_like(rows_scr)
    rows_scr[0:10, :own] = bias_ref[...].astype(f32)
    rows_scr[10:13, :own] = gain_ref[...].astype(f32)
    up_row = upb_ref[...].astype(f32).reshape(1, groups * own)
    for g in range(groups):
        rows_scr[13 + g : 14 + g, :own] = up_row[:, g * own : (g + 1) * own]
    length = lens_ref[0]
    rows_scr[17:18, :own] = jnp.full((1, own), length // 64, jnp.int32).astype(f32)
    rows_scr[18:19, :own] = jnp.full((1, own), length % 64, jnp.int32).astype(f32)
    one_ref[:, at : at + PAIR] = rows_scr[...].T[:own, :].astype(bf16)


def pack_weights(
    w_self, w_cross_kv, w_self_out, w_cross_q, w_up, w_cross_out, w_down, biases, gains, up_bias, lens, wide1, wide3
):
    own = w_self.shape[0]
    whole = pl.BlockSpec(memory_space=pltpu.VMEM)
    return pl.pallas_call(
        pack_kernel,
        out_shape=(jax.ShapeDtypeStruct((own, wide1), bf16), jax.ShapeDtypeStruct((own, wide3), bf16)),
        in_specs=[pl.BlockSpec(memory_space=pltpu.SMEM)] + [whole] * 10,
        out_specs=(whole, whole),
        scratch_shapes=[pltpu.VMEM((PAIR, PAIR), f32)],
        compiler_params=pltpu.CompilerParams(vmem_limit_bytes=VMEM["pack_kernel"] * 2**20),
        cost_estimate=pl.CostEstimate(flops=1, bytes_accessed=1, transcendentals=0),
    )(lens, w_self, w_cross_kv, w_self_out, w_cross_q, w_up, w_cross_out, w_down, biases, gains, up_bias)


class Routes:
    def __init__(self, n, n_dp):
        self.n, self.h = n, n // 2
        self.chips = n_dp // 2

    def all_chips(self, pairs):
        return [
            ((2 * k + c0) * self.n + z0, (2 * k + c1) * self.n + z1)
            for k in range(self.chips)
            for (c0, z0), (c1, z1) in pairs
        ]

    def gather(self, r):
        h = self.h
        pairs = []
        for c in range(2):
            for i in range(h):
                far = (c, (1 - c) * h + i)
                if r < h:
                    pairs.append(((c, c * h + i), (1 - c, c * h + (i + r) % h)))
                    pairs.append((far, (c, c * h + (i + r - 1) % h)))
                else:
                    pairs.append((far, (1 - c, c * h + (i + h - 1) % h)))
        return self.all_chips(pairs)

    def rows(self, odd):
        n, h = self.n, self.h
        pairs = []
        for c in range(2):
            for z in range(n):
                chunk = 2 * z + odd
                w = chunk if chunk < n else 2 * n - 1 - chunk
                pairs.append(((c, z), (w % 2, c * h + w // 2)))
        return self.all_chips(pairs)


def back(pairs):
    return [(b, a) for a, b in pairs]


BOTH = ("dp", "sp")


def after(first, then):
    return lax.optimization_barrier((first, then))[1]


def on_device(
    inputs, encoder, cotangent, w_self, w_self_out, w_cross_q, w_cross_kv, w_cross_out, w_up, w_down,
    biases, norm_gains, up_bias, source_lengths,
):
    here = Here()
    n, n_dp, h = here.n, here.n_dp, here.h
    chips = n_dp // 2
    _, rows, width = inputs.shape
    size = rows // 2
    length = n * rows
    hidden_units = w_up.shape[1]
    own = w_self.shape[0]
    piece = width // n
    up_piece = hidden_units // n
    cells = own // n
    groups = up_bias.shape[0] // own
    routes = Routes(n, n_dp)

    def swap(value):
        return lax.ppermute(value, "dp", [(i, i ^ 1) for i in range(n_dp)])

    def to_chip(value, m):
        return lax.ppermute(value, "dp", [(i, i ^ (2 * m)) for i in range(n_dp)])

    def shift(value, s):
        return lax.ppermute(value, "sp", [(i, (i + s) % n) for i in range(n)])

    def gather(value):
        return [lax.ppermute(value, BOTH, routes.gather(r)) for r in range(1, h + 1)]

    def together(value, arrived):
        return jnp.concatenate([jnp.where(here.home, value, arrived[-1])] + arrived[:-1], axis=0)

    def chip_blocks(value):
        return [value] + [to_chip(value, m) for m in range(1, chips)]

    def swap_blocks(blocks):
        shape = (sum(block.shape[0] for block in blocks), blocks[0].shape[1])
        return swap(run_kernel(stack_kernel, [(shape, bf16)], blocks)[0])

    wide1 = 3 * width + PAIR + 4 * width
    wide3 = hidden_units + width + groups * width
    pack1, pack3 = pack_weights(
        w_self, w_cross_kv, w_self_out, w_cross_q, w_up, w_cross_out, w_down,
        biases, norm_gains, up_bias, source_lengths.astype(jnp.int32), wide1, wide3,
    )
    x_arrived = gather(inputs[0])
    own1 = chip_blocks(pack1)
    partner1 = [swap_blocks(own1)]
    x_arrived, own1, pack3, enc_own = lax.optimization_barrier((x_arrived, own1, pack3, encoder[0]))
    x_mine = together(inputs[0], x_arrived)
    x_theirs = swap(x_mine)
    enc_arrived = gather(enc_own)
    near3 = [to_chip(pack3, m) for m in range(1, chips - 1)]

    q, k, v, att, lse, x_full, xq, vec = run_kernel(
        self_forward_kernel,
        [((rows, width), bf16), ((length, width), bf16), ((length, width), bf16),
         ((rows, width), bf16), ((rows, PAIR), f32), ((length, width), bf16), ((rows, width), bf16),
         ((32, width), f32)],
        (x_mine, x_theirs, Gathered(own1, partner1, 0, 3 * width), Gathered(own1, partner1, 3 * width, PAIR)),
    )
    at2 = 3 * width + PAIR
    wckv = Gathered(own1, partner1, at2, 2 * width)
    wso = Gathered(own1, partner1, at2 + 2 * width, width)
    wcq = Gathered(own1, partner1, at2 + 3 * width, width)
    enc_arrived, near3, att = lax.optimization_barrier((enc_arrived, near3, att))
    enc_mine = together(enc_own, enc_arrived)
    enc_theirs = swap(enc_mine)
    res1, cq = run_kernel(
        cross_query_kernel,
        [((rows, width), f32), ((rows, width), bf16)],
        (att, xq, wso, wcq, vec),
    )
    enc_theirs, cq = lax.optimization_barrier((enc_theirs, cq))
    near3 = [pack3] + near3
    partner3 = [swap_blocks(near3)]
    far3 = to_chip(after(enc_mine, pack3), chips - 1)
    late_cot = after(enc_mine, cotangent[0])
    cot0 = lax.ppermute(late_cot[:size], BOTH, routes.rows(0))
    cot1 = lax.ppermute(late_cot[size:], BOTH, routes.rows(1))
    ek, ev, catt, clse, enc_full = run_kernel(
        cross_forward_kernel,
        [((length, width), bf16), ((length, width), bf16), ((rows, width), bf16), ((rows, PAIR), f32),
         ((length, width), bf16)],
        (enc_mine, enc_theirs, cq, wckv, vec),
    )
    far3, partner3, cot0, cot1, catt = lax.optimization_barrier((far3, partner3, cot0, cot1, catt))
    own3 = near3 + [far3]
    partner3 = partner3 + [swap(far3)]
    wup = Gathered(own3, partner3, 0, hidden_units)
    wco = Gathered(own3, partner3, hidden_units, width)
    wdn = Gathered(own3, partner3, hidden_units + width, width, groups)
    block1 = (chips, n, own, piece + up_piece + groups * piece)
    out0, out1, gtwo, cgrad, mine1, theirs1, small = run_kernel(
        feed_forward_kernel,
        [((size, width), bf16), ((size, width), bf16), ((rows, width), f32), ((rows, width), bf16),
         (block1, bf16), (block1, bf16), ((24, width), f32)],
        (res1, catt, wco, wup, wdn, vec, cot0, cot1),
        scratch=[pltpu.VMEM((rows, hidden_units), f32), pltpu.VMEM((rows, hidden_units), bf16),
                 pltpu.VMEM((rows, hidden_units), bf16)],
    )

    def add(a, b):
        return (a.astype(f32) + b.astype(f32)).astype(bf16)

    def between_chips(mine, arrived):
        sums = [add(mine[m], arrived[m]) for m in range(chips)]
        return sums[0], [to_chip(sums[m], m) for m in range(1, chips)]

    def between_places(first, parts):
        total = first.astype(f32)
        for part in parts:
            total = total + part.astype(f32)
        low = total.astype(bf16)
        return low[0], [shift(low[s], s) for s in range(1, n)]

    def finish(first, parts):
        total = first.astype(f32)
        for part in parts:
            total = total + part.astype(f32)
        return total

    def pieces_home(mine, arrived):
        sums = [add(mine[t * rows : (t + 1) * rows], arrived[t * rows : (t + 1) * rows]) for t in range(h)]
        parts = [lax.ppermute(sums[r], BOTH, back(routes.gather(r))) for r in range(1, h)]
        last = lax.ppermute(sums[0], BOTH, back(routes.gather(h)))
        return sums, (jnp.where(here.home, sums[0], last), parts)

    half_low = (2 * PAIR, length)
    back_scratch = [
        pltpu.VMEM((width, rows), bf16), pltpu.VMEM((width, rows), bf16), pltpu.VMEM((rows, width), bf16),
        pltpu.VMEM((width, length), f32), pltpu.VMEM((width, length), f32),
    ]
    low_scratch = [pltpu.VMEM((2 * width, length), bf16)]
    arrived1 = swap(theirs1)
    dq_a, low_a = run_kernel(
        functools.partial(cross_backward_kernel, 0, 1),
        [((rows, width), bf16), (half_low, bf16)],
        (cq, ek, ev, catt, cgrad, clse, vec), scratch=back_scratch,
    )
    mine1, arrived1, low_a, out0, out1 = lax.optimization_barrier((mine1, arrived1, low_a, out0, out1))
    chips1 = between_chips(mine1, arrived1)
    out_parts = (
        lax.ppermute(out0, BOTH, back(routes.rows(0))), lax.ppermute(out1, BOTH, back(routes.rows(1)))
    )
    emine, etheirs, qgrad, gckv, evsum = run_kernel(
        cross_backward_rest_kernel,
        [((h * rows, width), bf16), ((h * rows, width), bf16), ((rows, width), bf16),
         ((width, 2 * width), bf16), ((8, width), f32)],
        (cq, ek, ev, catt, cgrad, clse, vec, dq_a, low_a, enc_full, wckv),
        scratch=back_scratch + low_scratch,
    )
    chips1, out_parts, etheirs, qgrad = lax.optimization_barrier((chips1, out_parts, etheirs, qgrad))
    earrived = swap(etheirs)
    gone, sgrad, gcq, gso, small = run_kernel(
        norm_one_backward_kernel,
        [((rows, width), f32), ((rows, width), bf16), ((width, width), bf16), ((width, width), bf16),
         ((24, width), f32)],
        (qgrad, wcq, wso, vec, res1, att, gtwo, small, evsum),
    )
    emine, earrived, sgrad = lax.optimization_barrier((emine, earrived, sgrad))
    _, enc_home = pieces_home(emine, earrived)
    places1 = between_places(*chips1)
    block2 = (chips, n, own, 7 * piece + PAIR)
    gmine, gtheirs, mine2, theirs2 = run_kernel(
        self_backward_kernel,
        [((h * rows, width), bf16), ((h * rows, width), bf16), (block2, bf16), (block2, bf16)],
        (q, k, v, att, sgrad, lse, x_full, Gathered(own1, partner1, 0, 3 * width), gone, small,
         gckv, gcq, gso),
        scratch=back_scratch + low_scratch
        + [pltpu.VMEM((length, width), f32), pltpu.VMEM((PAIR, width), f32),
           pltpu.VMEM((width + own, PAIR), f32)],
    )
    enc_home, places1, gtheirs, theirs2 = lax.optimization_barrier((enc_home, places1, gtheirs, theirs2))
    garrived = swap(gtheirs)
    arrived2 = swap(theirs2)
    in_sums, in_home = pieces_home(gmine, garrived)
    out_parts, enc_home = after(in_sums, (out_parts, enc_home))
    output = jnp.concatenate(out_parts, axis=0)[None]
    places2 = between_places(*between_chips(mine2, arrived2))
    g_self, g_so, g_cq, g_ckv, g_co, g_up, g_dn, g_bias, g_gain, g_upb = run_kernel(
        finish_kernel,
        [(shape, f32) for shape in (
            (own, 3 * piece), (own, piece), (own, piece), (own, 2 * piece), (own, piece), (own, up_piece),
            (groups * own, piece), (10, cells), (3, cells), (1, groups * cells),
        )],
        (places1[0], *places1[1], places2[0], *places2[1]),
        scratch=[pltpu.VMEM((PAIR, PAIR), f32)],
    )
    return (
        output,
        finish(*in_home)[None],
        finish(*enc_home)[None],
        g_self,
        g_so,
        g_cq,
        g_ckv,
        g_co,
        g_up,
        g_dn,
        g_bias,
        g_gain,
        g_upb.reshape(groups * cells),
    )


def solution(mesh):
    weight = P("dp", None)
    tokens = P("dp", "sp", None)
    return jax.shard_map(
        on_device,
        mesh=mesh,
        in_specs=(tokens,) * 3 + (weight,) * 7 + (P(None, "dp"), P(None, "dp"), P("dp"), P("dp")),
        out_specs=(tokens,) * 3
        + (P("dp", "sp"),) * 7
        + (P(None, ("dp", "sp")), P(None, ("dp", "sp")), P(("dp", "sp"))),
        check_vma=False,
    )
```

```python
import functools

import jax
import jax.numpy as jnp
from jax import lax
from jax.experimental import pallas as pl
from jax.experimental.pallas import tpu as pltpu
from jax.sharding import PartitionSpec as P

H = 8
DH = 64
PAIR = 128

eps_norm = 1e-05
masked_out = -1e30
bf16 = jnp.bfloat16
f32 = jnp.float32
SCALE = DH ** (-0.5)

VMEM = {
    "self_forward_kernel": 11,
    "cross_query_kernel": 10,
    "cross_forward_kernel": 12,
    "feed_forward_kernel": 26,
    "cross_backward_kernel": 20,
    "cross_backward_rest_kernel": 27,
    "norm_one_backward_kernel": 12,
    "self_backward_kernel": 28,
    "finish_kernel": 6,
    "pack_kernel": 60,
    "stack_kernel": 4,
    "together_kernel": 2,
}


def nn(left, right):
    return lax.dot_general(left, right, (((1,), (0,)), ((), ())), preferred_element_type=f32)


def nt(left, right):
    return lax.dot_general(left, right, (((1,), (1,)), ((), ())), preferred_element_type=f32)


def tn(left, right):
    return lax.dot_general(left, right, (((0,), (0,)), ((), ())), preferred_element_type=f32)


def norm_stats(resid):
    centred = resid - jnp.mean(resid, axis=-1, keepdims=True)
    inv_std = lax.rsqrt(jnp.mean(centred * centred, axis=-1, keepdims=True) + eps_norm)
    return centred * inv_std, inv_std


def norm_backward(upstream, normed, inv_std, gain):
    scaled = upstream * gain
    centre_term = jnp.mean(scaled, axis=-1, keepdims=True)
    slope_term = jnp.mean(scaled * normed, axis=-1, keepdims=True)
    return inv_std * (scaled - centre_term - normed * slope_term)


def col_sum(value):
    return jnp.sum(value, axis=0, keepdims=True)


def chunk_of(d, block, n):
    even = d if d % 2 == 0 else 2 * n - 1 - d
    return even if block == 0 else 2 * n - 1 - even


def lane_head(rows, cols=PAIR):
    return lax.broadcasted_iota(jnp.int32, (rows, cols), 1) // DH


def one_head(pair_value, head):
    return jnp.where(lane_head(*pair_value.shape) == head, pair_value, jnp.zeros_like(pair_value))


def pair_slice(pair):
    return pl.ds(pl.multiple_of(pair * PAIR, PAIR), PAIR)


class Here:
    def __init__(self):
        self.n, self.n_dp = lax.axis_size("sp"), lax.axis_size("dp")
        dp = lax.axis_index("dp").astype(jnp.int32)
        self.z = lax.axis_index("sp").astype(jnp.int32)
        self.h = self.n // 2
        self.chip, self.core = dp // 2, dp % 2
        self.dp = dp
        self.half = self.z // self.h
        self.local = self.z % self.h
        self.worker = 2 * self.local + self.core
        self.seq = 2 * self.chip + self.half
        self.home = self.core == self.half

    def slots(self):
        h, c, g = self.h, self.half, self.local

        def part(home):
            at_home = [self.z] + [(1 - c) * h + (g + h - (r - 1)) % h for r in range(1, h)]
            at_other = [(1 - c) * h + (g + 1) % h] + [c * h + (g + h - r) % h for r in range(1, h)]
            return [jnp.where(home, a, b) for a, b in zip(at_home, at_other)]

        return part(self.home) + part(jnp.logical_not(self.home))

    def even_chunk(self):
        return jnp.where(self.worker % 2 == 0, self.worker, 2 * self.n - 1 - self.worker)


def write_grads(mine_ref, theirs_ref, here, value, col0):
    own = value.shape[0] // here.n_dp
    cols = value.shape[1] // here.n
    low = value.astype(bf16)
    first = here.core == 0
    for pair in range(here.n_dp // 2):
        m = pair ^ here.chip
        for j in range(here.n):
            s = (j + here.n - here.z) % here.n
            at = slice(j * cols, (j + 1) * cols)
            even = low[2 * pair * own : (2 * pair + 1) * own, at]
            odd = low[(2 * pair + 1) * own : (2 * pair + 2) * own, at]
            mine_ref[m, s, :own, col0 : col0 + cols] = jnp.where(first, even, odd)
            theirs_ref[m, s, :own, col0 : col0 + cols] = jnp.where(first, odd, even)


def attend_rows(q_ref, k_ref, v_ref, att_ref, lse_ref, row0, rows, parts, pair):
    cols = pair_slice(pair)
    q2 = q_ref[row0 : row0 + rows, cols]
    both = []
    lse_now = lse_ref[row0 : row0 + rows, :]
    lane = lax.broadcasted_iota(jnp.int32, (rows, PAIR), 1)
    for h in range(2):
        qm = one_head(q2, h)
        scores = []
        for start, size, mask in parts:
            s = nt(qm, k_ref[start : start + size, cols])
            if mask is not None:
                s = jnp.where(mask(rows, size), s, masked_out)
            scores.append(s)
        top = functools.reduce(
            jnp.maximum, [jnp.max(s, axis=-1, keepdims=True) for s in scores]
        )
        total = 0.0
        result = 0.0
        for s, (start, size, _) in zip(scores, parts):
            e = jnp.exp(s - top)
            total = total + jnp.sum(e, axis=-1, keepdims=True)
            result = result + nn(e.astype(bf16), v_ref[start : start + size, cols])
        both.append(result / total)
        lse_now = jnp.where(lane == pair * 2 + h, top + jnp.log(total), lse_now)
    lse_ref[row0 : row0 + rows, :] = lse_now
    att_ref[row0 : row0 + rows, cols] = jnp.where(
        lane_head(rows) == 0, both[0], both[1]
    ).astype(bf16)


def attend_rows_back(
    q_ref, k_ref, v_ref, att_ref, g_ref, lse_ref, qt_ref, gt_ref,
    dq_ref, dkt_ref, dvt_ref, row0, rows, parts, pair,
):
    cols = pair_slice(pair)
    q2 = q_ref[row0 : row0 + rows, cols]
    g2 = g_ref[row0 : row0 + rows, cols]
    prod = g2.astype(f32) * att_ref[row0 : row0 + rows, cols].astype(f32)
    lse_all = lse_ref[row0 : row0 + rows, :]
    lane = lax.broadcasted_iota(jnp.int32, (rows, PAIR), 1)
    both = []
    for h in range(2):
        head = pair * 2 + h
        hrows = pl.ds(pl.multiple_of(head * DH, DH), DH)
        qm = one_head(q2, h)
        gm = one_head(g2, h)
        qt = qt_ref[hrows, row0 : row0 + rows]
        gt = gt_ref[hrows, row0 : row0 + rows]
        lse = jnp.sum(jnp.where(lane == head, lse_all, 0.0), axis=-1, keepdims=True)
        delta = jnp.sum(jnp.where(lane // DH == h, prod, 0.0), axis=-1, keepdims=True)
        dq = 0.0
        for start, size, mask, adds in parts:
            k2 = k_ref[start : start + size, cols]
            v2 = v_ref[start : start + size, cols]
            p = jnp.exp(nt(qm, k2) - lse)
            if mask is not None:
                p = jnp.where(mask(rows, size), p, 0.0)
            ds = (p * (nt(gm, v2) - delta)).astype(bf16)
            dq = dq + nn(ds, k2)
            dk = nn(qt, ds)
            dv = nn(gt, p.astype(bf16))
            if adds:
                dk = dk + dkt_ref[hrows, start : start + size]
                dv = dv + dvt_ref[hrows, start : start + size]
            dkt_ref[hrows, start : start + size] = dk
            dvt_ref[hrows, start : start + size] = dv
        both.append(dq)
    dq_ref[row0 : row0 + rows, cols] = (
        jnp.where(lane_head(rows) == 0, both[0], both[1]).astype(bf16)
    )


def diagonal(rows, size):
    row = lax.broadcasted_iota(jnp.int32, (rows, size), 0)
    col = lax.broadcasted_iota(jnp.int32, (rows, size), 1)
    return col <= row


def causal_parts(chunk, size):
    def below(rows, count):
        row = lax.broadcasted_iota(jnp.int32, (rows, count), 0) + (count - rows)
        return lax.broadcasted_iota(jnp.int32, (rows, count), 1) <= row

    parts, left = [], chunk + 1
    while left > 4:
        parts.append(((chunk + 1 - left) * size, 4 * size, None))
        left -= 4
    parts.append(((chunk + 1 - left) * size, left * size, below))
    return parts


def self_forward_kernel(*refs):
    here = Here()
    n = here.n
    halves, refs = refs[:2], refs[2:]
    w_ref, s_ref, q_ref, k_ref, v_ref, att_ref, lse_ref, x_ref, xq_ref, vec_ref = refs
    length, width = x_ref.shape
    rows = q_ref.shape[0]
    size = rows // 2
    vec_ref[...] = s_ref[...].astype(f32).T[: vec_ref.shape[0], :]
    for t, piece in enumerate(here.slots()):
        at = pl.ds(pl.multiple_of(piece * rows, rows), rows)
        block = halves[t // here.h][(t % here.h) * rows : (t % here.h + 1) * rows, :]
        x_ref[at, :] = block
        kv = nn(block, w_ref[:, width : 3 * width])
        k_ref[at, :] = kv[:, :width].astype(bf16)
        v_ref[at, :] = (kv[:, width:] + vec_ref[1:2, :]).astype(bf16)
    even = here.even_chunk()
    for block in range(2):
        chunk = even if block == 0 else 2 * n - 1 - even
        xb = x_ref[pl.ds(pl.multiple_of(chunk * size, size), size), :]
        own_rows = slice(block * size, (block + 1) * size)
        xq_ref[own_rows, :] = xb
        q_ref[own_rows, :] = ((nn(xb, w_ref[:, :width]) + vec_ref[0:1, :]) * SCALE).astype(bf16)
    lse_ref[...] = jnp.zeros_like(lse_ref)

    for which in range(n):

        @pl.when(here.worker == which)
        def _(which=which):
            def pairs(pair, carry):
                for block in range(2):
                    chunk = chunk_of(which, block, n)
                    attend_rows(
                        q_ref, k_ref, v_ref, att_ref, lse_ref, block * size, size,
                        causal_parts(chunk, size), pair,
                    )
                return carry

            lax.fori_loop(0, H // 2, pairs, 0)


def cross_query_kernel(att_ref, xq_ref, wso_ref, wcq_ref, vec_ref, res_ref, cq_ref):
    res_ref[...] = xq_ref[...].astype(f32) + nn(att_ref[...], wso_ref[...]) + vec_ref[2:3, :]
    normed, _ = norm_stats(res_ref[...])
    hidden = (normed * vec_ref[10:11, :] + vec_ref[7:8, :]).astype(bf16)
    cq_ref[...] = ((nn(hidden, wcq_ref[...]) + vec_ref[3:4, :]) * SCALE).astype(bf16)


def length_limit(here, vec_ref):
    packed = vec_ref[17:18, :] * 64.0 + vec_ref[18:19, :]
    lane = lax.broadcasted_iota(jnp.int32, packed.shape, 1)
    picked = jnp.where(lane == here.seq * (packed.shape[1] // here.n_dp), packed, 0.0)
    return jnp.sum(picked, axis=-1, keepdims=True).astype(jnp.int32)


def cross_forward_kernel(*refs):
    here = Here()
    n = here.n
    halves, refs = refs[:2], refs[2:]
    cq_ref, wckv_ref, vec_ref, ek_ref, ev_ref, catt_ref, clse_ref, enc_ref = refs
    length, width = enc_ref.shape
    rows = cq_ref.shape[0]
    size = rows // 2
    for t, piece in enumerate(here.slots()):
        at = pl.ds(pl.multiple_of(piece * rows, rows), rows)
        block = halves[t // here.h][(t % here.h) * rows : (t % here.h + 1) * rows, :]
        enc_ref[at, :] = block
        kv = nn(block, wckv_ref[...])
        ek_ref[at, :] = kv[:, :width].astype(bf16)
        ev_ref[at, :] = (kv[:, width:] + vec_ref[4:5, :]).astype(bf16)
    clse_ref[...] = jnp.zeros_like(clse_ref)
    limit = length_limit(here, vec_ref)

    def visible(count, keys):
        return lax.broadcasted_iota(jnp.int32, (count, keys), 1) < limit

    def pairs(pair, carry):
        for block in range(2):
            attend_rows(
                cq_ref, ek_ref, ev_ref, catt_ref, clse_ref, block * size, size,
                [(0, length, visible)], pair,
            )
        return carry

    lax.fori_loop(0, H // 2, pairs, 0)


def feed_forward_kernel(
    res1_ref, catt_ref, wco_ref, wup_ref, wdn_ref, vec_ref, cot0_ref, cot1_ref,
    out0_ref, out1_ref, gtwo_ref, cgrad_ref, mine_ref, theirs_ref, small_ref,
    up_scr, act_scr, upl_scr,
):
    here = Here()
    rows, width = res1_ref.shape
    size = rows // 2
    hidden_units = wup_ref.shape[1]
    step = width
    blocks = hidden_units // step
    own = width // here.n_dp
    groups = hidden_units // width
    normed, _ = norm_stats(res1_ref[...])
    hidden_one = normed * vec_ref[10:11, :] + vec_ref[7:8, :]
    res2 = hidden_one + nn(catt_ref[...], wco_ref[...]) + vec_ref[5:6, :]
    normed2, inv2 = norm_stats(res2)
    hidden_two = normed2 * vec_ref[11:12, :] + vec_ref[8:9, :]
    h2_low = hidden_two.astype(bf16)
    down = jnp.zeros((rows, width), f32)
    for b in range(blocks):
        cols = slice(b * step, (b + 1) * step)
        shift = jnp.concatenate(
            [
                vec_ref[13 + q : 14 + q, i * own : (i + 1) * own]
                for i in range(b * here.n_dp // blocks, (b + 1) * here.n_dp // blocks)
                for q in range(groups)
            ],
            axis=1,
        )
        up = nn(h2_low, wup_ref[:, cols]) + shift
        up_scr[:, cols] = up
        act = (up * jax.nn.sigmoid(up)).astype(bf16)
        act_scr[:, cols] = act
        down = down + nn(act, wdn_ref[cols, :])
    res3 = hidden_two + down + vec_ref[6:7, :]
    normed3, inv3 = norm_stats(res3)
    result = (normed3 * vec_ref[12:13, :] + vec_ref[9:10, :]).astype(bf16)
    out0_ref[...] = result[:size]
    out1_ref[...] = result[size:]
    upstream = jnp.concatenate([cot0_ref[...], cot1_ref[...]], axis=0).astype(f32)
    small_ref[...] = jnp.zeros_like(small_ref)
    small_ref[12:13, :] = col_sum(upstream * normed3)
    small_ref[9:10, :] = col_sum(upstream)
    grad_three = norm_backward(upstream, normed3, inv3, vec_ref[12:13, :])
    small_ref[6:7, :] = col_sum(grad_three)
    down_low = grad_three.astype(bf16)
    h2_t = h2_low.T
    grad_h2 = grad_three
    piece = width // here.n
    up_piece = hidden_units // here.n
    part_rows = hidden_units // here.n_dp
    first = here.core == 0
    for b in range(blocks):
        cols = slice(b * step, (b + 1) * step)
        gdown = tn(act_scr[:, cols], down_low).astype(bf16)
        for pair in range(here.n_dp // 2 // blocks):
            m = (b * (here.n_dp // 2 // blocks) + pair) ^ here.chip
            for j in range(here.n):
                s = (j + here.n - here.z) % here.n
                for g in range(groups):
                    at = 2 * pair * part_rows + g * own
                    lanes = slice(j * piece, (j + 1) * piece)
                    even = gdown[at : at + own, lanes]
                    odd = gdown[at + part_rows : at + part_rows + own, lanes]
                    base = piece + up_piece + g * piece
                    mine_ref[m, s, :, base : base + piece] = jnp.where(first, even, odd)
                    theirs_ref[m, s, :, base : base + piece] = jnp.where(first, odd, even)
        up = up_scr[:, cols]
        sig = jax.nn.sigmoid(up)
        up_low = (
            nt(down_low, wdn_ref[cols, :]) * sig * (1.0 + up * (1.0 - sig))
        ).astype(bf16)
        upl_scr[:, cols] = up_low
        small_ref[16 + b : 17 + b, :] = col_sum(up_low.astype(f32))
        grad_h2 = grad_h2 + nt(up_low, wup_ref[:, cols])
    write_grads(mine_ref, theirs_ref, here, nn(h2_t, upl_scr[...]), piece)
    small_ref[11:12, :] = col_sum(grad_h2 * normed2)
    small_ref[8:9, :] = col_sum(grad_h2)
    grad_two = norm_backward(grad_h2, normed2, inv2, vec_ref[11:12, :])
    small_ref[5:6, :] = col_sum(grad_two)
    gtwo_ref[...] = grad_two
    two_low = grad_two.astype(bf16)
    write_grads(mine_ref, theirs_ref, here, tn(catt_ref[...], two_low), 0)
    cgrad_ref[...] = nt(two_low, wco_ref[...]).astype(bf16)


def ones_sum(t_ref):
    return nt(jnp.ones((8, t_ref.shape[1]), bf16), t_ref[...])[0:1, :]


def cross_backward_pairs(here, q_ref, k_ref, v_ref, att_ref, g_ref, lse_ref, vec_ref, scratch, first, last):
    qt_scr, gt_scr, dq_scr, dkt_scr, dvt_scr = scratch
    length = k_ref.shape[0]
    qt_scr[...] = q_ref[...].T
    gt_scr[...] = g_ref[...].T
    step = length // 4
    limit = length_limit(here, vec_ref)

    def pairs(pair, carry):
        parts = []
        for part in range(4):
            start = part * step

            def visible(count, keys, start=start):
                return lax.broadcasted_iota(jnp.int32, (count, keys), 1) + start < limit

            parts.append((start, step, visible, False))
        attend_rows_back(
            q_ref, k_ref, v_ref, att_ref, g_ref, lse_ref, qt_scr, gt_scr,
            dq_scr, dkt_scr, dvt_scr, 0, q_ref.shape[0], parts, pair,
        )
        return carry

    lax.fori_loop(first, last, pairs, 0)


def cross_backward_kernel(
    first, last, cq_ref, ek_ref, ev_ref, catt_ref, cgrad_ref, clse_ref, vec_ref,
    dq_ref, low_ref, *scratch,
):
    cross_backward_pairs(
        Here(), cq_ref, ek_ref, ev_ref, catt_ref, cgrad_ref, clse_ref, vec_ref, scratch, first, last
    )
    _, _, dq_scr, dkt_scr, dvt_scr = scratch
    done = last * PAIR
    dq_ref[:, :done] = dq_scr[:, :done]
    low_ref[:done, :] = dkt_scr[:done, :].astype(bf16)
    low_ref[done:, :] = dvt_scr[:done, :].astype(bf16)


def cross_backward_rest_kernel(
    cq_ref, ek_ref, ev_ref, catt_ref, cgrad_ref, clse_ref, vec_ref, dq_in_ref, low_in_ref, enc_ref, wckv_ref,
    mine_ref, theirs_ref, qgrad_ref, gw_ref, evsum_ref, *scratch,
):
    here = Here()
    low_scr = scratch[-1]
    length, width = enc_ref.shape
    rows = cq_ref.shape[0]
    done = PAIR
    cross_backward_pairs(
        here, cq_ref, ek_ref, ev_ref, catt_ref, cgrad_ref, clse_ref, vec_ref, scratch[:-1], 1, H // 2
    )
    _, _, dq_scr, dkt_scr, dvt_scr = scratch[:-1]
    dq_scr[:, :done] = dq_in_ref[:, :done]
    low_scr[:done, :] = low_in_ref[:done, :]
    low_scr[done:width, :] = dkt_scr[done:, :].astype(bf16)
    low_scr[width : width + done, :] = low_in_ref[done:, :]
    low_scr[width + done :, :] = dvt_scr[done:, :].astype(bf16)
    for t, piece in enumerate(here.slots()):
        at = pl.ds(pl.multiple_of(piece * rows, rows), rows)
        out_ref, slot = (mine_ref, t) if t < here.h else (theirs_ref, t - here.h)
        out_ref[slot * rows : (slot + 1) * rows, :] = (
            nn(wckv_ref[...], low_scr[:, at]).T.astype(bf16)
        )
    qgrad_ref[...] = (dq_scr[...].astype(f32) * SCALE).astype(bf16)
    evsum_ref[...] = jnp.zeros_like(evsum_ref)
    evsum_ref[0:1, :] = ones_sum(low_scr.at[width:, :])
    gw_ref[...] = nn(low_scr[...], enc_ref[...]).T.astype(bf16)


def norm_one_backward_kernel(
    qgrad_ref, wcq_ref, wso_ref, vec_ref, res1_ref, att_ref, gtwo_ref, small_in_ref, evsum_ref,
    gone_ref, sgrad_ref, gcq_ref, gso_ref, small_ref,
):
    small_ref[...] = small_in_ref[...]
    small_ref[3:4, :] = col_sum(qgrad_ref[...].astype(f32))
    small_ref[4:5, :] = evsum_ref[0:1, :]
    normed, inv = norm_stats(res1_ref[...])
    grad_h1 = gtwo_ref[...] + nt(qgrad_ref[...], wcq_ref[...])
    small_ref[10:11, :] = col_sum(grad_h1 * normed)
    small_ref[7:8, :] = col_sum(grad_h1)
    grad_one = norm_backward(grad_h1, normed, inv, vec_ref[10:11, :])
    small_ref[2:3, :] = col_sum(grad_one)
    gone_ref[...] = grad_one
    one_low = grad_one.astype(bf16)
    sgrad_ref[...] = nt(one_low, wso_ref[...]).astype(bf16)
    hidden = (normed * vec_ref[10:11, :] + vec_ref[7:8, :]).astype(bf16)
    gcq_ref[...] = tn(hidden, qgrad_ref[...]).astype(bf16)
    gso_ref[...] = tn(att_ref[...], one_low).astype(bf16)


def self_backward_kernel(
    q_ref, k_ref, v_ref, att_ref, sgrad_ref, lse_ref, x_ref, w_ref, gone_ref,
    small_in_ref, gckv_ref, gcq_ref, gso_ref,
    mine_ref, theirs_ref, gmine_ref, gtheirs_ref,
    qt_scr, gt_scr, dq_scr, dkt_scr, dvt_scr, low_scr, gin_scr, small_scr, small_t_scr,
):
    here = Here()
    n = here.n
    length, width = x_ref.shape
    rows = q_ref.shape[0]
    size = rows // 2
    qt_scr[...] = q_ref[...].T
    gt_scr[...] = sgrad_ref[...].T
    for which in range(n):

        @pl.when(here.worker == which)
        def _(which=which):
            order = sorted(range(2), key=lambda block: -chunk_of(which, block, n))
            top = chunk_of(which, order[0], n)
            if top + 1 < 2 * n:
                rest = (2 * n - 1 - top) * size
                dkt_scr[:, (top + 1) * size :] = jnp.zeros((width, rest), f32)
                dvt_scr[:, (top + 1) * size :] = jnp.zeros((width, rest), f32)

            def pairs(pair, carry):
                for order_place, block in enumerate(order):
                    chunk = chunk_of(which, block, n)
                    parts = []
                    for start, count, mask in causal_parts(chunk, size):
                        while count > 4 * size:
                            parts.append((start, 4 * size, mask, order_place == 1))
                            start, count = start + 4 * size, count - 4 * size
                        parts.append((start, count, mask, order_place == 1))
                    attend_rows_back(
                        q_ref, k_ref, v_ref, att_ref, sgrad_ref, lse_ref, qt_scr, gt_scr,
                        dq_scr, dkt_scr, dvt_scr, block * size, size, parts, pair,
                    )
                return carry

            lax.fori_loop(0, H // 2, pairs, 0)

    low_scr[:width, :] = dkt_scr[...].astype(bf16)
    low_scr[width:, :] = dvt_scr[...].astype(bf16)
    q_grad = (dq_scr[...].astype(f32) * SCALE).astype(bf16)
    small_scr[...] = jnp.zeros_like(small_scr)
    small_scr[: small_in_ref.shape[0], :] = small_in_ref[...]
    small_scr[0:1, :] = col_sum(q_grad.astype(f32))
    small_scr[1:2, :] = ones_sum(low_scr.at[width:, :])
    for t in range(n):
        at = slice(t * rows, (t + 1) * rows)
        gin_scr[at, :] = nn(w_ref[:, width:], low_scr[:, at]).T
    even = here.even_chunk()
    wq_grad = jnp.zeros((width, width), f32)
    for block in range(2):
        chunk = even if block == 0 else 2 * n - 1 - even
        at = pl.ds(pl.multiple_of(chunk * size, size), size)
        own_rows = slice(block * size, (block + 1) * size)
        wq_grad = wq_grad + tn(x_ref[at, :], q_grad[own_rows])
        gin_scr[at, :] += gone_ref[own_rows, :] + nt(q_grad[own_rows], w_ref[:, :width])
    for t, piece in enumerate(here.slots()):
        at = pl.ds(pl.multiple_of(piece * rows, rows), rows)
        out_ref, slot = (mine_ref, t) if t < here.h else (theirs_ref, t - here.h)
        out_ref[slot * rows : (slot + 1) * rows, :] = gin_scr[at, :].astype(bf16)
    kv_grad = nn(low_scr[...], x_ref[...]).T.astype(bf16)
    piece = width // n
    own = width // here.n_dp
    grads = jnp.concatenate([wq_grad.astype(bf16), kv_grad], axis=1)
    write_grads(gmine_ref, gtheirs_ref, here, grads, 0)
    write_grads(gmine_ref, gtheirs_ref, here, gcq_ref[...], 3 * piece)
    write_grads(gmine_ref, gtheirs_ref, here, gckv_ref[...], 4 * piece)
    write_grads(gmine_ref, gtheirs_ref, here, gso_ref[...], 6 * piece)
    small_t_scr[width:, :] = jnp.zeros((own, PAIR), f32)
    small_t_scr[:width, :] = small_scr[...].T
    cells = own // n
    up_cells = GROUPS * cells
    first = here.core == 0
    lane = lax.broadcasted_iota(jnp.int32, (own, PAIR), 1)

    def tiny(i, j):
        at = i * own + j * cells
        up = (i * GROUPS * own + j * up_cells) % width
        return jnp.where(lane < 16, small_t_scr[at : at + own, :], small_t_scr[up : up + own, :]).astype(bf16)

    for pair in range(here.n_dp // 2):
        m = pair ^ here.chip
        for j in range(n):
            s = (j + n - here.z) % n
            even_block, odd_block = tiny(2 * pair, j), tiny(2 * pair + 1, j)
            gmine_ref[m, s, :, 7 * piece :] = jnp.where(first, even_block, odd_block)
            gtheirs_ref[m, s, :, 7 * piece :] = jnp.where(first, odd_block, even_block)


def finish_kernel(*refs):
    here = Here()
    n = here.n
    one_refs, refs = refs[:n], refs[n:]
    two_refs, refs = refs[:n], refs[n:]
    self_ref, so_ref, cq_ref, kv_ref, co_ref, up_ref, dn_ref, bias_ref, gain_ref, upb_ref, square_scr = refs
    own, piece = so_ref.shape
    cells = bias_ref.shape[1]
    one = functools.reduce(jnp.add, [ref[...].astype(f32) for ref in one_refs])
    two = functools.reduce(jnp.add, [ref[...].astype(f32) for ref in two_refs])
    up_piece = up_ref.shape[1]
    co_ref[...] = one[:, :piece]
    up_ref[...] = one[:, piece : piece + up_piece]
    for g in range(GROUPS):
        base = piece + up_piece + g * piece
        dn_ref[g * own : (g + 1) * own, :] = one[:, base : base + piece]
    self_ref[...] = two[:, : 3 * piece]
    cq_ref[...] = two[:, 3 * piece : 4 * piece]
    kv_ref[...] = two[:, 4 * piece : 6 * piece]
    so_ref[...] = two[:, 6 * piece : 7 * piece]
    small = two[:, 7 * piece :]
    lane = lax.broadcasted_iota(jnp.int32, small.shape, 1)
    column = 16 + (here.dp * GROUPS * own + here.z * GROUPS * cells) // (own * here.n_dp)
    value = jnp.sum(jnp.where(lane == column, small, 0.0), axis=-1, keepdims=True)
    square_scr[...] = jnp.zeros_like(square_scr)
    square_scr[:own, :] = jnp.where(lane == 24, value, small)
    turned = square_scr[...].T
    bias_ref[...] = turned[0:10, :cells]
    gain_ref[...] = turned[10:13, :cells]
    upb_ref[...] = turned[24:25, : GROUPS * cells]


GROUPS = 4


class Gathered:
    def __init__(self, blocks, partners, start, cols, groups=1):
        self.blocks, self.partners, self.start, self.cols, self.groups = blocks, partners, start, cols, groups
        self.own = blocks[0].shape[0]
        self.rows = 2 * len(blocks) * self.own * groups

    def arrays(self):
        return [*self.blocks, *self.partners]

    def started(self, refs, held_ref, here, sems):
        own = self.own
        chips = len(self.blocks)
        copies = []
        others = [
            ref.at[i * own : (i + 1) * own, :] for ref in refs[chips:] for i in range(ref.shape[0] // own)
        ]
        for m in range(chips):
            for side in range(2):
                place = 2 * (here.chip ^ m) + (here.core ^ side)
                source = refs[m] if side == 0 else others[m]
                for g in range(self.groups):
                    row = pl.multiple_of((place * self.groups + g) * own, own)
                    start = self.start + g * self.cols
                    copies.append(
                        pltpu.make_async_copy(
                            source.at[:, start : start + self.cols],
                            held_ref.at[pl.ds(row, own), :],
                            sems[len(copies)],
                        )
                    )
                    copies[-1].start()
        return copies


def run_kernel(kernel, outs, args, scratch=()):
    name = getattr(kernel, "func", kernel).__name__
    whole = pl.BlockSpec(memory_space=pltpu.VMEM)
    plain = [arg for arg in args if not isinstance(arg, Gathered)]
    parts = [arg for arg in args if isinstance(arg, Gathered)]
    sources = []
    for part in parts:
        for array in part.arrays():
            if not any(array is source for source in sources):
                sources.append(array)
    where = [
        [[i for i, source in enumerate(sources) if source is array][0] for array in part.arrays()]
        for part in parts
    ]
    specs = [whole] * len(plain) + [pl.BlockSpec(memory_space=pltpu.HBM)] * len(sources)
    held = [pltpu.VMEM((part.rows, part.cols), bf16) for part in parts]
    counts = [2 * len(part.blocks) * part.groups for part in parts]
    extra = held + ([pltpu.SemaphoreType.DMA((sum(counts),))] if parts else [])

    def body(*refs):
        plain_refs, refs = refs[: len(plain)], refs[len(plain) :]
        source_refs, refs = refs[: len(sources)], refs[len(sources) :]
        extra_refs, refs = refs[len(refs) - len(extra) :], refs[: len(refs) - len(extra)]
        copies = []
        if parts:
            here = Here()
            for part, places, held_ref, count in zip(parts, where, extra_refs, counts):
                part_refs = [source_refs[i] for i in places]
                sems = [extra_refs[-1].at[len(copies) + i] for i in range(count)]
                copies += part.started(part_refs, held_ref, here, sems)
        for copy in copies:
            copy.wait()
        left, held_refs, in_refs = list(plain_refs), list(extra_refs), []
        for arg in args:
            in_refs.append(held_refs.pop(0) if isinstance(arg, Gathered) else left.pop(0))
        kernel(*in_refs, *refs)

    return pl.pallas_call(
        body,
        out_shape=tuple(jax.ShapeDtypeStruct(shape, kind) for shape, kind in outs),
        in_specs=specs,
        out_specs=tuple(whole for _ in outs),
        scratch_shapes=list(scratch) + extra,
        compiler_params=pltpu.CompilerParams(vmem_limit_bytes=VMEM[name] * 2**20),
        cost_estimate=pl.CostEstimate(flops=1, bytes_accessed=1, transcendentals=0),
    )(*plain, *sources)


def stack_kernel(*refs):
    out_ref = refs[-1]
    start = 0
    for ref in refs[:-1]:
        out_ref[start : start + ref.shape[0], :] = ref[...]
        start += ref.shape[0]


def together_kernel(own_ref, *refs):
    here = Here()
    arrived_refs, out_ref = refs[:-1], refs[-1]
    rows = own_ref.shape[0]

    @pl.when(here.home)
    def _():
        out_ref[:rows, :] = own_ref[...]

    @pl.when(jnp.logical_not(here.home))
    def _():
        out_ref[:rows, :] = arrived_refs[-1][...]

    for t, ref in enumerate(arrived_refs[:-1]):
        out_ref[(t + 1) * rows : (t + 2) * rows, :] = ref[...]


def pack_kernel(
    lens_ref, self_ref, kv_ref, so_ref, cq_ref, up_ref, co_ref, dn_ref, bias_ref, gain_ref, upb_ref,
    one_ref, three_ref, rows_scr,
):
    own = self_ref.shape[0]
    groups = GROUPS
    at = self_ref.shape[1]
    one_ref[:, :at] = self_ref[...]
    start = at + PAIR
    for ref in (kv_ref, so_ref, cq_ref):
        one_ref[:, start : start + ref.shape[1]] = ref[...]
        start += ref.shape[1]
    start = 0
    for ref in [up_ref, co_ref] + [dn_ref.at[g * own : (g + 1) * own, :] for g in range(groups)]:
        three_ref[:, start : start + ref.shape[1]] = ref[...]
        start += ref.shape[1]
    rows_scr[...] = jnp.zeros_like(rows_scr)
    rows_scr[0:10, :own] = bias_ref[...].astype(f32)
    rows_scr[10:13, :own] = gain_ref[...].astype(f32)
    up_row = upb_ref[...].astype(f32).reshape(1, groups * own)
    for g in range(groups):
        rows_scr[13 + g : 14 + g, :own] = up_row[:, g * own : (g + 1) * own]
    length = lens_ref[0]
    rows_scr[17:18, :own] = jnp.full((1, own), length // 64, jnp.int32).astype(f32)
    rows_scr[18:19, :own] = jnp.full((1, own), length % 64, jnp.int32).astype(f32)
    one_ref[:, at : at + PAIR] = rows_scr[...].T[:own, :].astype(bf16)


def pack_weights(
    w_self, w_cross_kv, w_self_out, w_cross_q, w_up, w_cross_out, w_down, biases, gains, up_bias, lens, wide1, wide3
):
    own = w_self.shape[0]
    whole = pl.BlockSpec(memory_space=pltpu.VMEM)
    return pl.pallas_call(
        pack_kernel,
        out_shape=(jax.ShapeDtypeStruct((own, wide1), bf16), jax.ShapeDtypeStruct((own, wide3), bf16)),
        in_specs=[pl.BlockSpec(memory_space=pltpu.SMEM)] + [whole] * 10,
        out_specs=(whole, whole),
        scratch_shapes=[pltpu.VMEM((PAIR, PAIR), f32)],
        compiler_params=pltpu.CompilerParams(vmem_limit_bytes=VMEM["pack_kernel"] * 2**20),
        cost_estimate=pl.CostEstimate(flops=1, bytes_accessed=1, transcendentals=0),
    )(lens, w_self, w_cross_kv, w_self_out, w_cross_q, w_up, w_cross_out, w_down, biases, gains, up_bias)


class Routes:
    def __init__(self, n, n_dp):
        self.n, self.h = n, n // 2
        self.chips = n_dp // 2

    def all_chips(self, pairs):
        return [
            ((2 * k + c0) * self.n + z0, (2 * k + c1) * self.n + z1)
            for k in range(self.chips)
            for (c0, z0), (c1, z1) in pairs
        ]

    def gather(self, r):
        h = self.h
        pairs = []
        for c in range(2):
            for i in range(h):
                far = (c, (1 - c) * h + i)
                if r < h:
                    pairs.append(((c, c * h + i), (1 - c, c * h + (i + r) % h)))
                    pairs.append((far, (c, c * h + (i + r - 1) % h)))
                else:
                    pairs.append((far, (1 - c, c * h + (i + h - 1) % h)))
        return self.all_chips(pairs)

    def rows(self, odd):
        n, h = self.n, self.h
        pairs = []
        for c in range(2):
            for z in range(n):
                chunk = 2 * z + odd
                w = chunk if chunk < n else 2 * n - 1 - chunk
                pairs.append(((c, z), (w % 2, c * h + w // 2)))
        return self.all_chips(pairs)


def back(pairs):
    return [(b, a) for a, b in pairs]


BOTH = ("dp", "sp")


def after(first, then):
    return lax.optimization_barrier((first, then))[1]


def on_device(
    inputs, encoder, cotangent, w_self, w_self_out, w_cross_q, w_cross_kv, w_cross_out, w_up, w_down,
    biases, norm_gains, up_bias, source_lengths,
):
    here = Here()
    n, n_dp, h = here.n, here.n_dp, here.h
    chips = n_dp // 2
    _, rows, width = inputs.shape
    size = rows // 2
    length = n * rows
    hidden_units = w_up.shape[1]
    own = w_self.shape[0]
    piece = width // n
    up_piece = hidden_units // n
    cells = own // n
    groups = up_bias.shape[0] // own
    routes = Routes(n, n_dp)

    def swap(value):
        return lax.ppermute(value, "dp", [(i, i ^ 1) for i in range(n_dp)])

    def to_chip(value, m):
        return lax.ppermute(value, "dp", [(i, i ^ (2 * m)) for i in range(n_dp)])

    def shift(value, s):
        return lax.ppermute(value, "sp", [(i, (i + s) % n) for i in range(n)])

    def gather(value):
        return [lax.ppermute(value, BOTH, routes.gather(r)) for r in range(1, h + 1)]

    def together(value, arrived):
        return jnp.concatenate([jnp.where(here.home, value, arrived[-1])] + arrived[:-1], axis=0)

    def chip_blocks(value):
        return [value] + [to_chip(value, m) for m in range(1, chips)]

    def swap_blocks(blocks):
        shape = (sum(block.shape[0] for block in blocks), blocks[0].shape[1])
        return swap(run_kernel(stack_kernel, [(shape, bf16)], blocks)[0])

    wide1 = 3 * width + PAIR + 4 * width
    wide3 = hidden_units + width + groups * width
    pack1, pack3 = pack_weights(
        w_self, w_cross_kv, w_self_out, w_cross_q, w_up, w_cross_out, w_down,
        biases, norm_gains, up_bias, source_lengths.astype(jnp.int32), wide1, wide3,
    )
    x_arrived = gather(inputs[0])
    own1 = chip_blocks(pack1)
    partner1 = [swap_blocks(own1)]
    x_arrived, own1, pack3, enc_own = lax.optimization_barrier((x_arrived, own1, pack3, encoder[0]))
    x_mine = together(inputs[0], x_arrived)
    x_theirs = swap(x_mine)
    enc_arrived = gather(enc_own)
    near3 = [to_chip(pack3, m) for m in range(1, chips - 1)]

    q, k, v, att, lse, x_full, xq, vec = run_kernel(
        self_forward_kernel,
        [((rows, width), bf16), ((length, width), bf16), ((length, width), bf16),
         ((rows, width), bf16), ((rows, PAIR), f32), ((length, width), bf16), ((rows, width), bf16),
         ((32, width), f32)],
        (x_mine, x_theirs, Gathered(own1, partner1, 0, 3 * width), Gathered(own1, partner1, 3 * width, PAIR)),
    )
    at2 = 3 * width + PAIR
    wckv = Gathered(own1, partner1, at2, 2 * width)
    wso = Gathered(own1, partner1, at2 + 2 * width, width)
    wcq = Gathered(own1, partner1, at2 + 3 * width, width)
    enc_arrived, near3, att = lax.optimization_barrier((enc_arrived, near3, att))
    enc_mine = together(enc_own, enc_arrived)
    enc_theirs = swap(enc_mine)
    res1, cq = run_kernel(
        cross_query_kernel,
        [((rows, width), f32), ((rows, width), bf16)],
        (att, xq, wso, wcq, vec),
    )
    enc_theirs, cq = lax.optimization_barrier((enc_theirs, cq))
    near3 = [pack3] + near3
    partner3 = [swap_blocks(near3)]
    far3 = to_chip(after(enc_mine, pack3), chips - 1)
    late_cot = after(enc_mine, cotangent[0])
    cot0 = lax.ppermute(late_cot[:size], BOTH, routes.rows(0))
    cot1 = lax.ppermute(late_cot[size:], BOTH, routes.rows(1))
    ek, ev, catt, clse, enc_full = run_kernel(
        cross_forward_kernel,
        [((length, width), bf16), ((length, width), bf16), ((rows, width), bf16), ((rows, PAIR), f32),
         ((length, width), bf16)],
        (enc_mine, enc_theirs, cq, wckv, vec),
    )
    far3, partner3, cot0, cot1, catt = lax.optimization_barrier((far3, partner3, cot0, cot1, catt))
    own3 = near3 + [far3]
    partner3 = partner3 + [swap(far3)]
    wup = Gathered(own3, partner3, 0, hidden_units)
    wco = Gathered(own3, partner3, hidden_units, width)
    wdn = Gathered(own3, partner3, hidden_units + width, width, groups)
    block1 = (chips, n, own, piece + up_piece + groups * piece)
    out0, out1, gtwo, cgrad, mine1, theirs1, small = run_kernel(
        feed_forward_kernel,
        [((size, width), bf16), ((size, width), bf16), ((rows, width), f32), ((rows, width), bf16),
         (block1, bf16), (block1, bf16), ((24, width), f32)],
        (res1, catt, wco, wup, wdn, vec, cot0, cot1),
        scratch=[pltpu.VMEM((rows, hidden_units), f32), pltpu.VMEM((rows, hidden_units), bf16),
                 pltpu.VMEM((rows, hidden_units), bf16)],
    )

    def add(a, b):
        return (a.astype(f32) + b.astype(f32)).astype(bf16)

    def between_chips(mine, arrived):
        sums = [add(mine[m], arrived[m]) for m in range(chips)]
        return sums[0], [to_chip(sums[m], m) for m in range(1, chips)]

    def between_places(first, parts):
        total = first.astype(f32)
        for part in parts:
            total = total + part.astype(f32)
        low = total.astype(bf16)
        return low[0], [shift(low[s], s) for s in range(1, n)]

    def finish(first, parts):
        total = first.astype(f32)
        for part in parts:
            total = total + part.astype(f32)
        return total

    def pieces_home(mine, arrived):
        sums = [add(mine[t * rows : (t + 1) * rows], arrived[t * rows : (t + 1) * rows]) for t in range(h)]
        parts = [lax.ppermute(sums[r], BOTH, back(routes.gather(r))) for r in range(1, h)]
        last = lax.ppermute(sums[0], BOTH, back(routes.gather(h)))
        return sums, (jnp.where(here.home, sums[0], last), parts)

    half_low = (2 * PAIR, length)
    back_scratch = [
        pltpu.VMEM((width, rows), bf16), pltpu.VMEM((width, rows), bf16), pltpu.VMEM((rows, width), bf16),
        pltpu.VMEM((width, length), f32), pltpu.VMEM((width, length), f32),
    ]
    low_scratch = [pltpu.VMEM((2 * width, length), bf16)]
    arrived1 = swap(theirs1)
    dq_a, low_a = run_kernel(
        functools.partial(cross_backward_kernel, 0, 1),
        [((rows, width), bf16), (half_low, bf16)],
        (cq, ek, ev, catt, cgrad, clse, vec), scratch=back_scratch,
    )
    mine1, arrived1, low_a, out0, out1 = lax.optimization_barrier((mine1, arrived1, low_a, out0, out1))
    chips1 = between_chips(mine1, arrived1)
    out_parts = (
        lax.ppermute(out0, BOTH, back(routes.rows(0))), lax.ppermute(out1, BOTH, back(routes.rows(1)))
    )
    emine, etheirs, qgrad, gckv, evsum = run_kernel(
        cross_backward_rest_kernel,
        [((h * rows, width), bf16), ((h * rows, width), bf16), ((rows, width), bf16),
         ((width, 2 * width), bf16), ((8, width), f32)],
        (cq, ek, ev, catt, cgrad, clse, vec, dq_a, low_a, enc_full, wckv),
        scratch=back_scratch + low_scratch,
    )
    chips1, out_parts, etheirs, qgrad = lax.optimization_barrier((chips1, out_parts, etheirs, qgrad))
    earrived = swap(etheirs)
    gone, sgrad, gcq, gso, small = run_kernel(
        norm_one_backward_kernel,
        [((rows, width), f32), ((rows, width), bf16), ((width, width), bf16), ((width, width), bf16),
         ((24, width), f32)],
        (qgrad, wcq, wso, vec, res1, att, gtwo, small, evsum),
    )
    emine, earrived, sgrad = lax.optimization_barrier((emine, earrived, sgrad))
    _, enc_home = pieces_home(emine, earrived)
    places1 = between_places(*chips1)
    block2 = (chips, n, own, 7 * piece + PAIR)
    gmine, gtheirs, mine2, theirs2 = run_kernel(
        self_backward_kernel,
        [((h * rows, width), bf16), ((h * rows, width), bf16), (block2, bf16), (block2, bf16)],
        (q, k, v, att, sgrad, lse, x_full, Gathered(own1, partner1, 0, 3 * width), gone, small,
         gckv, gcq, gso),
        scratch=back_scratch + low_scratch
        + [pltpu.VMEM((length, width), f32), pltpu.VMEM((PAIR, width), f32),
           pltpu.VMEM((width + own, PAIR), f32)],
    )
    enc_home, places1, gtheirs, theirs2 = lax.optimization_barrier((enc_home, places1, gtheirs, theirs2))
    garrived = swap(gtheirs)
    arrived2 = swap(theirs2)
    in_sums, in_home = pieces_home(gmine, garrived)
    out_parts, enc_home = after(in_sums, (out_parts, enc_home))
    output = jnp.concatenate(out_parts, axis=0)[None]
    places2 = between_places(*between_chips(mine2, arrived2))
    g_self, g_so, g_cq, g_ckv, g_co, g_up, g_dn, g_bias, g_gain, g_upb = run_kernel(
        finish_kernel,
        [(shape, f32) for shape in (
            (own, 3 * piece), (own, piece), (own, piece), (own, 2 * piece), (own, piece), (own, up_piece),
            (groups * own, piece), (10, cells), (3, cells), (1, groups * cells),
        )],
        (places1[0], *places1[1], places2[0], *places2[1]),
        scratch=[pltpu.VMEM((PAIR, PAIR), f32)],
    )
    return (
        output,
        finish(*in_home)[None],
        finish(*enc_home)[None],
        g_self,
        g_so,
        g_cq,
        g_ckv,
        g_co,
        g_up,
        g_dn,
        g_bias,
        g_gain,
        g_upb.reshape(groups * cells),
    )


def solution(mesh):
    weight = P("dp", None)
    tokens = P("dp", "sp", None)
    return jax.shard_map(
        on_device,
        mesh=mesh,
        in_specs=(tokens,) * 3 + (weight,) * 7 + (P(None, "dp"), P(None, "dp"), P("dp"), P("dp")),
        out_specs=(tokens,) * 3
        + (P("dp", "sp"),) * 7
        + (P(None, ("dp", "sp")), P(None, ("dp", "sp")), P(("dp", "sp"))),
        check_vma=False,
    )
```

```python
import functools

import jax
import jax.numpy as jnp
from jax import lax
from jax.experimental import pallas as pl
from jax.experimental.pallas import tpu as pltpu
from jax.sharding import PartitionSpec as P

H = 8
DH = 64
PAIR = 128

eps_norm = 1e-05
masked_out = -1e30
bf16 = jnp.bfloat16
f32 = jnp.float32
SCALE = DH ** (-0.5)

VMEM = {
    "self_forward_kernel": 11,
    "cross_query_kernel": 10,
    "cross_forward_kernel": 12,
    "feed_forward_kernel": 26,
    "cross_backward_kernel": 20,
    "cross_backward_rest_kernel": 27,
    "norm_one_backward_kernel": 12,
    "self_backward_kernel": 28,
    "finish_kernel": 6,
    "pack_kernel": 60,
    "stack_kernel": 4,
    "together_kernel": 2,
}


def nn(left, right):
    return lax.dot_general(left, right, (((1,), (0,)), ((), ())), preferred_element_type=f32)


def nt(left, right):
    return lax.dot_general(left, right, (((1,), (1,)), ((), ())), preferred_element_type=f32)


def tn(left, right):
    return lax.dot_general(left, right, (((0,), (0,)), ((), ())), preferred_element_type=f32)


def norm_stats(resid):
    centred = resid - jnp.mean(resid, axis=-1, keepdims=True)
    inv_std = lax.rsqrt(jnp.mean(centred * centred, axis=-1, keepdims=True) + eps_norm)
    return centred * inv_std, inv_std


def norm_backward(upstream, normed, inv_std, gain):
    scaled = upstream * gain
    centre_term = jnp.mean(scaled, axis=-1, keepdims=True)
    slope_term = jnp.mean(scaled * normed, axis=-1, keepdims=True)
    return inv_std * (scaled - centre_term - normed * slope_term)


def col_sum(value):
    return jnp.sum(value, axis=0, keepdims=True)


def chunk_of(d, block, n):
    even = d if d % 2 == 0 else 2 * n - 1 - d
    return even if block == 0 else 2 * n - 1 - even


def lane_head(rows, cols=PAIR):
    return lax.broadcasted_iota(jnp.int32, (rows, cols), 1) // DH


def one_head(pair_value, head):
    return jnp.where(lane_head(*pair_value.shape) == head, pair_value, jnp.zeros_like(pair_value))


def pair_slice(pair):
    return pl.ds(pl.multiple_of(pair * PAIR, PAIR), PAIR)


class Here:
    def __init__(self):
        self.n, self.n_dp = lax.axis_size("sp"), lax.axis_size("dp")
        dp = lax.axis_index("dp").astype(jnp.int32)
        self.z = lax.axis_index("sp").astype(jnp.int32)
        self.h = self.n // 2
        self.chip, self.core = dp // 2, dp % 2
        self.dp = dp
        self.half = self.z // self.h
        self.local = self.z % self.h
        self.worker = 2 * self.local + self.core
        self.seq = 2 * self.chip + self.half
        self.home = self.core == self.half

    def slots(self):
        h, c, g = self.h, self.half, self.local

        def part(home):
            at_home = [self.z] + [(1 - c) * h + (g + h - (r - 1)) % h for r in range(1, h)]
            at_other = [(1 - c) * h + (g + 1) % h] + [c * h + (g + h - r) % h for r in range(1, h)]
            return [jnp.where(home, a, b) for a, b in zip(at_home, at_other)]

        return part(self.home) + part(jnp.logical_not(self.home))

    def even_chunk(self):
        return jnp.where(self.worker % 2 == 0, self.worker, 2 * self.n - 1 - self.worker)


def write_grads(mine_ref, theirs_ref, here, value, col0):
    own = value.shape[0] // here.n_dp
    cols = value.shape[1] // here.n
    low = value.astype(bf16)
    first = here.core == 0
    for pair in range(here.n_dp // 2):
        m = pair ^ here.chip
        for j in range(here.n):
            s = (j + here.n - here.z) % here.n
            at = slice(j * cols, (j + 1) * cols)
            even = low[2 * pair * own : (2 * pair + 1) * own, at]
            odd = low[(2 * pair + 1) * own : (2 * pair + 2) * own, at]
            mine_ref[m, s, :own, col0 : col0 + cols] = jnp.where(first, even, odd)
            theirs_ref[m, s, :own, col0 : col0 + cols] = jnp.where(first, odd, even)


def attend_rows(q_ref, k_ref, v_ref, att_ref, lse_ref, row0, rows, parts, pair):
    cols = pair_slice(pair)
    q2 = q_ref[row0 : row0 + rows, cols]
    both = []
    lse_now = lse_ref[row0 : row0 + rows, :]
    lane = lax.broadcasted_iota(jnp.int32, (rows, PAIR), 1)
    for h in range(2):
        qm = one_head(q2, h)
        scores = []
        for start, size, mask in parts:
            s = nt(qm, k_ref[start : start + size, cols])
            if mask is not None:
                s = jnp.where(mask(rows, size), s, masked_out)
            scores.append(s)
        top = functools.reduce(
            jnp.maximum, [jnp.max(s, axis=-1, keepdims=True) for s in scores]
        )
        total = 0.0
        result = 0.0
        for s, (start, size, _) in zip(scores, parts):
            e = jnp.exp(s - top)
            total = total + jnp.sum(e, axis=-1, keepdims=True)
            result = result + nn(e.astype(bf16), v_ref[start : start + size, cols])
        both.append(result / total)
        lse_now = jnp.where(lane == pair * 2 + h, top + jnp.log(total), lse_now)
    lse_ref[row0 : row0 + rows, :] = lse_now
    att_ref[row0 : row0 + rows, cols] = jnp.where(
        lane_head(rows) == 0, both[0], both[1]
    ).astype(bf16)


def attend_rows_back(
    q_ref, k_ref, v_ref, att_ref, g_ref, lse_ref, qt_ref, gt_ref,
    dq_ref, dkt_ref, dvt_ref, row0, rows, parts, pair,
):
    cols = pair_slice(pair)
    q2 = q_ref[row0 : row0 + rows, cols]
    g2 = g_ref[row0 : row0 + rows, cols]
    prod = g2.astype(f32) * att_ref[row0 : row0 + rows, cols].astype(f32)
    lse_all = lse_ref[row0 : row0 + rows, :]
    lane = lax.broadcasted_iota(jnp.int32, (rows, PAIR), 1)
    both = []
    for h in range(2):
        head = pair * 2 + h
        hrows = pl.ds(pl.multiple_of(head * DH, DH), DH)
        qm = one_head(q2, h)
        gm = one_head(g2, h)
        qt = qt_ref[hrows, row0 : row0 + rows]
        gt = gt_ref[hrows, row0 : row0 + rows]
        lse = jnp.sum(jnp.where(lane == head, lse_all, 0.0), axis=-1, keepdims=True)
        delta = jnp.sum(jnp.where(lane // DH == h, prod, 0.0), axis=-1, keepdims=True)
        dq = 0.0
        for start, size, mask, adds in parts:
            k2 = k_ref[start : start + size, cols]
            v2 = v_ref[start : start + size, cols]
            p = jnp.exp(nt(qm, k2) - lse)
            if mask is not None:
                p = jnp.where(mask(rows, size), p, 0.0)
            ds = (p * (nt(gm, v2) - delta)).astype(bf16)
            dq = dq + nn(ds, k2)
            dk = nn(qt, ds)
            dv = nn(gt, p.astype(bf16))
            if adds:
                dk = dk + dkt_ref[hrows, start : start + size]
                dv = dv + dvt_ref[hrows, start : start + size]
            dkt_ref[hrows, start : start + size] = dk
            dvt_ref[hrows, start : start + size] = dv
        both.append(dq)
    dq_ref[row0 : row0 + rows, cols] = (
        jnp.where(lane_head(rows) == 0, both[0], both[1]).astype(bf16)
    )


def diagonal(rows, size):
    row = lax.broadcasted_iota(jnp.int32, (rows, size), 0)
    col = lax.broadcasted_iota(jnp.int32, (rows, size), 1)
    return col <= row


def causal_parts(chunk, size):
    def below(rows, count):
        row = lax.broadcasted_iota(jnp.int32, (rows, count), 0) + (count - rows)
        return lax.broadcasted_iota(jnp.int32, (rows, count), 1) <= row

    parts, left = [], chunk + 1
    while left > 4:
        parts.append(((chunk + 1 - left) * size, 4 * size, None))
        left -= 4
    parts.append(((chunk + 1 - left) * size, left * size, below))
    return parts


def self_forward_kernel(*refs):
    here = Here()
    n = here.n
    halves, refs = refs[:2], refs[2:]
    w_ref, s_ref, q_ref, k_ref, v_ref, att_ref, lse_ref, x_ref, xq_ref, vec_ref = refs
    length, width = x_ref.shape
    rows = q_ref.shape[0]
    size = rows // 2
    vec_ref[...] = s_ref[...].astype(f32).T[: vec_ref.shape[0], :]
    for t, piece in enumerate(here.slots()):
        at = pl.ds(pl.multiple_of(piece * rows, rows), rows)
        block = halves[t // here.h][(t % here.h) * rows : (t % here.h + 1) * rows, :]
        x_ref[at, :] = block
        kv = nn(block, w_ref[:, width : 3 * width])
        k_ref[at, :] = kv[:, :width].astype(bf16)
        v_ref[at, :] = (kv[:, width:] + vec_ref[1:2, :]).astype(bf16)
    even = here.even_chunk()
    for block in range(2):
        chunk = even if block == 0 else 2 * n - 1 - even
        xb = x_ref[pl.ds(pl.multiple_of(chunk * size, size), size), :]
        own_rows = slice(block * size, (block + 1) * size)
        xq_ref[own_rows, :] = xb
        q_ref[own_rows, :] = ((nn(xb, w_ref[:, :width]) + vec_ref[0:1, :]) * SCALE).astype(bf16)
    lse_ref[...] = jnp.zeros_like(lse_ref)

    for which in range(n):

        @pl.when(here.worker == which)
        def _(which=which):
            def pairs(pair, carry):
                for block in range(2):
                    chunk = chunk_of(which, block, n)
                    attend_rows(
                        q_ref, k_ref, v_ref, att_ref, lse_ref, block * size, size,
                        causal_parts(chunk, size), pair,
                    )
                return carry

            lax.fori_loop(0, H // 2, pairs, 0)


def cross_query_kernel(att_ref, xq_ref, wso_ref, wcq_ref, vec_ref, res_ref, cq_ref):
    res_ref[...] = xq_ref[...].astype(f32) + nn(att_ref[...], wso_ref[...]) + vec_ref[2:3, :]
    normed, _ = norm_stats(res_ref[...])
    hidden = (normed * vec_ref[10:11, :] + vec_ref[7:8, :]).astype(bf16)
    cq_ref[...] = ((nn(hidden, wcq_ref[...]) + vec_ref[3:4, :]) * SCALE).astype(bf16)


def length_limit(here, vec_ref):
    packed = vec_ref[17:18, :] * 64.0 + vec_ref[18:19, :]
    lane = lax.broadcasted_iota(jnp.int32, packed.shape, 1)
    picked = jnp.where(lane == here.seq * (packed.shape[1] // here.n_dp), packed, 0.0)
    return jnp.sum(picked, axis=-1, keepdims=True).astype(jnp.int32)


def cross_forward_kernel(*refs):
    here = Here()
    n = here.n
    halves, refs = refs[:2], refs[2:]
    cq_ref, wckv_ref, vec_ref, ek_ref, ev_ref, catt_ref, clse_ref, enc_ref = refs
    length, width = enc_ref.shape
    rows = cq_ref.shape[0]
    size = rows // 2
    for t, piece in enumerate(here.slots()):
        at = pl.ds(pl.multiple_of(piece * rows, rows), rows)
        block = halves[t // here.h][(t % here.h) * rows : (t % here.h + 1) * rows, :]
        enc_ref[at, :] = block
        kv = nn(block, wckv_ref[...])
        ek_ref[at, :] = kv[:, :width].astype(bf16)
        ev_ref[at, :] = (kv[:, width:] + vec_ref[4:5, :]).astype(bf16)
    clse_ref[...] = jnp.zeros_like(clse_ref)
    limit = length_limit(here, vec_ref)

    def visible(count, keys):
        return lax.broadcasted_iota(jnp.int32, (count, keys), 1) < limit

    def pairs(pair, carry):
        for block in range(2):
            attend_rows(
                cq_ref, ek_ref, ev_ref, catt_ref, clse_ref, block * size, size,
                [(0, length, visible)], pair,
            )
        return carry

    lax.fori_loop(0, H // 2, pairs, 0)


def feed_forward_kernel(
    res1_ref, catt_ref, wco_ref, wup_ref, wdn_ref, vec_ref, cot0_ref, cot1_ref,
    out0_ref, out1_ref, gtwo_ref, cgrad_ref, mine_ref, theirs_ref, small_ref,
    up_scr, act_scr, upl_scr,
):
    here = Here()
    rows, width = res1_ref.shape
    size = rows // 2
    hidden_units = wup_ref.shape[1]
    step = width
    blocks = hidden_units // step
    own = width // here.n_dp
    groups = hidden_units // width
    normed, _ = norm_stats(res1_ref[...])
    hidden_one = normed * vec_ref[10:11, :] + vec_ref[7:8, :]
    res2 = hidden_one + nn(catt_ref[...], wco_ref[...]) + vec_ref[5:6, :]
    normed2, inv2 = norm_stats(res2)
    hidden_two = normed2 * vec_ref[11:12, :] + vec_ref[8:9, :]
    h2_low = hidden_two.astype(bf16)
    down = jnp.zeros((rows, width), f32)
    for b in range(blocks):
        cols = slice(b * step, (b + 1) * step)
        shift = jnp.concatenate(
            [
                vec_ref[13 + q : 14 + q, i * own : (i + 1) * own]
                for i in range(b * here.n_dp // blocks, (b + 1) * here.n_dp // blocks)
                for q in range(groups)
            ],
            axis=1,
        )
        up = nn(h2_low, wup_ref[:, cols]) + shift
        up_scr[:, cols] = up
        act = (up * jax.nn.sigmoid(up)).astype(bf16)
        act_scr[:, cols] = act
        down = down + nn(act, wdn_ref[cols, :])
    res3 = hidden_two + down + vec_ref[6:7, :]
    normed3, inv3 = norm_stats(res3)
    result = (normed3 * vec_ref[12:13, :] + vec_ref[9:10, :]).astype(bf16)
    out0_ref[...] = result[:size]
    out1_ref[...] = result[size:]
    upstream = jnp.concatenate([cot0_ref[...], cot1_ref[...]], axis=0).astype(f32)
    small_ref[...] = jnp.zeros_like(small_ref)
    small_ref[12:13, :] = col_sum(upstream * normed3)
    small_ref[9:10, :] = col_sum(upstream)
    grad_three = norm_backward(upstream, normed3, inv3, vec_ref[12:13, :])
    small_ref[6:7, :] = col_sum(grad_three)
    down_low = grad_three.astype(bf16)
    h2_t = h2_low.T
    grad_h2 = grad_three
    piece = width // here.n
    up_piece = hidden_units // here.n
    part_rows = hidden_units // here.n_dp
    first = here.core == 0
    for b in range(blocks):
        cols = slice(b * step, (b + 1) * step)
        gdown = tn(act_scr[:, cols], down_low).astype(bf16)
        for pair in range(here.n_dp // 2 // blocks):
            m = (b * (here.n_dp // 2 // blocks) + pair) ^ here.chip
            for j in range(here.n):
                s = (j + here.n - here.z) % here.n
                for g in range(groups):
                    at = 2 * pair * part_rows + g * own
                    lanes = slice(j * piece, (j + 1) * piece)
                    even = gdown[at : at + own, lanes]
                    odd = gdown[at + part_rows : at + part_rows + own, lanes]
                    base = piece + up_piece + g * piece
                    mine_ref[m, s, :, base : base + piece] = jnp.where(first, even, odd)
                    theirs_ref[m, s, :, base : base + piece] = jnp.where(first, odd, even)
        up = up_scr[:, cols]
        sig = jax.nn.sigmoid(up)
        up_low = (
            nt(down_low, wdn_ref[cols, :]) * sig * (1.0 + up * (1.0 - sig))
        ).astype(bf16)
        upl_scr[:, cols] = up_low
        small_ref[16 + b : 17 + b, :] = col_sum(up_low.astype(f32))
        grad_h2 = grad_h2 + nt(up_low, wup_ref[:, cols])
    write_grads(mine_ref, theirs_ref, here, nn(h2_t, upl_scr[...]), piece)
    small_ref[11:12, :] = col_sum(grad_h2 * normed2)
    small_ref[8:9, :] = col_sum(grad_h2)
    grad_two = norm_backward(grad_h2, normed2, inv2, vec_ref[11:12, :])
    small_ref[5:6, :] = col_sum(grad_two)
    gtwo_ref[...] = grad_two
    two_low = grad_two.astype(bf16)
    write_grads(mine_ref, theirs_ref, here, tn(catt_ref[...], two_low), 0)
    cgrad_ref[...] = nt(two_low, wco_ref[...]).astype(bf16)


def ones_sum(t_ref):
    return nt(jnp.ones((8, t_ref.shape[1]), bf16), t_ref[...])[0:1, :]


def cross_backward_pairs(here, q_ref, k_ref, v_ref, att_ref, g_ref, lse_ref, vec_ref, scratch, first, last):
    qt_scr, gt_scr, dq_scr, dkt_scr, dvt_scr = scratch
    length = k_ref.shape[0]
    qt_scr[...] = q_ref[...].T
    gt_scr[...] = g_ref[...].T
    step = length // 4
    limit = length_limit(here, vec_ref)

    def pairs(pair, carry):
        parts = []
        for part in range(4):
            start = part * step

            def visible(count, keys, start=start):
                return lax.broadcasted_iota(jnp.int32, (count, keys), 1) + start < limit

            parts.append((start, step, visible, False))
        attend_rows_back(
            q_ref, k_ref, v_ref, att_ref, g_ref, lse_ref, qt_scr, gt_scr,
            dq_scr, dkt_scr, dvt_scr, 0, q_ref.shape[0], parts, pair,
        )
        return carry

    lax.fori_loop(first, last, pairs, 0)


def cross_backward_kernel(
    first, last, cq_ref, ek_ref, ev_ref, catt_ref, cgrad_ref, clse_ref, vec_ref,
    dq_ref, low_ref, *scratch,
):
    cross_backward_pairs(
        Here(), cq_ref, ek_ref, ev_ref, catt_ref, cgrad_ref, clse_ref, vec_ref, scratch, first, last
    )
    _, _, dq_scr, dkt_scr, dvt_scr = scratch
    done = last * PAIR
    dq_ref[:, :done] = dq_scr[:, :done]
    low_ref[:done, :] = dkt_scr[:done, :].astype(bf16)
    low_ref[done:, :] = dvt_scr[:done, :].astype(bf16)


def cross_backward_rest_kernel(
    cq_ref, ek_ref, ev_ref, catt_ref, cgrad_ref, clse_ref, vec_ref, dq_in_ref, low_in_ref, enc_ref, wckv_ref,
    mine_ref, theirs_ref, qgrad_ref, gw_ref, evsum_ref, *scratch,
):
    here = Here()
    low_scr = scratch[-1]
    length, width = enc_ref.shape
    rows = cq_ref.shape[0]
    done = PAIR
    cross_backward_pairs(
        here, cq_ref, ek_ref, ev_ref, catt_ref, cgrad_ref, clse_ref, vec_ref, scratch[:-1], 1, H // 2
    )
    _, _, dq_scr, dkt_scr, dvt_scr = scratch[:-1]
    dq_scr[:, :done] = dq_in_ref[:, :done]
    low_scr[:done, :] = low_in_ref[:done, :]
    low_scr[done:width, :] = dkt_scr[done:, :].astype(bf16)
    low_scr[width : width + done, :] = low_in_ref[done:, :]
    low_scr[width + done :, :] = dvt_scr[done:, :].astype(bf16)
    for t, piece in enumerate(here.slots()):
        at = pl.ds(pl.multiple_of(piece * rows, rows), rows)
        out_ref, slot = (mine_ref, t) if t < here.h else (theirs_ref, t - here.h)
        out_ref[slot * rows : (slot + 1) * rows, :] = (
            nn(wckv_ref[...], low_scr[:, at]).T.astype(bf16)
        )
    qgrad_ref[...] = (dq_scr[...].astype(f32) * SCALE).astype(bf16)
    evsum_ref[...] = jnp.zeros_like(evsum_ref)
    evsum_ref[0:1, :] = ones_sum(low_scr.at[width:, :])
    gw_ref[...] = nn(low_scr[...], enc_ref[...]).T.astype(bf16)


def norm_one_backward_kernel(
    qgrad_ref, wcq_ref, wso_ref, vec_ref, res1_ref, att_ref, gtwo_ref, small_in_ref, evsum_ref,
    gone_ref, sgrad_ref, gcq_ref, gso_ref, small_ref,
):
    small_ref[...] = small_in_ref[...]
    small_ref[3:4, :] = col_sum(qgrad_ref[...].astype(f32))
    small_ref[4:5, :] = evsum_ref[0:1, :]
    normed, inv = norm_stats(res1_ref[...])
    grad_h1 = gtwo_ref[...] + nt(qgrad_ref[...], wcq_ref[...])
    small_ref[10:11, :] = col_sum(grad_h1 * normed)
    small_ref[7:8, :] = col_sum(grad_h1)
    grad_one = norm_backward(grad_h1, normed, inv, vec_ref[10:11, :])
    small_ref[2:3, :] = col_sum(grad_one)
    gone_ref[...] = grad_one
    one_low = grad_one.astype(bf16)
    sgrad_ref[...] = nt(one_low, wso_ref[...]).astype(bf16)
    hidden = (normed * vec_ref[10:11, :] + vec_ref[7:8, :]).astype(bf16)
    gcq_ref[...] = tn(hidden, qgrad_ref[...]).astype(bf16)
    gso_ref[...] = tn(att_ref[...], one_low).astype(bf16)


def self_backward_kernel(
    q_ref, k_ref, v_ref, att_ref, sgrad_ref, lse_ref, x_ref, w_ref, gone_ref,
    small_in_ref, gckv_ref, gcq_ref, gso_ref,
    mine_ref, theirs_ref, gmine_ref, gtheirs_ref,
    qt_scr, gt_scr, dq_scr, dkt_scr, dvt_scr, low_scr, gin_scr, small_scr, small_t_scr,
):
    here = Here()
    n = here.n
    length, width = x_ref.shape
    rows = q_ref.shape[0]
    size = rows // 2
    qt_scr[...] = q_ref[...].T
    gt_scr[...] = sgrad_ref[...].T
    for which in range(n):

        @pl.when(here.worker == which)
        def _(which=which):
            order = sorted(range(2), key=lambda block: -chunk_of(which, block, n))
            top = chunk_of(which, order[0], n)
            if top + 1 < 2 * n:
                rest = (2 * n - 1 - top) * size
                dkt_scr[:, (top + 1) * size :] = jnp.zeros((width, rest), f32)
                dvt_scr[:, (top + 1) * size :] = jnp.zeros((width, rest), f32)

            def pairs(pair, carry):
                for order_place, block in enumerate(order):
                    chunk = chunk_of(which, block, n)
                    parts = []
                    for start, count, mask in causal_parts(chunk, size):
                        while count > 4 * size:
                            parts.append((start, 4 * size, mask, order_place == 1))
                            start, count = start + 4 * size, count - 4 * size
                        parts.append((start, count, mask, order_place == 1))
                    attend_rows_back(
                        q_ref, k_ref, v_ref, att_ref, sgrad_ref, lse_ref, qt_scr, gt_scr,
                        dq_scr, dkt_scr, dvt_scr, block * size, size, parts, pair,
                    )
                return carry

            lax.fori_loop(0, H // 2, pairs, 0)

    low_scr[:width, :] = dkt_scr[...].astype(bf16)
    low_scr[width:, :] = dvt_scr[...].astype(bf16)
    q_grad = (dq_scr[...].astype(f32) * SCALE).astype(bf16)
    small_scr[...] = jnp.zeros_like(small_scr)
    small_scr[: small_in_ref.shape[0], :] = small_in_ref[...]
    small_scr[0:1, :] = col_sum(q_grad.astype(f32))
    small_scr[1:2, :] = ones_sum(low_scr.at[width:, :])
    for t in range(n):
        at = slice(t * rows, (t + 1) * rows)
        gin_scr[at, :] = nn(w_ref[:, width:], low_scr[:, at]).T
    even = here.even_chunk()
    wq_grad = jnp.zeros((width, width), f32)
    for block in range(2):
        chunk = even if block == 0 else 2 * n - 1 - even
        at = pl.ds(pl.multiple_of(chunk * size, size), size)
        own_rows = slice(block * size, (block + 1) * size)
        wq_grad = wq_grad + tn(x_ref[at, :], q_grad[own_rows])
        gin_scr[at, :] += gone_ref[own_rows, :] + nt(q_grad[own_rows], w_ref[:, :width])
    for t, piece in enumerate(here.slots()):
        at = pl.ds(pl.multiple_of(piece * rows, rows), rows)
        out_ref, slot = (mine_ref, t) if t < here.h else (theirs_ref, t - here.h)
        out_ref[slot * rows : (slot + 1) * rows, :] = gin_scr[at, :].astype(bf16)
    kv_grad = nn(low_scr[...], x_ref[...]).T.astype(bf16)
    piece = width // n
    own = width // here.n_dp
    grads = jnp.concatenate([wq_grad.astype(bf16), kv_grad], axis=1)
    write_grads(gmine_ref, gtheirs_ref, here, grads, 0)
    write_grads(gmine_ref, gtheirs_ref, here, gcq_ref[...], 3 * piece)
    write_grads(gmine_ref, gtheirs_ref, here, gckv_ref[...], 4 * piece)
    write_grads(gmine_ref, gtheirs_ref, here, gso_ref[...], 6 * piece)
    small_t_scr[width:, :] = jnp.zeros((own, PAIR), f32)
    small_t_scr[:width, :] = small_scr[...].T
    cells = own // n
    up_cells = GROUPS * cells
    first = here.core == 0
    lane = lax.broadcasted_iota(jnp.int32, (own, PAIR), 1)

    def tiny(i, j):
        at = i * own + j * cells
        up = (i * GROUPS * own + j * up_cells) % width
        return jnp.where(lane < 16, small_t_scr[at : at + own, :], small_t_scr[up : up + own, :]).astype(bf16)

    for pair in range(here.n_dp // 2):
        m = pair ^ here.chip
        for j in range(n):
            s = (j + n - here.z) % n
            even_block, odd_block = tiny(2 * pair, j), tiny(2 * pair + 1, j)
            gmine_ref[m, s, :, 7 * piece :] = jnp.where(first, even_block, odd_block)
            gtheirs_ref[m, s, :, 7 * piece :] = jnp.where(first, odd_block, even_block)


def finish_kernel(*refs):
    here = Here()
    n = here.n
    one_refs, refs = refs[:n], refs[n:]
    two_refs, refs = refs[:n], refs[n:]
    self_ref, so_ref, cq_ref, kv_ref, co_ref, up_ref, dn_ref, bias_ref, gain_ref, upb_ref, square_scr = refs
    own, piece = so_ref.shape
    cells = bias_ref.shape[1]
    one = functools.reduce(jnp.add, [ref[...].astype(f32) for ref in one_refs])
    two = functools.reduce(jnp.add, [ref[...].astype(f32) for ref in two_refs])
    up_piece = up_ref.shape[1]
    co_ref[...] = one[:, :piece]
    up_ref[...] = one[:, piece : piece + up_piece]
    for g in range(GROUPS):
        base = piece + up_piece + g * piece
        dn_ref[g * own : (g + 1) * own, :] = one[:, base : base + piece]
    self_ref[...] = two[:, : 3 * piece]
    cq_ref[...] = two[:, 3 * piece : 4 * piece]
    kv_ref[...] = two[:, 4 * piece : 6 * piece]
    so_ref[...] = two[:, 6 * piece : 7 * piece]
    small = two[:, 7 * piece :]
    lane = lax.broadcasted_iota(jnp.int32, small.shape, 1)
    column = 16 + (here.dp * GROUPS * own + here.z * GROUPS * cells) // (own * here.n_dp)
    value = jnp.sum(jnp.where(lane == column, small, 0.0), axis=-1, keepdims=True)
    square_scr[...] = jnp.zeros_like(square_scr)
    square_scr[:own, :] = jnp.where(lane == 24, value, small)
    turned = square_scr[...].T
    bias_ref[...] = turned[0:10, :cells]
    gain_ref[...] = turned[10:13, :cells]
    upb_ref[...] = turned[24:25, : GROUPS * cells]


GROUPS = 4


class Gathered:
    def __init__(self, blocks, partners, start, cols, groups=1):
        self.blocks, self.partners, self.start, self.cols, self.groups = blocks, partners, start, cols, groups
        self.own = blocks[0].shape[0]
        self.rows = 2 * len(blocks) * self.own * groups

    def arrays(self):
        return [*self.blocks, *self.partners]

    def started(self, refs, held_ref, here, sems):
        own = self.own
        chips = len(self.blocks)
        copies = []
        others = [
            ref.at[i * own : (i + 1) * own, :] for ref in refs[chips:] for i in range(ref.shape[0] // own)
        ]
        for m in range(chips):
            for side in range(2):
                place = 2 * (here.chip ^ m) + (here.core ^ side)
                source = refs[m] if side == 0 else others[m]
                for g in range(self.groups):
                    row = pl.multiple_of((place * self.groups + g) * own, own)
                    start = self.start + g * self.cols
                    copies.append(
                        pltpu.make_async_copy(
                            source.at[:, start : start + self.cols],
                            held_ref.at[pl.ds(row, own), :],
                            sems[len(copies)],
                        )
                    )
                    copies[-1].start()
        return copies


def run_kernel(kernel, outs, args, scratch=()):
    name = getattr(kernel, "func", kernel).__name__
    whole = pl.BlockSpec(memory_space=pltpu.VMEM)
    plain = [arg for arg in args if not isinstance(arg, Gathered)]
    parts = [arg for arg in args if isinstance(arg, Gathered)]
    sources = []
    for part in parts:
        for array in part.arrays():
            if not any(array is source for source in sources):
                sources.append(array)
    where = [
        [[i for i, source in enumerate(sources) if source is array][0] for array in part.arrays()]
        for part in parts
    ]
    specs = [whole] * len(plain) + [pl.BlockSpec(memory_space=pltpu.HBM)] * len(sources)
    held = [pltpu.VMEM((part.rows, part.cols), bf16) for part in parts]
    counts = [2 * len(part.blocks) * part.groups for part in parts]
    extra = held + ([pltpu.SemaphoreType.DMA((sum(counts),))] if parts else [])

    def body(*refs):
        plain_refs, refs = refs[: len(plain)], refs[len(plain) :]
        source_refs, refs = refs[: len(sources)], refs[len(sources) :]
        extra_refs, refs = refs[len(refs) - len(extra) :], refs[: len(refs) - len(extra)]
        copies = []
        if parts:
            here = Here()
            for part, places, held_ref, count in zip(parts, where, extra_refs, counts):
                part_refs = [source_refs[i] for i in places]
                sems = [extra_refs[-1].at[len(copies) + i] for i in range(count)]
                copies += part.started(part_refs, held_ref, here, sems)
        for copy in copies:
            copy.wait()
        left, held_refs, in_refs = list(plain_refs), list(extra_refs), []
        for arg in args:
            in_refs.append(held_refs.pop(0) if isinstance(arg, Gathered) else left.pop(0))
        kernel(*in_refs, *refs)

    return pl.pallas_call(
        body,
        out_shape=tuple(jax.ShapeDtypeStruct(shape, kind) for shape, kind in outs),
        in_specs=specs,
        out_specs=tuple(whole for _ in outs),
        scratch_shapes=list(scratch) + extra,
        compiler_params=pltpu.CompilerParams(vmem_limit_bytes=VMEM[name] * 2**20),
        cost_estimate=pl.CostEstimate(flops=1, bytes_accessed=1, transcendentals=0),
    )(*plain, *sources)


def stack_kernel(*refs):
    out_ref = refs[-1]
    start = 0
    for ref in refs[:-1]:
        out_ref[start : start + ref.shape[0], :] = ref[...]
        start += ref.shape[0]


def together_kernel(own_ref, *refs):
    here = Here()
    arrived_refs, out_ref = refs[:-1], refs[-1]
    rows = own_ref.shape[0]

    @pl.when(here.home)
    def _():
        out_ref[:rows, :] = own_ref[...]

    @pl.when(jnp.logical_not(here.home))
    def _():
        out_ref[:rows, :] = arrived_refs[-1][...]

    for t, ref in enumerate(arrived_refs[:-1]):
        out_ref[(t + 1) * rows : (t + 2) * rows, :] = ref[...]


def pack_kernel(
    lens_ref, self_ref, kv_ref, so_ref, cq_ref, up_ref, co_ref, dn_ref, bias_ref, gain_ref, upb_ref,
    one_ref, three_ref, rows_scr,
):
    own = self_ref.shape[0]
    groups = GROUPS
    at = self_ref.shape[1]
    one_ref[:, :at] = self_ref[...]
    start = at + PAIR
    for ref in (kv_ref, so_ref, cq_ref):
        one_ref[:, start : start + ref.shape[1]] = ref[...]
        start += ref.shape[1]
    start = 0
    for ref in [up_ref, co_ref] + [dn_ref.at[g * own : (g + 1) * own, :] for g in range(groups)]:
        three_ref[:, start : start + ref.shape[1]] = ref[...]
        start += ref.shape[1]
    rows_scr[...] = jnp.zeros_like(rows_scr)
    rows_scr[0:10, :own] = bias_ref[...].astype(f32)
    rows_scr[10:13, :own] = gain_ref[...].astype(f32)
    up_row = upb_ref[...].astype(f32).reshape(1, groups * own)
    for g in range(groups):
        rows_scr[13 + g : 14 + g, :own] = up_row[:, g * own : (g + 1) * own]
    length = lens_ref[0]
    rows_scr[17:18, :own] = jnp.full((1, own), length // 64, jnp.int32).astype(f32)
    rows_scr[18:19, :own] = jnp.full((1, own), length % 64, jnp.int32).astype(f32)
    one_ref[:, at : at + PAIR] = rows_scr[...].T[:own, :].astype(bf16)


def pack_weights(
    w_self, w_cross_kv, w_self_out, w_cross_q, w_up, w_cross_out, w_down, biases, gains, up_bias, lens, wide1, wide3
):
    own = w_self.shape[0]
    whole = pl.BlockSpec(memory_space=pltpu.VMEM)
    return pl.pallas_call(
        pack_kernel,
        out_shape=(jax.ShapeDtypeStruct((own, wide1), bf16), jax.ShapeDtypeStruct((own, wide3), bf16)),
        in_specs=[pl.BlockSpec(memory_space=pltpu.SMEM)] + [whole] * 10,
        out_specs=(whole, whole),
        scratch_shapes=[pltpu.VMEM((PAIR, PAIR), f32)],
        compiler_params=pltpu.CompilerParams(vmem_limit_bytes=VMEM["pack_kernel"] * 2**20),
        cost_estimate=pl.CostEstimate(flops=1, bytes_accessed=1, transcendentals=0),
    )(lens, w_self, w_cross_kv, w_self_out, w_cross_q, w_up, w_cross_out, w_down, biases, gains, up_bias)


class Routes:
    def __init__(self, n, n_dp):
        self.n, self.h = n, n // 2
        self.chips = n_dp // 2

    def all_chips(self, pairs):
        return [
            ((2 * k + c0) * self.n + z0, (2 * k + c1) * self.n + z1)
            for k in range(self.chips)
            for (c0, z0), (c1, z1) in pairs
        ]

    def gather(self, r):
        h = self.h
        pairs = []
        for c in range(2):
            for i in range(h):
                far = (c, (1 - c) * h + i)
                if r < h:
                    pairs.append(((c, c * h + i), (1 - c, c * h + (i + r) % h)))
                    pairs.append((far, (c, c * h + (i + r - 1) % h)))
                else:
                    pairs.append((far, (1 - c, c * h + (i + h - 1) % h)))
        return self.all_chips(pairs)

    def rows(self, odd):
        n, h = self.n, self.h
        pairs = []
        for c in range(2):
            for z in range(n):
                chunk = 2 * z + odd
                w = chunk if chunk < n else 2 * n - 1 - chunk
                pairs.append(((c, z), (w % 2, c * h + w // 2)))
        return self.all_chips(pairs)


def back(pairs):
    return [(b, a) for a, b in pairs]


BOTH = ("dp", "sp")


def after(first, then):
    return lax.optimization_barrier((first, then))[1]


def on_device(
    inputs, encoder, cotangent, w_self, w_self_out, w_cross_q, w_cross_kv, w_cross_out, w_up, w_down,
    biases, norm_gains, up_bias, source_lengths,
):
    here = Here()
    n, n_dp, h = here.n, here.n_dp, here.h
    chips = n_dp // 2
    _, rows, width = inputs.shape
    size = rows // 2
    length = n * rows
    hidden_units = w_up.shape[1]
    own = w_self.shape[0]
    piece = width // n
    up_piece = hidden_units // n
    cells = own // n
    groups = up_bias.shape[0] // own
    routes = Routes(n, n_dp)

    def swap(value):
        return lax.ppermute(value, "dp", [(i, i ^ 1) for i in range(n_dp)])

    def to_chip(value, m):
        return lax.ppermute(value, "dp", [(i, i ^ (2 * m)) for i in range(n_dp)])

    def shift(value, s):
        return lax.ppermute(value, "sp", [(i, (i + s) % n) for i in range(n)])

    def gather(value):
        return [lax.ppermute(value, BOTH, routes.gather(r)) for r in range(1, h + 1)]

    def together(value, arrived):
        return jnp.concatenate([jnp.where(here.home, value, arrived[-1])] + arrived[:-1], axis=0)

    def chip_blocks(value):
        return [value] + [to_chip(value, m) for m in range(1, chips)]

    def swap_blocks(blocks):
        shape = (sum(block.shape[0] for block in blocks), blocks[0].shape[1])
        return swap(run_kernel(stack_kernel, [(shape, bf16)], blocks)[0])

    wide1 = 3 * width + PAIR + 4 * width
    wide3 = hidden_units + width + groups * width
    pack1, pack3 = pack_weights(
        w_self, w_cross_kv, w_self_out, w_cross_q, w_up, w_cross_out, w_down,
        biases, norm_gains, up_bias, source_lengths.astype(jnp.int32), wide1, wide3,
    )
    x_arrived = gather(inputs[0])
    own1 = chip_blocks(pack1)
    partner1 = [swap_blocks(own1)]
    x_arrived, own1, pack3, enc_own = lax.optimization_barrier((x_arrived, own1, pack3, encoder[0]))
    x_mine = together(inputs[0], x_arrived)
    x_theirs = swap(x_mine)
    enc_arrived = gather(enc_own)
    near3 = [to_chip(pack3, m) for m in range(1, chips - 1)]

    q, k, v, att, lse, x_full, xq, vec = run_kernel(
        self_forward_kernel,
        [((rows, width), bf16), ((length, width), bf16), ((length, width), bf16),
         ((rows, width), bf16), ((rows, PAIR), f32), ((length, width), bf16), ((rows, width), bf16),
         ((32, width), f32)],
        (x_mine, x_theirs, Gathered(own1, partner1, 0, 3 * width), Gathered(own1, partner1, 3 * width, PAIR)),
    )
    at2 = 3 * width + PAIR
    wckv = Gathered(own1, partner1, at2, 2 * width)
    wso = Gathered(own1, partner1, at2 + 2 * width, width)
    wcq = Gathered(own1, partner1, at2 + 3 * width, width)
    enc_arrived, near3, att = lax.optimization_barrier((enc_arrived, near3, att))
    enc_mine = together(enc_own, enc_arrived)
    enc_theirs = swap(enc_mine)
    res1, cq = run_kernel(
        cross_query_kernel,
        [((rows, width), f32), ((rows, width), bf16)],
        (att, xq, wso, wcq, vec),
    )
    enc_theirs, cq = lax.optimization_barrier((enc_theirs, cq))
    near3 = [pack3] + near3
    partner3 = [swap_blocks(near3)]
    far3 = to_chip(after(enc_mine, pack3), chips - 1)
    late_cot = after((enc_mine, cq), cotangent[0])
    cot0 = lax.ppermute(late_cot[:size], BOTH, routes.rows(0))
    cot1 = lax.ppermute(late_cot[size:], BOTH, routes.rows(1))
    ek, ev, catt, clse, enc_full = run_kernel(
        cross_forward_kernel,
        [((length, width), bf16), ((length, width), bf16), ((rows, width), bf16), ((rows, PAIR), f32),
         ((length, width), bf16)],
        (enc_mine, enc_theirs, cq, wckv, vec),
    )
    far3, partner3, cot0, cot1, catt = lax.optimization_barrier((far3, partner3, cot0, cot1, catt))
    own3 = near3 + [far3]
    partner3 = partner3 + [swap(far3)]
    wup = Gathered(own3, partner3, 0, hidden_units)
    wco = Gathered(own3, partner3, hidden_units, width)
    wdn = Gathered(own3, partner3, hidden_units + width, width, groups)
    block1 = (chips, n, own, piece + up_piece + groups * piece)
    out0, out1, gtwo, cgrad, mine1, theirs1, small = run_kernel(
        feed_forward_kernel,
        [((size, width), bf16), ((size, width), bf16), ((rows, width), f32), ((rows, width), bf16),
         (block1, bf16), (block1, bf16), ((24, width), f32)],
        (res1, catt, wco, wup, wdn, vec, cot0, cot1),
        scratch=[pltpu.VMEM((rows, hidden_units), f32), pltpu.VMEM((rows, hidden_units), bf16),
                 pltpu.VMEM((rows, hidden_units), bf16)],
    )

    def add(a, b):
        return (a.astype(f32) + b.astype(f32)).astype(bf16)

    def between_chips(mine, arrived):
        sums = [add(mine[m], arrived[m]) for m in range(chips)]
        return sums[0], [to_chip(sums[m], m) for m in range(1, chips)]

    def between_places(first, parts):
        total = first.astype(f32)
        for part in parts:
            total = total + part.astype(f32)
        low = total.astype(bf16)
        return low[0], [shift(low[s], s) for s in range(1, n)]

    def finish(first, parts):
        total = first.astype(f32)
        for part in parts:
            total = total + part.astype(f32)
        return total

    def pieces_home(mine, arrived):
        sums = [add(mine[t * rows : (t + 1) * rows], arrived[t * rows : (t + 1) * rows]) for t in range(h)]
        parts = [lax.ppermute(sums[r], BOTH, back(routes.gather(r))) for r in range(1, h)]
        last = lax.ppermute(sums[0], BOTH, back(routes.gather(h)))
        return sums, (jnp.where(here.home, sums[0], last), parts)

    half_low = (2 * PAIR, length)
    back_scratch = [
        pltpu.VMEM((width, rows), bf16), pltpu.VMEM((width, rows), bf16), pltpu.VMEM((rows, width), bf16),
        pltpu.VMEM((width, length), f32), pltpu.VMEM((width, length), f32),
    ]
    low_scratch = [pltpu.VMEM((2 * width, length), bf16)]
    arrived1 = swap(theirs1)
    dq_a, low_a = run_kernel(
        functools.partial(cross_backward_kernel, 0, 1),
        [((rows, width), bf16), (half_low, bf16)],
        (cq, ek, ev, catt, cgrad, clse, vec), scratch=back_scratch,
    )
    mine1, arrived1, low_a, out0, out1 = lax.optimization_barrier((mine1, arrived1, low_a, out0, out1))
    chips1 = between_chips(mine1, arrived1)
    out_parts = (
        lax.ppermute(out0, BOTH, back(routes.rows(0))), lax.ppermute(out1, BOTH, back(routes.rows(1)))
    )
    emine, etheirs, qgrad, gckv, evsum = run_kernel(
        cross_backward_rest_kernel,
        [((h * rows, width), bf16), ((h * rows, width), bf16), ((rows, width), bf16),
         ((width, 2 * width), bf16), ((8, width), f32)],
        (cq, ek, ev, catt, cgrad, clse, vec, dq_a, low_a, enc_full, wckv),
        scratch=back_scratch + low_scratch,
    )
    chips1, out_parts, etheirs, qgrad = lax.optimization_barrier((chips1, out_parts, etheirs, qgrad))
    earrived = swap(etheirs)
    gone, sgrad, gcq, gso, small = run_kernel(
        norm_one_backward_kernel,
        [((rows, width), f32), ((rows, width), bf16), ((width, width), bf16), ((width, width), bf16),
         ((24, width), f32)],
        (qgrad, wcq, wso, vec, res1, att, gtwo, small, evsum),
    )
    emine, earrived, sgrad = lax.optimization_barrier((emine, earrived, sgrad))
    _, enc_home = pieces_home(emine, earrived)
    places1 = between_places(*chips1)
    block2 = (chips, n, own, 7 * piece + PAIR)
    gmine, gtheirs, mine2, theirs2 = run_kernel(
        self_backward_kernel,
        [((h * rows, width), bf16), ((h * rows, width), bf16), (block2, bf16), (block2, bf16)],
        (q, k, v, att, sgrad, lse, x_full, Gathered(own1, partner1, 0, 3 * width), gone, small,
         gckv, gcq, gso),
        scratch=back_scratch + low_scratch
        + [pltpu.VMEM((length, width), f32), pltpu.VMEM((PAIR, width), f32),
           pltpu.VMEM((width + own, PAIR), f32)],
    )
    enc_home, places1, gtheirs, theirs2 = lax.optimization_barrier((enc_home, places1, gtheirs, theirs2))
    garrived = swap(gtheirs)
    arrived2 = swap(theirs2)
    in_sums, in_home = pieces_home(gmine, garrived)
    out_parts, enc_home = after(in_sums, (out_parts, enc_home))
    output = jnp.concatenate(out_parts, axis=0)[None]
    places2 = between_places(*between_chips(mine2, arrived2))
    g_self, g_so, g_cq, g_ckv, g_co, g_up, g_dn, g_bias, g_gain, g_upb = run_kernel(
        finish_kernel,
        [(shape, f32) for shape in (
            (own, 3 * piece), (own, piece), (own, piece), (own, 2 * piece), (own, piece), (own, up_piece),
            (groups * own, piece), (10, cells), (3, cells), (1, groups * cells),
        )],
        (places1[0], *places1[1], places2[0], *places2[1]),
        scratch=[pltpu.VMEM((PAIR, PAIR), f32)],
    )
    return (
        output,
        finish(*in_home)[None],
        finish(*enc_home)[None],
        g_self,
        g_so,
        g_cq,
        g_ckv,
        g_co,
        g_up,
        g_dn,
        g_bias,
        g_gain,
        g_upb.reshape(groups * cells),
    )


def solution(mesh):
    weight = P("dp", None)
    tokens = P("dp", "sp", None)
    return jax.shard_map(
        on_device,
        mesh=mesh,
        in_specs=(tokens,) * 3 + (weight,) * 7 + (P(None, "dp"), P(None, "dp"), P("dp"), P("dp")),
        out_specs=(tokens,) * 3
        + (P("dp", "sp"),) * 7
        + (P(None, ("dp", "sp")), P(None, ("dp", "sp")), P(("dp", "sp"))),
        check_vma=False,
    )
```
